128 devices in a mesh: row: 16 (over y, z_hi, core), col: 8 (over x, z_lo).
Axes of the slice: x: 4, y: 4, z: 4 (z_hi: 2, z_lo: 2; z = z_hi * 2 + z_lo), core: 2. Of those that a mesh axis runs over, the one named last changes fastest.
Arguments:
- embeddings: bfloat16 [65536, 1024], P('row'), may hold values from -1 to 1
- labels: int32 [65536], P(('row', 'col')), may hold values from 0 to 127
- pair_rows: int32 [16, 8, 24], P('row', 'col'), may hold values from 0 to 7, as said below
- pair_cols: int32 [16, 8, 24], P('row', 'col'), may hold values from 0 to 15, as said below
- pair_count: int32 [16, 8], P('row', 'col'), may hold values from 1 to 24, as said below
Outputs:
- vectors: float32 [64, 65536], P(None, ('row', 'col'))
The draws below stay inside these ranges and needn't reach their ends.
Inputs may be any that keep to these rules, and one draw needn't show every extreme that they name: `pair_rows`: within one list the pairs (t, q) are distinct; slot 0 of slab r and block c is t = c, q = r. `pair_cols`: see pair_rows. `pair_count`: some device has exactly 24 live slots in every draw.
All inputs are finite; a program needn't handle non-finite values.
Results may differ from the reference program's by a relative error of at most 0.0036.
Values may be sent and summed in bfloat16 or wider, within the bound.
No kernel may reach another device: no remote copies, remote signals or barrier semaphores. Data moves between devices by JAX's collectives and lax.ppermute only.
A program may use at most 128 MiB of HBM per device.

```python
import jax
import jax.numpy as jnp
from jax import lax

WIDTH = 1024
TILE = 512
K = 64
ITERS = 2
PAIRS = 24
N = 65536
N_ROW = 16
N_COL = 8


def draw_embeddings(key, part):
    key = jax.random.fold_in(key, 11)
    centre_key, member_key, noise_key, share_key = jax.random.split(key, 4)
    unit = WIDTH ** (-0.5)
    bound = min(6.0 * unit, 1.0)
    centres = jnp.clip(jax.random.normal(centre_key, (K, WIDTH), jnp.float32), -6.0, 6.0) * unit
    member = jax.random.randint(member_key, (N,), 0, K, dtype=jnp.int32)
    share = jnp.exp(jax.random.uniform(share_key, (N, 1), jnp.float32, jnp.log(0.05), jnp.log(0.2)))
    noise = jnp.clip(jax.random.normal(noise_key, (N, WIDTH), jnp.float32), -6.0, 6.0) * unit
    mixed = jnp.sqrt(1.0 - share) * centres[member] + jnp.sqrt(share) * noise
    return jnp.clip(mixed, -bound, bound).astype(jnp.bfloat16)


def draw_labels(key, part):
    key = jax.random.fold_in(key, 13)
    class_key, sign_key = jax.random.split(key)
    classes = jax.random.randint(class_key, (N,), 0, K, dtype=jnp.int32)
    negative = (jax.random.randint(sign_key, (N,), 0, 5, dtype=jnp.int32) == 0).astype(jnp.int32)
    return (classes + K * negative).astype(jnp.int32)


def pattern(key):
    devices = N_ROW * N_COL
    candidates = N_COL * N_ROW
    device_keys = jax.random.split(jax.random.fold_in(key, 3), devices)
    orders = jax.vmap(lambda single: jax.random.permutation(single, candidates))(device_keys).astype(jnp.int32)
    device_index = jnp.arange(devices, dtype=jnp.int32)
    own_slot = device_index % N_COL * N_ROW + device_index // N_COL
    where_self = jnp.argmax((orders == own_slot[:, None]).astype(jnp.int32), axis=1)
    leading = orders[:, 0]
    orders = orders.at[device_index, where_self].set(leading)
    orders = orders.at[:, 0].set(own_slot)
    chosen = orders[:, :PAIRS]
    row_tiles = (chosen // N_ROW).reshape(N_ROW, N_COL, PAIRS)
    col_tiles = (chosen % N_ROW).reshape(N_ROW, N_COL, PAIRS)
    count_key, pick_key = jax.random.split(jax.random.fold_in(key, 5))
    lowest = max(1, PAIRS // 4)
    ramp = lowest + (PAIRS - lowest) * device_index // max(devices - 1, 1)
    spread = PAIRS // 8
    jitter = jax.random.randint(count_key, (devices,), -spread, spread + 1, dtype=jnp.int32)
    counts = jnp.clip(ramp + jitter, 1, PAIRS)
    busiest = jax.random.randint(pick_key, (), 0, devices, dtype=jnp.int32)
    counts = jnp.where(device_index == busiest, PAIRS, counts).astype(jnp.int32)
    return (row_tiles, col_tiles, counts.reshape(N_ROW, N_COL))


def draw_pair_rows(key, part):
    row_tiles, col_tiles, counts = pattern(key)
    return row_tiles


def draw_pair_cols(key, part):
    row_tiles, col_tiles, counts = pattern(key)
    return col_tiles


def draw_pair_count(key, part):
    row_tiles, col_tiles, counts = pattern(key)
    return counts


def setup_inputs(seed: int = 0) -> dict:
    key_of = jax.random.split(jax.random.key(seed), 6)
    return {
        "embeddings": draw_embeddings(jax.random.fold_in(key_of[5], 71), 0),
        "labels": draw_labels(jax.random.fold_in(key_of[5], 71), 0),
        "pair_rows": draw_pair_rows(jax.random.fold_in(key_of[5], 71), 0),
        "pair_cols": draw_pair_cols(jax.random.fold_in(key_of[5], 71), 0),
        "pair_count": draw_pair_count(jax.random.fold_in(key_of[5], 71), 0),
    }


KERNEL_SCALE = 0.5

def affinity(left_rows, left_sq, right_rows, right_sq, on_diagonal):
    inner_dot = jnp.dot(left_rows.astype(jnp.float32), right_rows.T.astype(jnp.float32), preferred_element_type=jnp.float32)
    distance = left_sq[:, None] + right_sq[None, :] - 2.0 * inner_dot
    kernel = jnp.exp(-distance / KERNEL_SCALE)
    extent = kernel.shape[0]
    diagonal_mask = lax.broadcasted_iota(jnp.int32, (extent, extent), 0) == lax.broadcasted_iota(jnp.int32, (extent, extent), 1)
    kernel = jnp.where(jnp.logical_and(on_diagonal, diagonal_mask), 0.0, kernel)
    return kernel.astype(jnp.bfloat16)

def reference(embeddings, labels, pair_rows, pair_cols, pair_count):
    tile_grid = embeddings.reshape(N_ROW, N_COL, TILE, WIDTH)
    squares = lax.optimization_barrier(jnp.sum(jnp.square(tile_grid.astype(jnp.float32)), axis=3))
    device_total = N_ROW * N_COL
    device_range = jnp.arange(device_total, dtype=jnp.int32)
    slot_range = jnp.arange(PAIRS, dtype=jnp.int32)
    local_range = jnp.arange(N_COL, dtype=jnp.int32)

    def build_device(device_index):
        slab_index = device_index // N_COL
        block_index = device_index % N_COL
        row_tiles = pair_rows[slab_index, block_index]
        col_tiles = pair_cols[slab_index, block_index]
        live_count = pair_count[slab_index, block_index]

        def build_slot(position):
            row_tile = row_tiles[position]
            col_tile = col_tiles[position]

            def compute(unused):
                return affinity(tile_grid[slab_index, row_tile], squares[slab_index, row_tile], tile_grid[col_tile, block_index], squares[col_tile, block_index], jnp.logical_and(col_tile == slab_index, row_tile == block_index))

            def vacant(unused):
                return jnp.zeros((TILE, TILE), jnp.bfloat16)
            return lax.cond(position < live_count, compute, vacant, 0)
        return lax.map(build_slot, slot_range)
    tile_store = lax.map(build_device, device_range)

    def degree_device(device_index):
        row_tiles = pair_rows[device_index // N_COL, device_index % N_COL]
        row_sums = lax.optimization_barrier(jnp.sum(tile_store[device_index].astype(jnp.float32), axis=2))
        row_pick = (row_tiles[:, None] == local_range[None, :]).astype(jnp.float32)
        return jnp.dot(row_pick.T, row_sums, precision=lax.Precision.HIGHEST)
    device_parts = lax.map(degree_device, device_range)
    degree = lax.optimization_barrier(jnp.sum(device_parts.reshape(N_ROW, N_COL, N_COL, TILE), axis=1)).reshape(N)

    def apply(scaled):
        column_view = scaled.reshape(K, N_ROW, N_COL, TILE)

        def product_device(device_index):
            slab_index = device_index // N_COL
            block_index = device_index % N_COL
            row_tiles = pair_rows[slab_index, block_index]
            col_tiles = pair_cols[slab_index, block_index]
            column_block = column_view[:, :, block_index, :]

            def slot_term(position):
                vec_piece = column_block[:, col_tiles[position], :]
                return jnp.dot(vec_piece.astype(jnp.float32), tile_store[device_index, position].T.astype(jnp.float32), preferred_element_type=jnp.float32)
            contributions = lax.map(slot_term, slot_range)
            row_pick = (row_tiles[:, None] == local_range[None, :]).astype(jnp.float32)
            return jnp.einsum('pkx,ps->ksx', contributions, row_pick, precision=lax.Precision.HIGHEST)
        products = lax.map(product_device, device_range)
        summed = lax.optimization_barrier(jnp.sum(products.reshape(N_ROW, N_COL, K, N_COL, TILE), axis=1))
        return jnp.transpose(summed, (1, 0, 2, 3)).reshape(K, N)
    inv_root = lax.rsqrt(degree)
    root_degree = jnp.sqrt(degree)
    degree_total = jnp.sum(degree)
    label_sign = jnp.where(labels < K, 1.0, -1.0).astype(jnp.float32)
    vectors = ((labels % K)[None, :] == jnp.arange(K, dtype=jnp.int32)[:, None]).astype(jnp.float32) * label_sign[None, :]
    for iteration in range(ITERS):
        scaled = (vectors * inv_root[None, :]).astype(jnp.bfloat16)
        image_block = apply(scaled) * inv_root[None, :]
        top_weight = jnp.dot(image_block, root_degree, precision=lax.Precision.HIGHEST)
        projected = image_block - top_weight[:, None] * root_degree[None, :] / degree_total
        gram_matrix = jnp.dot(projected, projected.T, precision=lax.Precision.HIGHEST) / N
        cholesky_factor = jnp.linalg.cholesky(gram_matrix)
        vectors = jax.scipy.linalg.solve_triangular(cholesky_factor, projected, lower=True)
    return vectors
```

```python
import functools

import jax
import jax.numpy as jnp
import numpy as np
from jax import lax
from jax.experimental import pallas as pl
from jax.experimental.pallas import tpu as pltpu
from jax.sharding import Mesh
from jax.sharding import PartitionSpec as P

TILE = 512
K = 64
ITERS = 2
PAIRS = 24
WIDTH = 1024
KERNEL_SCALE = 0.5
RATE = 2.0 / KERNEL_SCALE * float(np.log2(np.e))
F32 = jnp.float32
BF16 = jnp.bfloat16

ROW = ("y", "zh", "core")
COL = ("x", "zl")
CHIPS = ("y", "zh", "x", "zl")
SLAB_TILES = 8
BLOCK_TILES = 16
VMEM_LIMIT = 48 * 1024 * 1024


def build_kernel(info, slab, column, half_rows, tiles, degree, left, right, made, sem_in, sem_out):
    count = info[0]
    slab_index = info[1]
    block_index = info[2]
    degree[...] = jnp.zeros_like(degree)

    def fetches(position, slot):
        t = info[8 + position]
        q = info[8 + PAIRS + position]
        return (
            pltpu.make_async_copy(slab.at[t], left.at[slot], sem_in.at[0, slot]),
            pltpu.make_async_copy(column.at[q], right.at[slot], sem_in.at[1, slot]),
        )

    def store(position, slot):
        return pltpu.make_async_copy(made.at[slot], tiles.at[position], sem_out.at[slot])

    for copy in fetches(0, 0):
        copy.start()

    def step(position, carry):
        slot = lax.rem(position, 2)

        @pl.when(position + 1 < count)
        def _():
            for copy in fetches(position + 1, 1 - slot):
                copy.start()

        @pl.when(position >= 2)
        def _():
            store(position - 2, slot).wait()

        for copy in fetches(position, slot):
            copy.wait()
        t = info[8 + position]
        q = info[8 + PAIRS + position]
        b = right[slot]
        bf = b.astype(F32)
        half_b = 0.5 * jnp.sum(bf * bf, axis=1, keepdims=True)
        sums = []
        for n in range(2):
            lanes = pl.ds(n * 256, 256)
            inner = lax.dot_general(
                b, left[slot, lanes, :], (((1,), (1,)), ((), ())), preferred_element_type=F32
            )
            half_a = half_rows[pl.ds(t, 1), lanes]
            w = jnp.exp2(RATE * ((inner - half_a) - half_b)).astype(BF16)
            made[slot, :, lanes] = w
            sums.append(jnp.sum(w.astype(F32), axis=0, keepdims=True))
        on_diagonal = jnp.logical_and(t == block_index, q == slab_index)
        old = degree[pl.ds(t, 1), :]
        degree[pl.ds(t, 1), :] = old + jnp.concatenate(sums, axis=1)

        @pl.when(on_diagonal)
        def _():
            w = made[slot]
            same = lax.broadcasted_iota(jnp.int32, (TILE, TILE), 0) == lax.broadcasted_iota(
                jnp.int32, (TILE, TILE), 1
            )
            w = jnp.where(same, jnp.zeros_like(w), w)
            made[slot] = w
            degree[pl.ds(t, 1), :] = old + jnp.sum(w.astype(F32), axis=0, keepdims=True)

        store(position, slot).start()
        return carry

    lax.fori_loop(0, count, step, 0)

    @pl.when(count >= 2)
    def _():
        store(count - 2, lax.rem(count, 2)).wait()

    store(count - 1, lax.rem(count - 1, 2)).wait()


def build(info, slab, column, half_rows):
    any_space = pl.BlockSpec(memory_space=pl.ANY)
    return pl.pallas_call(
        build_kernel,
        out_shape=(
            jax.ShapeDtypeStruct((PAIRS, TILE, TILE), BF16),
            jax.ShapeDtypeStruct((SLAB_TILES, TILE), F32),
        ),
        in_specs=[
            pl.BlockSpec(memory_space=pltpu.SMEM),
            any_space,
            any_space,
            pl.BlockSpec(memory_space=pltpu.VMEM),
        ],
        out_specs=(any_space, pl.BlockSpec(memory_space=pltpu.VMEM)),
        scratch_shapes=[
            pltpu.VMEM((2, TILE, WIDTH), BF16),
            pltpu.VMEM((2, TILE, WIDTH), BF16),
            pltpu.VMEM((2, TILE, TILE), BF16),
            pltpu.SemaphoreType.DMA((2, 2)),
            pltpu.SemaphoreType.DMA((2,)),
        ],
        compiler_params=pltpu.CompilerParams(vmem_limit_bytes=VMEM_LIMIT),
        name="build_tiles",
    )(info, slab, column, half_rows)


def product_kernel(first, info, tiles, *refs):
    if first:
        labels, inv_root, running, held, sem = refs
    else:
        scaled, running, held, sem = refs
    count = info[0]
    running[...] = jnp.zeros_like(running)
    depth = held.shape[0]

    def fetch(position):
        slot = lax.rem(position, depth)
        return pltpu.make_async_copy(tiles.at[position], held.at[slot], sem.at[slot])

    for ahead in range(depth - 1):

        @pl.when(ahead < count)
        def _():
            fetch(ahead).start()

    def step(position, carry):
        @pl.when(position + depth - 1 < count)
        def _():
            fetch(position + depth - 1).start()

        t = info[8 + position]
        q = info[8 + PAIRS + position]
        if first:
            label = labels[pl.ds(q, 1), :]
            value = inv_root[pl.ds(q, 1), :]
            value = jnp.where(label < K, value, -value)
            mine = (label & (K - 1)) == lax.broadcasted_iota(jnp.int32, (K, TILE), 0)
            piece = jnp.where(mine, jnp.broadcast_to(value, (K, TILE)), 0.0).astype(BF16)
        else:
            piece = scaled[q]
        fetch(position).wait()
        running[t] += jnp.dot(
            piece, held[lax.rem(position, depth)], preferred_element_type=F32
        )
        return carry

    lax.fori_loop(0, count, step, 0)


def product(info, tiles, *operands):
    vmem = pl.BlockSpec(memory_space=pltpu.VMEM)
    return pl.pallas_call(
        functools.partial(product_kernel, len(operands) == 2),
        out_shape=jax.ShapeDtypeStruct((SLAB_TILES, K, TILE), F32),
        in_specs=[
            pl.BlockSpec(memory_space=pltpu.SMEM),
            pl.BlockSpec(memory_space=pl.ANY),
        ]
        + [vmem] * len(operands),
        out_specs=vmem,
        scratch_shapes=[
            pltpu.VMEM((4, TILE, TILE), BF16),
            pltpu.SemaphoreType.DMA((4,)),
        ],
        compiler_params=pltpu.CompilerParams(vmem_limit_bytes=VMEM_LIMIT),
        name="product",
    )(info, tiles, *operands)


def weigh_kernel(parts, inv_root, root, image, message):
    block = jnp.sum(parts[...], axis=0) * inv_root[...]
    image[...] = block
    heavy = jnp.concatenate([block, jnp.broadcast_to(root[...], (8, TILE))], axis=0)
    weights = lax.dot_general(
        heavy,
        heavy,
        (((1,), (1,)), ((), ())),
        precision=lax.Precision.HIGHEST,
        preferred_element_type=F32,
    )
    half = K // 2
    message[...] = jnp.concatenate(
        [
            weights[:half, :half],
            weights[half:K, :half],
            weights[half:K, half:K],
            weights[:half, K : K + 8],
            weights[half:K, K : K + 8],
            jnp.broadcast_to(weights[K : K + 1, K : K + 1], (half, 16)),
        ],
        axis=1,
    )


def weigh(parts, inv_root, root):
    vmem = pl.BlockSpec(memory_space=pltpu.VMEM)
    return pl.pallas_call(
        weigh_kernel,
        out_shape=(
            jax.ShapeDtypeStruct((K, TILE), F32),
            jax.ShapeDtypeStruct((K // 2, 128), F32),
        ),
        in_specs=[vmem] * 3,
        out_specs=(vmem, vmem),
        compiler_params=pltpu.CompilerParams(vmem_limit_bytes=VMEM_LIMIT),
        name="weigh",
    )(parts, inv_root, root)


def orthonormalize_kernel(scale, message, image, inv_root, root, out):
    half = K // 2
    sums = message[...]
    lower = sums[:, half : 2 * half]
    gram = jnp.concatenate(
        [
            jnp.concatenate([sums[:, :half], lower.T], axis=1),
            jnp.concatenate([lower, sums[:, 2 * half : 3 * half]], axis=1),
        ],
        axis=0,
    )
    top = jnp.concatenate([sums[:, 96:97], sums[:, 104:105]], axis=0)
    total = sums[:1, 112:113]
    rows = lax.broadcasted_iota(jnp.int32, (K, K), 0)
    columns = lax.broadcasted_iota(jnp.int32, (K, K), 1)
    across = jnp.sum(jnp.where(rows == columns, top, 0.0), axis=0, keepdims=True)
    gram = (gram - top * across / total) * scale
    work = jnp.concatenate([gram, (rows == columns).astype(F32)], axis=1)
    index = lax.broadcasted_iota(jnp.int32, (K, 1), 0)
    pivots = jnp.ones((K, 1), F32)
    for j in range(K):
        row = work[j : j + 1, :]
        pivot = work[j : j + 1, j : j + 1]
        column = work[:, j : j + 1]
        pivots = jnp.where(index == j, pivot, pivots)
        if j < K - 1:
            first = j // 8 * 8
            below = jnp.where(index[first:] > j, column[first:], 0.0)
            rest = work[first:] - below * (row / pivot)
            work = jnp.concatenate([work[:first], rest], axis=0) if first else rest
    inverse = work[:, K:] * lax.rsqrt(pivots)
    projected = image[...] - top * root[...] / total
    vectors = jnp.dot(
        inverse, projected, precision=lax.Precision.HIGHEST, preferred_element_type=F32
    )
    if out.dtype == BF16:
        out[...] = (vectors * inv_root[...]).astype(BF16)
    else:
        out[...] = vectors


def orthonormalize(message, image, inv_root, root, scale, dtype):
    vmem = pl.BlockSpec(memory_space=pltpu.VMEM)
    return pl.pallas_call(
        functools.partial(orthonormalize_kernel, scale),
        out_shape=jax.ShapeDtypeStruct((K, TILE), dtype),
        in_specs=[vmem] * 4,
        out_specs=vmem,
        compiler_params=pltpu.CompilerParams(vmem_limit_bytes=VMEM_LIMIT),
        name="orthonormalize",
    )(message, image, inv_root, root)


def swap_cores(value):
    return lax.ppermute(value, "core", [(0, 1), (1, 0)])


def share(value, axes):
    size = lax.axis_size(axes)
    return lax.all_to_all(
        jnp.broadcast_to(value[None], (size,) + value.shape), axes, 0, 0, tiled=True
    )


def share_row(value):
    mine = share(value, ("y", "zh"))
    other = swap_cores(mine)
    first = lax.axis_index("core") == 0
    pair = jnp.where(first, jnp.stack([mine, other], 1), jnp.stack([other, mine], 1))
    return pair.reshape((BLOCK_TILES,) + value.shape)


def sum_all(message):
    rows = message.shape[0] // 2
    core = lax.axis_index("core")
    keep = lax.dynamic_slice_in_dim(message, core * rows, rows, 0)
    give = lax.dynamic_slice_in_dim(message, (1 - core) * rows, rows, 0)
    summed = jnp.sum(share(keep + swap_cores(give), CHIPS), axis=0)
    other = swap_cores(summed)
    first = core == 0
    return jnp.concatenate([jnp.where(first, summed, other), jnp.where(first, other, summed)], 0)


def shards(embeddings, labels, pair_rows, pair_cols, pair_count):
    slab_index = lax.axis_index(ROW)
    block_index = lax.axis_index(COL)
    head = jnp.stack([pair_count[0, 0], slab_index, block_index] + [jnp.int32(0)] * 5)
    info = jnp.concatenate([head, pair_rows[0, 0], pair_cols[0, 0]]).astype(jnp.int32)
    slab = embeddings.reshape(SLAB_TILES, TILE, WIDTH)
    own = lax.dynamic_index_in_dim(slab, block_index, 0, keepdims=False)
    column = lax.all_gather(own, ROW, axis=0)
    half_rows = 0.5 * jnp.sum(jnp.square(slab.astype(F32)), axis=2)
    tiles, partial_degree = build(info, slab, column, half_rows)

    degree = jnp.sum(
        lax.all_to_all(partial_degree.reshape(SLAB_TILES, 1, TILE), COL, 0, 0, tiled=True), axis=0
    )
    inv_root = lax.rsqrt(degree)
    root = jnp.sqrt(degree)
    known = share_row(jnp.concatenate([inv_root, labels.astype(F32)[None]], axis=0))
    column_inv_root = known[:, 0]
    column_labels = known[:, 1].astype(jnp.int32)

    out = None
    for iteration in range(ITERS):
        if iteration == 0:
            running = product(info, tiles, column_labels, column_inv_root)
        else:
            running = product(info, tiles, share_row(out))
        parts = lax.all_to_all(running, COL, 0, 0, tiled=True)
        image, message = weigh(parts, inv_root, root)
        dtype = F32 if iteration == ITERS - 1 else BF16
        out = orthonormalize(
            sum_all(message), image, inv_root, root, 1.0 / (BLOCK_TILES * SLAB_TILES * TILE), dtype
        )
    return out


def solution(mesh):
    fine = Mesh(np.asarray(mesh.devices).reshape(4, 2, 2, 4, 2), ROW + COL)
    in_specs = (
        P(ROW, None),
        P(ROW + COL),
        P(ROW, COL, None),
        P(ROW, COL, None),
        P(ROW, COL),
    )
    return jax.shard_map(
        shards, mesh=fine, in_specs=in_specs, out_specs=P(None, ROW + COL), check_vma=False
    )
```

```python
import functools

import jax
import jax.numpy as jnp
import numpy as np
from jax import lax
from jax.experimental import pallas as pl
from jax.experimental.pallas import tpu as pltpu
from jax.sharding import Mesh
from jax.sharding import PartitionSpec as P

TILE = 512
K = 64
ITERS = 2
PAIRS = 24
WIDTH = 1024
KERNEL_SCALE = 0.5
RATE = 2.0 / KERNEL_SCALE * float(np.log2(np.e))
F32 = jnp.float32
BF16 = jnp.bfloat16

ROW = ("y", "zh", "core")
COL = ("x", "zl")
CHIPS = ("y", "zh", "x", "zl")
SLAB_TILES = 8
BLOCK_TILES = 16
VMEM_LIMIT = 48 * 1024 * 1024


def build_kernel(first, arrived, info, slab, half_rows, *refs):
    columns, refs = refs[:arrived], refs[arrived:]
    if first:
        _, old_degree, *refs = refs
    tiles, degree, order, left, right, made, sem_left, sem_right, sem_out = refs
    live = info[0]
    slab_index = info[1]
    block_index = info[2]
    ahead, stores = left.shape[0] - 1, made.shape[0]
    if first:
        degree[...] = old_degree[...]
    else:
        degree[...] = jnp.zeros_like(degree)

    count = jnp.int32(0)
    group = jnp.int32(-1)
    for s in range(arrived):
        slab_of = info[8 + 2 * PAIRS + first + s]

        def pick(position, carry):
            count, group, seen = carry
            hit = jnp.logical_and(position < live, info[8 + PAIRS + position] == slab_of)
            fresh = jnp.logical_and(hit, jnp.logical_not(seen))
            group = group + fresh.astype(jnp.int32)

            @pl.when(hit)
            def _():
                order[0, count] = position
                order[1, count] = s
                order[2, count] = group
                order[3, count] = fresh.astype(jnp.int32)

            return count + hit.astype(jnp.int32), group, jnp.logical_or(seen, hit)

        count, group, _ = lax.fori_loop(0, PAIRS, pick, (count, group, jnp.bool_(False)))

    def left_copy(entry):
        slot = lax.rem(entry, ahead + 1)
        t = info[8 + order[0, entry]]
        return pltpu.make_async_copy(slab.at[t], left.at[slot], sem_left.at[slot])

    def right_copy(entry, s):
        slot = lax.rem(order[2, entry], right.shape[0])
        return pltpu.make_async_copy(columns[s], right.at[slot], sem_right.at[slot])

    def fetch(entry):
        left_copy(entry).start()
        for s in range(arrived):

            @pl.when(jnp.logical_and(order[3, entry] == 1, order[1, entry] == s))
            def _():
                right_copy(entry, s).start()

    def store(entry):
        slot = lax.rem(entry, stores)
        return pltpu.make_async_copy(made.at[slot], tiles.at[order[0, entry]], sem_out.at[slot])

    for entry in range(ahead):

        @pl.when(entry < count)
        def _():
            fetch(jnp.int32(entry))

    def step(entry, carry):
        @pl.when(entry + ahead < count)
        def _():
            fetch(entry + ahead)

        @pl.when(entry >= stores)
        def _():
            store(entry - stores).wait()

        left_copy(entry).wait()

        @pl.when(order[3, entry] == 1)
        def _():
            right_copy(entry, 0).wait()

        a_slot = lax.rem(entry, ahead + 1)
        b_slot = lax.rem(order[2, entry], right.shape[0])
        m_slot = lax.rem(entry, stores)
        t = info[8 + order[0, entry]]
        b = right[b_slot]
        wide = b.astype(F32)
        half_b = 0.5 * jnp.sum(wide * wide, axis=1, keepdims=True)
        sums = []
        for n in range(2):
            lanes = pl.ds(n * 256, 256)
            inner = lax.dot_general(
                b, left[a_slot, lanes, :], (((1,), (1,)), ((), ())), preferred_element_type=F32
            )
            half_a = half_rows[pl.ds(t, 1), lanes]
            w = jnp.exp2(RATE * ((inner - half_a) - half_b)).astype(BF16)
            made[m_slot, :, lanes] = w
            sums.append(jnp.sum(w.astype(F32), axis=0, keepdims=True))
        old = degree[pl.ds(t, 1), :]
        degree[pl.ds(t, 1), :] = old + jnp.concatenate(sums, axis=1)
        if first == 0:
            q = info[8 + PAIRS + order[0, entry]]

            @pl.when(jnp.logical_and(t == block_index, q == slab_index))
            def _():
                w = made[m_slot]
                same = lax.broadcasted_iota(jnp.int32, (TILE, TILE), 0) == lax.broadcasted_iota(
                    jnp.int32, (TILE, TILE), 1
                )
                w = jnp.where(same, jnp.zeros_like(w), w)
                made[m_slot] = w
                degree[pl.ds(t, 1), :] = old + jnp.sum(w.astype(F32), axis=0, keepdims=True)

        store(entry).start()
        return carry

    lax.fori_loop(0, count, step, 0)
    for back in range(stores):

        @pl.when(count > back)
        def _():
            store(count - 1 - back).wait()


def build(first, info, slab, half_rows, columns, made):
    any_space = pl.BlockSpec(memory_space=pl.ANY)
    vmem = pl.BlockSpec(memory_space=pltpu.VMEM)
    arrived = len(columns)
    pairs = PAIRS * arrived // BLOCK_TILES
    return pl.pallas_call(
        functools.partial(build_kernel, first, arrived),
        out_shape=(
            jax.ShapeDtypeStruct((PAIRS, TILE, TILE), BF16),
            jax.ShapeDtypeStruct((SLAB_TILES, TILE), F32),
        ),
        in_specs=[pl.BlockSpec(memory_space=pltpu.SMEM), any_space, vmem]
        + [any_space] * arrived
        + ([any_space, vmem] if made else []),
        out_specs=(any_space, vmem),
        scratch_shapes=[
            pltpu.SMEM((4, PAIRS), jnp.int32),
            pltpu.VMEM((3, TILE, WIDTH), BF16),
            pltpu.VMEM((3, TILE, WIDTH), BF16),
            pltpu.VMEM((4, TILE, TILE), BF16),
            pltpu.SemaphoreType.DMA((3,)),
            pltpu.SemaphoreType.DMA((3,)),
            pltpu.SemaphoreType.DMA((4,)),
        ],
        input_output_aliases={3 + arrived: 0} if made else {},
        compiler_params=pltpu.CompilerParams(vmem_limit_bytes=20 * 1024 * 1024),
        cost_estimate=pl.CostEstimate(
            flops=pairs * 2 * TILE * TILE * WIDTH,
            bytes_accessed=pairs * 5 * TILE * WIDTH,
            transcendentals=pairs * TILE * TILE,
        ),
        name="build_tiles",
    )(info, slab, half_rows, *columns, *made)


def product_kernel(first, info, tiles, *refs):
    if first:
        labels, inv_root, running, held, sem = refs
    else:
        scaled, running, held, sem = refs
    count = info[0]
    running[...] = jnp.zeros_like(running)
    depth = held.shape[0]

    def fetch(position):
        slot = lax.rem(position, depth)
        return pltpu.make_async_copy(tiles.at[position], held.at[slot], sem.at[slot])

    for ahead in range(depth - 1):

        @pl.when(ahead < count)
        def _():
            fetch(ahead).start()

    def step(position, carry):
        @pl.when(position + depth - 1 < count)
        def _():
            fetch(position + depth - 1).start()

        t = info[8 + position]
        q = info[8 + PAIRS + position]
        if first:
            label = labels[pl.ds(q, 1), :]
            value = inv_root[pl.ds(q, 1), :]
            value = jnp.where(label < K, value, -value)
            mine = (label & (K - 1)) == lax.broadcasted_iota(jnp.int32, (K, TILE), 0)
            piece = jnp.where(mine, jnp.broadcast_to(value, (K, TILE)), 0.0).astype(BF16)
        else:
            piece = scaled[q]
        fetch(position).wait()
        running[t] += jnp.dot(
            piece, held[lax.rem(position, depth)], preferred_element_type=F32
        )
        return carry

    lax.fori_loop(0, count, step, 0)


def product(info, tiles, *operands):
    vmem = pl.BlockSpec(memory_space=pltpu.VMEM)
    return pl.pallas_call(
        functools.partial(product_kernel, len(operands) == 2),
        out_shape=jax.ShapeDtypeStruct((SLAB_TILES, K, TILE), F32),
        in_specs=[
            pl.BlockSpec(memory_space=pltpu.SMEM),
            pl.BlockSpec(memory_space=pl.ANY),
        ]
        + [vmem] * len(operands),
        out_specs=vmem,
        scratch_shapes=[
            pltpu.VMEM((4, TILE, TILE), BF16),
            pltpu.SemaphoreType.DMA((4,)),
        ],
        compiler_params=pltpu.CompilerParams(vmem_limit_bytes=VMEM_LIMIT),
        name="product",
    )(info, tiles, *operands)


def weigh_kernel(parts, inv_root, root, image, message):
    block = jnp.sum(parts[...], axis=0) * inv_root[...]
    image[...] = block
    heavy = jnp.concatenate([block, jnp.broadcast_to(root[...], (8, TILE))], axis=0)
    weights = lax.dot_general(
        heavy,
        heavy,
        (((1,), (1,)), ((), ())),
        precision=lax.Precision.HIGHEST,
        preferred_element_type=F32,
    )
    half = K // 2
    message[...] = jnp.concatenate(
        [
            weights[:half, :half],
            weights[half:K, :half],
            weights[half:K, half:K],
            weights[:half, K : K + 8],
            weights[half:K, K : K + 8],
            jnp.broadcast_to(weights[K : K + 1, K : K + 1], (half, 16)),
        ],
        axis=1,
    )


def weigh(parts, inv_root, root):
    vmem = pl.BlockSpec(memory_space=pltpu.VMEM)
    return pl.pallas_call(
        weigh_kernel,
        out_shape=(
            jax.ShapeDtypeStruct((K, TILE), F32),
            jax.ShapeDtypeStruct((K // 2, 128), F32),
        ),
        in_specs=[vmem] * 3,
        out_specs=(vmem, vmem),
        compiler_params=pltpu.CompilerParams(vmem_limit_bytes=VMEM_LIMIT),
        name="weigh",
    )(parts, inv_root, root)


def orthonormalize_kernel(scale, message, image, inv_root, root, out):
    half = K // 2
    sums = message[...]
    lower = sums[:, half : 2 * half]
    gram = jnp.concatenate(
        [
            jnp.concatenate([sums[:, :half], lower.T], axis=1),
            jnp.concatenate([lower, sums[:, 2 * half : 3 * half]], axis=1),
        ],
        axis=0,
    )
    top = jnp.concatenate([sums[:, 96:97], sums[:, 104:105]], axis=0)
    total = sums[:1, 112:113]
    rows = lax.broadcasted_iota(jnp.int32, (K, K), 0)
    columns = lax.broadcasted_iota(jnp.int32, (K, K), 1)
    across = jnp.sum(jnp.where(rows == columns, top, 0.0), axis=0, keepdims=True)
    gram = (gram - top * across / total) * scale
    work = jnp.concatenate([gram, (rows == columns).astype(F32)], axis=1)
    index = lax.broadcasted_iota(jnp.int32, (K, 1), 0)
    pivots = jnp.ones((K, 1), F32)
    for j in range(K):
        row = work[j : j + 1, :]
        pivot = work[j : j + 1, j : j + 1]
        column = work[:, j : j + 1]
        pivots = jnp.where(index == j, pivot, pivots)
        if j < K - 1:
            first = j // 8 * 8
            below = jnp.where(index[first:] > j, column[first:], 0.0)
            rest = work[first:] - below * (row / pivot)
            work = jnp.concatenate([work[:first], rest], axis=0) if first else rest
    inverse = work[:, K:] * lax.rsqrt(pivots)
    projected = image[...] - top * root[...] / total
    vectors = jnp.dot(
        inverse, projected, precision=lax.Precision.HIGHEST, preferred_element_type=F32
    )
    if out.dtype == BF16:
        out[...] = (vectors * inv_root[...]).astype(BF16)
    else:
        out[...] = vectors


def orthonormalize(message, image, inv_root, root, scale, dtype):
    vmem = pl.BlockSpec(memory_space=pltpu.VMEM)
    return pl.pallas_call(
        functools.partial(orthonormalize_kernel, scale),
        out_shape=jax.ShapeDtypeStruct((K, TILE), dtype),
        in_specs=[vmem] * 4,
        out_specs=vmem,
        compiler_params=pltpu.CompilerParams(vmem_limit_bytes=VMEM_LIMIT),
        name="orthonormalize",
    )(message, image, inv_root, root)


def swap_cores(value):
    return lax.ppermute(value, "core", [(0, 1), (1, 0)])


def share(value, axes):
    size = lax.axis_size(axes)
    return lax.all_to_all(
        jnp.broadcast_to(value[None], (size,) + value.shape), axes, 0, 0, tiled=True
    )


def share_row(value):
    mine = share(value, ("y", "zh"))
    other = swap_cores(mine)
    first = lax.axis_index("core") == 0
    pair = jnp.where(first, jnp.stack([mine, other], 1), jnp.stack([other, mine], 1))
    return pair.reshape((BLOCK_TILES,) + value.shape)


def sum_all(message):
    rows = message.shape[0] // 2
    core = lax.axis_index("core")
    keep = lax.dynamic_slice_in_dim(message, core * rows, rows, 0)
    give = lax.dynamic_slice_in_dim(message, (1 - core) * rows, rows, 0)
    summed = jnp.sum(share(keep + swap_cores(give), CHIPS), axis=0)
    other = swap_cores(summed)
    first = core == 0
    return jnp.concatenate([jnp.where(first, summed, other), jnp.where(first, other, summed)], 0)


def up(value):
    return lax.ppermute(value, "y", [(i, (i + 1) % 4) for i in range(4)])


def down(value):
    return lax.ppermute(value, "y", [(i, (i + 3) % 4) for i in range(4)])


def apart(value):
    return lax.ppermute(
        value,
        ("y", "core"),
        [(2 * i + k, 2 * ((i + 1 + 2 * k) % 4) + k) for i in range(4) for k in range(2)],
    )


def apart_z(value):
    moves = []
    for z in range(4):
        for k in range(2):
            to = (z + 1 + 2 * k) % 4
            moves.append((z // 2 * 4 + k * 2 + z % 2, to // 2 * 4 + k * 2 + to % 2))
    return lax.ppermute(value, ("zh", "core", "zl"), moves)


def cross(value):
    return lax.ppermute(value, ("zh", "zl"), [(0, 3), (3, 0), (1, 2), (2, 1)])


def shards(embeddings, labels, pair_rows, pair_cols, pair_count):
    y, zh, core = (lax.axis_index(a) for a in ROW)
    slab_index = lax.axis_index(ROW)
    block_index = lax.axis_index(COL)
    zero = core == 0
    slab = embeddings.reshape(SLAB_TILES, TILE, WIDTH)

    def of(dy, dz, k):
        return ((y + dy) % 4 * 2 + (zh + dz) % 2) * 2 + k

    side = lambda k: jnp.where(k == 0, 3, 1)
    arrivals = []
    for k in (core, 1 - core):
        arrivals.append(
            [
                of(0, 0, k),
                of(0, 1, k),
                of(3, 0, k),
                of(1, 0, k),
                of(2, 0, k),
                of(side(k), 1, k),
                of(2, 1, k),
                of(4 - side(k), 1, k),
            ]
        )
    arrivals = [q for both in zip(*arrivals, strict=True) for q in both]
    head = [pair_count[0, 0], slab_index, block_index] + [jnp.int32(0)] * 5
    info = jnp.concatenate(
        [jnp.stack(head), pair_rows[0, 0], pair_cols[0, 0], jnp.stack(arrivals)]
    ).astype(jnp.int32)

    own = lax.dynamic_index_in_dim(slab, block_index, 0, keepdims=False)
    give = lax.dynamic_index_in_dim(slab, block_index ^ 1, 0, keepdims=False)
    across = cross(give)
    below = up(own)
    above = down(own)
    beyond = apart(jnp.where(zero, below, above))
    near = apart(across)
    far = apart(near)
    other = apart_z(apart_z(jnp.where(zero, above, below)))
    half_rows = 0.5 * jnp.sum(jnp.square(slab.astype(F32)), axis=2)
    column_labels = share_row(labels[None].astype(F32))[:, 0].astype(jnp.int32)
    made = ()
    first = 0
    for stage in ((own,), (across, below, above), (beyond, near), (far, other)):
        columns = [piece for tile in stage for piece in (tile, swap_cores(tile))]
        made = build(first, info, slab, half_rows, columns, made)
        first += len(columns)
    tiles, partial_degree = made

    spread = jnp.broadcast_to(partial_degree[None, :, None], (8, SLAB_TILES, 1, TILE))
    got = lax.all_to_all(
        spread.reshape(8 * SLAB_TILES, 1, TILE), CHIPS, 0, 0, tiled=True
    )
    mine = jnp.sum(got.reshape(8, SLAB_TILES, TILE), axis=1)
    others = swap_cores(mine)
    column_degree = jnp.where(
        zero, jnp.stack([mine, others], 1), jnp.stack([others, mine], 1)
    ).reshape(BLOCK_TILES, TILE)
    column_inv_root = lax.rsqrt(column_degree)
    degree = lax.dynamic_slice_in_dim(column_degree, slab_index, 1, 0)
    inv_root = lax.rsqrt(degree)
    root = jnp.sqrt(degree)

    out = None
    for iteration in range(ITERS):
        if iteration == 0:
            running = product(info, tiles, column_labels, column_inv_root)
        else:
            running = product(info, tiles, share_row(out))
        parts = lax.all_to_all(running, COL, 0, 0, tiled=True)
        image, message = weigh(parts, inv_root, root)
        dtype = F32 if iteration == ITERS - 1 else BF16
        out = orthonormalize(
            sum_all(message), image, inv_root, root, 1.0 / (BLOCK_TILES * SLAB_TILES * TILE), dtype
        )
    return out


def solution(mesh):
    fine = Mesh(np.asarray(mesh.devices).reshape(4, 2, 2, 4, 2), ROW + COL)
    in_specs = (
        P(ROW, None),
        P(ROW + COL),
        P(ROW, COL, None),
        P(ROW, COL, None),
        P(ROW, COL),
    )
    return jax.shard_map(
        shards, mesh=fine, in_specs=in_specs, out_specs=P(None, ROW + COL), check_vma=False
    )
```

```python
import functools

import jax
import jax.numpy as jnp
import numpy as np
from jax import lax
from jax.experimental import pallas as pl
from jax.experimental.pallas import tpu as pltpu
from jax.sharding import Mesh
from jax.sharding import PartitionSpec as P

TILE = 512
K = 64
ITERS = 2
PAIRS = 24
WIDTH = 1024
KERNEL_SCALE = 0.5
RATE = 2.0 / KERNEL_SCALE * float(np.log2(np.e))
F32 = jnp.float32
BF16 = jnp.bfloat16

ROW = ("y", "zh", "core")
COL = ("x", "zl")
CHIPS = ("y", "zh", "x", "zl")
SLAB_TILES = 8
BLOCK_TILES = 16
VMEM_LIMIT = 10 * 1024 * 1024
ROWS, SLABS, RANKS, GROUPS, STARTS = (8 + PAIRS * i for i in range(5))


def build_kernel(first, arrived, info, slab, half_rows, *refs):
    columns, refs = refs[:arrived], refs[arrived:]
    if first:
        _, old_degree, *refs = refs
    tiles, degree, left, right, made, sem_left, sem_right, sem_out = refs
    block_index = info[1]
    ahead, stores = left.shape[0] - 1, made.shape[0]
    if first:
        degree[...] = old_degree[...]
    else:
        degree[...] = jnp.zeros_like(degree)

    begin, end = info[STARTS + first], info[STARTS + first + arrived]

    def left_copy(entry):
        slot = lax.rem(entry, ahead + 1)
        t = info[ROWS + entry]
        return pltpu.make_async_copy(slab.at[t], left.at[slot], sem_left.at[slot])

    def right_copy(entry, s):
        slot = lax.rem(info[GROUPS + entry], right.shape[0])
        return pltpu.make_async_copy(columns[s], right.at[slot], sem_right.at[slot])

    def fresh(entry):
        return jnp.logical_or(entry == begin, info[GROUPS + entry] != info[GROUPS + entry - 1])

    def fetch(entry):
        left_copy(entry).start()
        for s in range(arrived):

            @pl.when(jnp.logical_and(fresh(entry), info[RANKS + entry] == first + s))
            def _():
                right_copy(entry, s).start()

    def store(entry):
        slot = lax.rem(entry, stores)
        return pltpu.make_async_copy(made.at[slot], tiles.at[entry], sem_out.at[slot])

    for entry in range(ahead):

        @pl.when(begin + entry < end)
        def _():
            fetch(begin + entry)

    def step(entry, carry):
        @pl.when(entry + ahead < end)
        def _():
            fetch(entry + ahead)

        @pl.when(entry - begin >= stores)
        def _():
            store(entry - stores).wait()

        left_copy(entry).wait()

        @pl.when(fresh(entry))
        def _():
            right_copy(entry, 0).wait()

        a_slot = lax.rem(entry, ahead + 1)
        b_slot = lax.rem(info[GROUPS + entry], right.shape[0])
        m_slot = lax.rem(entry, stores)
        t = info[ROWS + entry]
        b = right[b_slot]
        wide = b.astype(F32)
        half_b = 0.5 * jnp.sum(wide * wide, axis=1, keepdims=True)
        sums = []
        for n in range(2):
            lanes = pl.ds(n * 256, 256)
            inner = lax.dot_general(
                b, left[a_slot, lanes, :], (((1,), (1,)), ((), ())), preferred_element_type=F32
            )
            half_a = half_rows[pl.ds(t, 1), lanes]
            w = jnp.exp2(RATE * ((inner - half_a) - half_b)).astype(BF16)
            made[m_slot, :, lanes] = w
            sums.append(jnp.sum(w.astype(F32), axis=0, keepdims=True))
        old = degree[pl.ds(t, 1), :]
        degree[pl.ds(t, 1), :] = old + jnp.concatenate(sums, axis=1)
        if first == 0:
            @pl.when(jnp.logical_and(t == block_index, info[RANKS + entry] == 0))
            def _():
                w = made[m_slot]
                same = lax.broadcasted_iota(jnp.int32, (TILE, TILE), 0) == lax.broadcasted_iota(
                    jnp.int32, (TILE, TILE), 1
                )
                w = jnp.where(same, jnp.zeros_like(w), w)
                made[m_slot] = w
                degree[pl.ds(t, 1), :] = old + jnp.sum(w.astype(F32), axis=0, keepdims=True)

        store(entry).start()
        return carry

    lax.fori_loop(begin, end, step, 0)
    for back in range(stores):

        @pl.when(end - begin > back)
        def _():
            store(end - 1 - back).wait()


def build(first, info, slab, half_rows, columns, made):
    any_space = pl.BlockSpec(memory_space=pl.ANY)
    vmem = pl.BlockSpec(memory_space=pltpu.VMEM)
    arrived = len(columns)
    pairs = PAIRS * arrived // BLOCK_TILES
    return pl.pallas_call(
        functools.partial(build_kernel, first, arrived),
        out_shape=(
            jax.ShapeDtypeStruct((PAIRS, TILE, TILE), BF16),
            jax.ShapeDtypeStruct((SLAB_TILES, TILE), F32),
        ),
        in_specs=[pl.BlockSpec(memory_space=pltpu.SMEM), any_space, vmem]
        + [any_space] * arrived
        + ([any_space, vmem] if made else []),
        out_specs=(any_space, vmem),
        scratch_shapes=[
            pltpu.VMEM((3, TILE, WIDTH), BF16),
            pltpu.VMEM((3, TILE, WIDTH), BF16),
            pltpu.VMEM((4, TILE, TILE), BF16),
            pltpu.SemaphoreType.DMA((3,)),
            pltpu.SemaphoreType.DMA((3,)),
            pltpu.SemaphoreType.DMA((4,)),
        ],
        input_output_aliases={3 + arrived: 0} if made else {},
        compiler_params=pltpu.CompilerParams(vmem_limit_bytes=20 * 1024 * 1024),
        cost_estimate=pl.CostEstimate(
            flops=pairs * 2 * TILE * TILE * WIDTH,
            bytes_accessed=pairs * 5 * TILE * WIDTH,
            transcendentals=pairs * TILE * TILE,
        ),
        name="build_tiles",
    )(info, slab, half_rows, *columns, *made)


def product_kernel(first, info, tiles, *refs):
    if first:
        labels, inv_root, running, held, sem = refs
    else:
        scaled, running, held, sem = refs
    count = info[0]
    running[...] = jnp.zeros_like(running)
    depth = held.shape[0]

    def fetch(position):
        slot = lax.rem(position, depth)
        return pltpu.make_async_copy(tiles.at[position], held.at[slot], sem.at[slot])

    for ahead in range(depth - 1):

        @pl.when(ahead < count)
        def _():
            fetch(ahead).start()

    def step(position, carry):
        @pl.when(position + depth - 1 < count)
        def _():
            fetch(position + depth - 1).start()

        t = info[ROWS + position]
        q = info[SLABS + position]
        if first:
            label = labels[pl.ds(q, 1), :]
            value = inv_root[pl.ds(q, 1), :]
            value = jnp.where(label < K, value, -value)
            mine = (label & (K - 1)) == lax.broadcasted_iota(jnp.int32, (K, TILE), 0)
            piece = jnp.where(mine, jnp.broadcast_to(value, (K, TILE)), 0.0).astype(BF16)
        else:
            piece = scaled[q]
        fetch(position).wait()
        running[t] += jnp.dot(
            piece, held[lax.rem(position, depth)], preferred_element_type=F32
        )
        return carry

    lax.fori_loop(0, count, step, 0)


def product(info, tiles, *operands):
    vmem = pl.BlockSpec(memory_space=pltpu.VMEM)
    return pl.pallas_call(
        functools.partial(product_kernel, len(operands) == 2),
        out_shape=jax.ShapeDtypeStruct((SLAB_TILES, K, TILE), F32),
        in_specs=[
            pl.BlockSpec(memory_space=pltpu.SMEM),
            pl.BlockSpec(memory_space=pl.ANY),
        ]
        + [vmem] * len(operands),
        out_specs=vmem,
        scratch_shapes=[
            pltpu.VMEM((4, TILE, TILE), BF16),
            pltpu.SemaphoreType.DMA((4,)),
        ],
        compiler_params=pltpu.CompilerParams(vmem_limit_bytes=VMEM_LIMIT),
        name="product",
    )(info, tiles, *operands)


def weigh_kernel(parts, inv_root, root, image, message):
    block = jnp.sum(parts[...], axis=0) * inv_root[...]
    image[...] = block
    heavy = jnp.concatenate([block, jnp.broadcast_to(root[...], (8, TILE))], axis=0)
    weights = lax.dot_general(
        heavy,
        heavy,
        (((1,), (1,)), ((), ())),
        precision=lax.Precision.HIGHEST,
        preferred_element_type=F32,
    )
    half = K // 2
    message[...] = jnp.concatenate(
        [
            weights[:half, :half],
            weights[half:K, :half],
            weights[half:K, half:K],
            weights[:half, K : K + 8],
            weights[half:K, K : K + 8],
            jnp.broadcast_to(weights[K : K + 1, K : K + 1], (half, 16)),
        ],
        axis=1,
    )


def weigh(parts, inv_root, root):
    vmem = pl.BlockSpec(memory_space=pltpu.VMEM)
    return pl.pallas_call(
        weigh_kernel,
        out_shape=(
            jax.ShapeDtypeStruct((K, TILE), F32),
            jax.ShapeDtypeStruct((K // 2, 128), F32),
        ),
        in_specs=[vmem] * 3,
        out_specs=(vmem, vmem),
        compiler_params=pltpu.CompilerParams(vmem_limit_bytes=VMEM_LIMIT),
        name="weigh",
    )(parts, inv_root, root)


def orthonormalize_kernel(scale, message, image, inv_root, root, out):
    half = K // 2
    sums = message[...]
    lower = sums[:, half : 2 * half]
    gram = jnp.concatenate(
        [
            jnp.concatenate([sums[:, :half], lower.T], axis=1),
            jnp.concatenate([lower, sums[:, 2 * half : 3 * half]], axis=1),
        ],
        axis=0,
    )
    top = jnp.concatenate([sums[:, 96:97], sums[:, 104:105]], axis=0)
    total = sums[:1, 112:113]
    rows = lax.broadcasted_iota(jnp.int32, (K, K), 0)
    columns = lax.broadcasted_iota(jnp.int32, (K, K), 1)
    across = jnp.sum(jnp.where(rows == columns, top, 0.0), axis=0, keepdims=True)
    gram = (gram - top * across / total) * scale
    work = jnp.concatenate([gram, (rows == columns).astype(F32)], axis=1)
    index = lax.broadcasted_iota(jnp.int32, (K, 1), 0)
    pivots = jnp.ones((K, 1), F32)
    for j in range(K):
        row = work[j : j + 1, :]
        pivot = work[j : j + 1, j : j + 1]
        column = work[:, j : j + 1]
        pivots = jnp.where(index == j, pivot, pivots)
        if j < K - 1:
            first = j // 8 * 8
            below = jnp.where(index[first:] > j, column[first:], 0.0)
            rest = work[first:] - below * (row / pivot)
            work = jnp.concatenate([work[:first], rest], axis=0) if first else rest
    inverse = work[:, K:] * lax.rsqrt(pivots)
    projected = image[...] - top * root[...] / total
    vectors = jnp.dot(
        inverse, projected, precision=lax.Precision.HIGHEST, preferred_element_type=F32
    )
    if out.dtype == BF16:
        out[...] = (vectors * inv_root[...]).astype(BF16)
    else:
        out[...] = vectors


def orthonormalize(message, image, inv_root, root, scale, dtype):
    vmem = pl.BlockSpec(memory_space=pltpu.VMEM)
    return pl.pallas_call(
        functools.partial(orthonormalize_kernel, scale),
        out_shape=jax.ShapeDtypeStruct((K, TILE), dtype),
        in_specs=[vmem] * 4,
        out_specs=vmem,
        compiler_params=pltpu.CompilerParams(vmem_limit_bytes=VMEM_LIMIT),
        name="orthonormalize",
    )(message, image, inv_root, root)


def swap_cores(value):
    return lax.ppermute(value, "core", [(0, 1), (1, 0)])


def share(value, axes):
    size = lax.axis_size(axes)
    return lax.all_to_all(
        jnp.broadcast_to(value[None], (size,) + value.shape), axes, 0, 0, tiled=True
    )


def share_row(value):
    mine = share(value, ("y", "zh"))
    other = swap_cores(mine)
    first = lax.axis_index("core") == 0
    pair = jnp.where(first, jnp.stack([mine, other], 1), jnp.stack([other, mine], 1))
    return pair.reshape((BLOCK_TILES,) + value.shape)


def sum_all(message):
    rows = message.shape[0] // 2
    core = lax.axis_index("core")
    keep = lax.dynamic_slice_in_dim(message, core * rows, rows, 0)
    give = lax.dynamic_slice_in_dim(message, (1 - core) * rows, rows, 0)
    summed = jnp.sum(share(keep + swap_cores(give), CHIPS), axis=0)
    other = swap_cores(summed)
    first = core == 0
    return jnp.concatenate([jnp.where(first, summed, other), jnp.where(first, other, summed)], 0)


def up(value):
    return lax.ppermute(value, "y", [(i, (i + 1) % 4) for i in range(4)])


def down(value):
    return lax.ppermute(value, "y", [(i, (i + 3) % 4) for i in range(4)])


def apart(value):
    return lax.ppermute(
        value,
        ("y", "core"),
        [(2 * i + k, 2 * ((i + 1 + 2 * k) % 4) + k) for i in range(4) for k in range(2)],
    )


def apart_z(value):
    moves = []
    for z in range(4):
        for k in range(2):
            to = (z + 1 + 2 * k) % 4
            moves.append((z // 2 * 4 + k * 2 + z % 2, to // 2 * 4 + k * 2 + to % 2))
    return lax.ppermute(value, ("zh", "core", "zl"), moves)


def cross(value):
    return lax.ppermute(value, ("zh", "zl"), [(0, 3), (3, 0), (1, 2), (2, 1)])


def pair_list(count, block_index, rows, slabs, arrivals):
    slot = jnp.arange(PAIRS, dtype=jnp.int32)
    rank = jnp.sum(
        jnp.where(slabs[:, None] == arrivals[None, :], jnp.arange(BLOCK_TILES, dtype=jnp.int32), 0), 1
    )
    key = jnp.where(slot < count, rank * PAIRS + slot, BLOCK_TILES * PAIRS + slot)
    place = jnp.sum((key[None, :] < key[:, None]).astype(jnp.int32), axis=1)
    at = place[None, :] == slot[:, None]

    def ordered(value):
        return jnp.sum(jnp.where(at, value[None, :], 0), axis=1)

    ranks = ordered(rank)
    fresh = jnp.concatenate([jnp.zeros(1, bool), ranks[1:] != ranks[:-1]])
    groups = jnp.sum(jnp.where(slot[None, :] <= slot[:, None], fresh[None, :], False).astype(jnp.int32), 1)
    limit = jnp.arange(BLOCK_TILES + 1, dtype=jnp.int32) * PAIRS
    starts = jnp.sum((key[None, :] < limit[:, None]).astype(jnp.int32), axis=1)
    head = jnp.stack([count, block_index] + [jnp.int32(0)] * 6)
    return jnp.concatenate([head, ordered(rows), ordered(slabs), ranks, groups, starts]).astype(jnp.int32)


def shards(embeddings, labels, pair_rows, pair_cols, pair_count):
    y, zh, core = (lax.axis_index(a) for a in ROW)
    slab_index = lax.axis_index(ROW)
    block_index = lax.axis_index(COL)
    zero = core == 0
    slab = embeddings.reshape(SLAB_TILES, TILE, WIDTH)

    def of(dy, dz, k):
        return ((y + dy) % 4 * 2 + (zh + dz) % 2) * 2 + k

    side = lambda k: jnp.where(k == 0, 3, 1)
    arrivals = []
    for k in (core, 1 - core):
        arrivals.append(
            [
                of(0, 0, k),
                of(0, 1, k),
                of(3, 0, k),
                of(1, 0, k),
                of(2, 0, k),
                of(side(k), 1, k),
                of(2, 1, k),
                of(4 - side(k), 1, k),
            ]
        )
    first, second = arrivals
    arrivals = [q for both in zip(first[:6], second[:6], strict=True) for q in both]
    arrivals = jnp.stack(arrivals + first[6:] + second[6:])
    info = pair_list(pair_count[0, 0], block_index, pair_rows[0, 0], pair_cols[0, 0], arrivals)

    own = lax.dynamic_index_in_dim(slab, block_index, 0, keepdims=False)
    give = lax.dynamic_index_in_dim(slab, block_index ^ 1, 0, keepdims=False)
    across = cross(give)
    below = up(own)
    above = down(own)
    half_rows = 0.5 * jnp.sum(jnp.square(slab.astype(F32)), axis=2)
    column_labels = share_row(labels[None].astype(F32))[:, 0].astype(jnp.int32)

    def both(*pieces):
        return [each for piece in pieces for each in (piece, swap_cores(piece))]

    def after(made, *pieces):
        tied = lax.optimization_barrier((made[1], column_labels) + pieces)
        return (made[0], tied[0]), tied[2:]

    made = build(0, info, slab, half_rows, both(own), ())
    made, (across, below, above) = after(made, across, below, above)
    near = apart(across)
    beyond = apart(jnp.where(zero, below, above))
    other = apart_z(jnp.where(zero, above, below))
    made = build(2, info, slab, half_rows, both(across, below), made)
    made, (near, beyond, other) = after(made, near, beyond, other)
    far = apart(near)
    other = apart_z(other)
    made = build(6, info, slab, half_rows, both(above, beyond, near), made)
    made, last = after(made, far, other)
    made = build(12, info, slab, half_rows, last, made)
    made = build(14, info, slab, half_rows, [swap_cores(piece) for piece in last], made)
    tiles, partial_degree = made

    spread = jnp.broadcast_to(partial_degree[None, :, None], (8, SLAB_TILES, 1, TILE))
    got = lax.all_to_all(
        spread.reshape(8 * SLAB_TILES, 1, TILE), CHIPS, 0, 0, tiled=True
    )
    mine = jnp.sum(got.reshape(8, SLAB_TILES, TILE), axis=1)
    others = swap_cores(mine)
    column_degree = jnp.where(
        zero, jnp.stack([mine, others], 1), jnp.stack([others, mine], 1)
    ).reshape(BLOCK_TILES, TILE)
    column_inv_root = lax.rsqrt(column_degree)
    degree = lax.dynamic_slice_in_dim(column_degree, slab_index, 1, 0)
    inv_root = lax.rsqrt(degree)
    root = jnp.sqrt(degree)

    out = None
    for iteration in range(ITERS):
        if iteration == 0:
            running = product(info, tiles, column_labels, column_inv_root)
        else:
            running = product(info, tiles, share_row(out))
        parts = lax.all_to_all(running, COL, 0, 0, tiled=True)
        image, message = weigh(parts, inv_root, root)
        dtype = F32 if iteration == ITERS - 1 else BF16
        out = orthonormalize(
            sum_all(message), image, inv_root, root, 1.0 / (BLOCK_TILES * SLAB_TILES * TILE), dtype
        )
    return out


def solution(mesh):
    fine = Mesh(np.asarray(mesh.devices).reshape(4, 2, 2, 4, 2), ROW + COL)
    in_specs = (
        P(ROW, None),
        P(ROW + COL),
        P(ROW, COL, None),
        P(ROW, COL, None),
        P(ROW, COL),
    )
    return jax.shard_map(
        shards, mesh=fine, in_specs=in_specs, out_specs=P(None, ROW + COL), check_vma=False
    )
```

```python
import functools

import jax
import jax.numpy as jnp
import numpy as np
from jax import lax
from jax.experimental import pallas as pl
from jax.experimental.pallas import tpu as pltpu
from jax.sharding import Mesh
from jax.sharding import PartitionSpec as P

TILE = 512
K = 64
PAIRS = 24
WIDTH = 1024
KERNEL_SCALE = 0.5
RATE = 2.0 / KERNEL_SCALE * float(np.log2(np.e))
F32 = jnp.float32
BF16 = jnp.bfloat16

ROW = ("y", "zh", "core")
COL = ("x", "zl")
CHIPS = ("y", "zh", "x", "zl")
SLAB_TILES = 8
BLOCK_TILES = 16
VMEM_LIMIT = 10 * 1024 * 1024
ROWS, SLABS, RANKS, GROUPS, STARTS = (8 + PAIRS * i for i in range(5))


def build_kernel(first, arrived, info, slab, half_rows, *refs):
    columns, refs = refs[:arrived], refs[arrived:]
    if first:
        _, old_degree, *refs = refs
    tiles, degree, left, right, made, sem_left, sem_right, sem_out = refs
    block_index = info[1]
    ahead, stores = left.shape[0] - 1, made.shape[0]
    if first:
        degree[...] = old_degree[...]
    else:
        degree[...] = jnp.zeros_like(degree)

    begin, end = info[STARTS + first], info[STARTS + first + arrived]

    def left_copy(entry):
        slot = lax.rem(entry, ahead + 1)
        t = info[ROWS + entry]
        return pltpu.make_async_copy(slab.at[t], left.at[slot], sem_left.at[slot])

    def right_copy(entry, s):
        slot = lax.rem(info[GROUPS + entry], right.shape[0])
        return pltpu.make_async_copy(columns[s], right.at[slot], sem_right.at[slot])

    def fresh(entry):
        return jnp.logical_or(entry == begin, info[GROUPS + entry] != info[GROUPS + entry - 1])

    def fetch(entry):
        left_copy(entry).start()
        for s in range(arrived):

            @pl.when(jnp.logical_and(fresh(entry), info[RANKS + entry] == first + s))
            def _():
                right_copy(entry, s).start()

    def store(entry):
        slot = lax.rem(entry, stores)
        return pltpu.make_async_copy(made.at[slot], tiles.at[entry], sem_out.at[slot])

    for entry in range(ahead):

        @pl.when(begin + entry < end)
        def _():
            fetch(begin + entry)

    def step(entry, carry):
        @pl.when(entry + ahead < end)
        def _():
            fetch(entry + ahead)

        @pl.when(entry - begin >= stores)
        def _():
            store(entry - stores).wait()

        left_copy(entry).wait()

        @pl.when(fresh(entry))
        def _():
            right_copy(entry, 0).wait()

        a_slot = lax.rem(entry, ahead + 1)
        b_slot = lax.rem(info[GROUPS + entry], right.shape[0])
        m_slot = lax.rem(entry, stores)
        t = info[ROWS + entry]
        b = right[b_slot]
        wide = b.astype(F32)
        half_b = 0.5 * jnp.sum(wide * wide, axis=1, keepdims=True)
        sums = []
        for n in range(2):
            lanes = pl.ds(n * 256, 256)
            inner = lax.dot_general(
                b, left[a_slot, lanes, :], (((1,), (1,)), ((), ())), preferred_element_type=F32
            )
            half_a = half_rows[pl.ds(t, 1), lanes]
            w = jnp.exp2(RATE * ((inner - half_a) - half_b)).astype(BF16)
            made[m_slot, :, lanes] = w
            sums.append(jnp.sum(w.astype(F32), axis=0, keepdims=True))
        old = degree[pl.ds(t, 1), :]
        degree[pl.ds(t, 1), :] = old + jnp.concatenate(sums, axis=1)
        if first == 0:
            @pl.when(jnp.logical_and(t == block_index, info[RANKS + entry] == 0))
            def _():
                w = made[m_slot]
                same = lax.broadcasted_iota(jnp.int32, (TILE, TILE), 0) == lax.broadcasted_iota(
                    jnp.int32, (TILE, TILE), 1
                )
                w = jnp.where(same, jnp.zeros_like(w), w)
                made[m_slot] = w
                degree[pl.ds(t, 1), :] = old + jnp.sum(w.astype(F32), axis=0, keepdims=True)

        store(entry).start()
        return carry

    lax.fori_loop(begin, end, step, 0)
    for back in range(stores):

        @pl.when(end - begin > back)
        def _():
            store(end - 1 - back).wait()


def build(first, info, slab, half_rows, columns, made):
    any_space = pl.BlockSpec(memory_space=pl.ANY)
    hbm = pl.BlockSpec(memory_space=pltpu.HBM)
    vmem = pl.BlockSpec(memory_space=pltpu.VMEM)
    arrived = len(columns)
    pairs = PAIRS * arrived // BLOCK_TILES
    return pl.pallas_call(
        functools.partial(build_kernel, first, arrived),
        out_shape=(
            jax.ShapeDtypeStruct((PAIRS, TILE, TILE), BF16),
            jax.ShapeDtypeStruct((SLAB_TILES, TILE), F32),
        ),
        in_specs=[pl.BlockSpec(memory_space=pltpu.SMEM), hbm, vmem]
        + [any_space] * arrived
        + ([hbm, vmem] if made else []),
        out_specs=(hbm, vmem),
        scratch_shapes=[
            pltpu.VMEM((3, TILE, WIDTH), BF16),
            pltpu.VMEM((3, TILE, WIDTH), BF16),
            pltpu.VMEM((4, TILE, TILE), BF16),
            pltpu.SemaphoreType.DMA((3,)),
            pltpu.SemaphoreType.DMA((3,)),
            pltpu.SemaphoreType.DMA((4,)),
        ],
        input_output_aliases={3 + arrived: 0} if made else {},
        compiler_params=pltpu.CompilerParams(vmem_limit_bytes=20 * 1024 * 1024),
        cost_estimate=pl.CostEstimate(
            flops=pairs * 2 * TILE * TILE * WIDTH,
            bytes_accessed=pairs * 5 * TILE * WIDTH,
            transcendentals=pairs * TILE * TILE,
        ),
        name="build_tiles",
    )(info, slab, half_rows, *columns, *made)


def product_kernel(first, info, tiles, *refs):
    if first:
        labels, inv_root, running, held, sem = refs
    else:
        mine, others, inv_root, running, held, sem = refs
    count, core = info[0], info[2]
    depth = held.shape[0]
    running[...] = jnp.zeros_like(running)
    if not first:
        rest = jnp.sum(mine[:, K:, :], axis=0) + jnp.sum(others[:, K:, :], axis=0)
        for t in range(SLAB_TILES):
            running[t, K:, :] = rest

    def fetch(entry):
        slot = lax.rem(entry, depth)
        return pltpu.make_async_copy(tiles.at[entry], held.at[slot], sem.at[slot])

    def piece(entry):
        q = info[SLABS + entry]
        value = inv_root[pl.ds(q, 1), :]
        if first:
            label = labels[pl.ds(q, 1), :]
            value = jnp.where(label < K, value, -value)
            same = (label & (K - 1)) == lax.broadcasted_iota(jnp.int32, (K, TILE), 0)
            return jnp.where(same, jnp.broadcast_to(value, (K, TILE)), 0.0).astype(BF16)
        chip = q // 2
        vectors = jnp.where(q % 2 == core, mine[chip, :K, :], others[chip, :K, :]) * value
        high = vectors.astype(BF16)
        low = (vectors - high.astype(F32)).astype(BF16)
        return jnp.concatenate([high, low], axis=0)

    def term(entry):
        result = jnp.dot(
            piece(entry), held[lax.rem(entry, depth)], preferred_element_type=F32
        )
        return result if first else result[:K] + result[K:]

    for entry in range(depth - 2):

        @pl.when(entry < count)
        def _():
            fetch(jnp.int32(entry)).start()

    def step(pair, carry):
        one = 2 * pair
        two = one + 1
        for entry in (one, two):

            @pl.when(entry + depth - 2 < count)
            def _():
                fetch(entry + depth - 2).start()

        fetch(one).wait()

        @pl.when(two < count)
        def _():
            fetch(two).wait()

        one_term, two_term = term(one), term(two)
        running[info[ROWS + one], :K, :] += one_term
        running[info[ROWS + two], :K, :] += jnp.where(two < count, two_term, 0.0)
        return carry

    lax.fori_loop(0, (count + 1) // 2, step, 0)


def product(info, tiles, *operands):
    vmem = pl.BlockSpec(memory_space=pltpu.VMEM)
    first = len(operands) == 2
    return pl.pallas_call(
        functools.partial(product_kernel, first),
        out_shape=jax.ShapeDtypeStruct((SLAB_TILES, K if first else K + 8, TILE), F32),
        in_specs=[
            pl.BlockSpec(memory_space=pltpu.SMEM),
            pl.BlockSpec(memory_space=pltpu.HBM),
        ]
        + [vmem] * len(operands),
        out_specs=vmem,
        scratch_shapes=[
            pltpu.VMEM((8, TILE, TILE), BF16),
            pltpu.SemaphoreType.DMA((8,)),
        ],
        compiler_params=pltpu.CompilerParams(vmem_limit_bytes=20 * 1024 * 1024),
        name="product",
    )(info, tiles, *operands)


def weights_of(image, root):
    heavy = jnp.concatenate([image, jnp.broadcast_to(root, (8, TILE))], axis=0)
    weights = lax.dot_general(
        heavy,
        heavy,
        (((1,), (1,)), ((), ())),
        precision=lax.Precision.HIGHEST,
        preferred_element_type=F32,
    )
    half = K // 2
    return jnp.concatenate(
        [
            weights[:half, :half],
            weights[half:K, :half],
            weights[half:K, half:K],
            weights[:half, K : K + 8],
            weights[half:K, K : K + 8],
            jnp.broadcast_to(weights[K : K + 1, K : K + 1], (half, 16)),
        ],
        axis=1,
    )


def factor_of(sums, scale):
    half = K // 2
    lower = sums[:, half : 2 * half]
    gram = jnp.concatenate(
        [
            jnp.concatenate([sums[:, :half], lower.T], axis=1),
            jnp.concatenate([lower, sums[:, 2 * half : 3 * half]], axis=1),
        ],
        axis=0,
    )
    top = jnp.concatenate([sums[:, 96:97], sums[:, 104:105]], axis=0)
    total = sums[:1, 112:113]
    rows = lax.broadcasted_iota(jnp.int32, (K, K), 0)
    columns = lax.broadcasted_iota(jnp.int32, (K, K), 1)
    across = jnp.sum(jnp.where(rows == columns, top, 0.0), axis=0, keepdims=True)
    gram = (gram - top * across / total) * scale
    work = jnp.concatenate([gram, (rows == columns).astype(F32)], axis=1)
    index = lax.broadcasted_iota(jnp.int32, (K, 1), 0)
    pivots = jnp.ones((K, 1), F32)
    for j in range(K):
        row = work[j : j + 1, :]
        pivot = work[j : j + 1, j : j + 1]
        column = work[:, j : j + 1]
        pivots = jnp.where(index == j, pivot, pivots)
        if j < K - 1:
            first = j // 8 * 8
            below = jnp.where(index[first:] > j, column[first:], 0.0)
            rest = work[first:] - below * (row / pivot)
            work = jnp.concatenate([work[:first], rest], axis=0) if first else rest
    return work[:, K:] * lax.rsqrt(pivots), top / total


def times(factor, block):
    return jnp.dot(factor, block, precision=lax.Precision.HIGHEST, preferred_element_type=F32)


def weigh_kernel(parts, inv_root, root, out):
    image = jnp.sum(parts[...], axis=0) * inv_root[...]
    out[:K, :] = image
    packed = weights_of(image, root[...])
    out[K:, :] = jnp.concatenate([packed[8 * i : 8 * i + 8] for i in range(4)], axis=1)


def middle_kernel(scale, parts, inv_root, root, image, message):
    sums = jnp.sum(parts[...], axis=0)
    packed = jnp.concatenate([sums[K:, 128 * i : 128 * i + 128] for i in range(4)], axis=0)
    factor, lead = factor_of(packed, scale)
    block = times(factor, sums[:K] * inv_root[...] - lead * root[...])
    image[...] = block
    message[...] = weights_of(block, root[...])


def last_kernel(scale, message, image, root, out):
    factor, lead = factor_of(message[...], scale)
    out[...] = times(factor, image[...] - lead * root[...])


def local(kernel, name, out_shape, *operands):
    vmem = pl.BlockSpec(memory_space=pltpu.VMEM)
    return pl.pallas_call(
        kernel,
        out_shape=jax.tree.map(lambda shape: jax.ShapeDtypeStruct(shape, F32), out_shape, is_leaf=lambda x: isinstance(x[0], int)),
        in_specs=[vmem] * len(operands),
        out_specs=jax.tree.map(lambda shape: vmem, out_shape, is_leaf=lambda x: isinstance(x[0], int)),
        compiler_params=pltpu.CompilerParams(vmem_limit_bytes=VMEM_LIMIT),
        name=name,
    )(*operands)


def swap_cores(value):
    return lax.ppermute(value, "core", [(0, 1), (1, 0)])


def share(value, axes):
    size = lax.axis_size(axes)
    return lax.all_to_all(
        jnp.broadcast_to(value[None], (size,) + value.shape), axes, 0, 0, tiled=True
    )


def share_row(value):
    mine = share(value, ("y", "zh"))
    return mine, swap_cores(mine)


def sum_all(message):
    rows = message.shape[0] // 2
    core = lax.axis_index("core")
    keep = lax.dynamic_slice_in_dim(message, core * rows, rows, 0)
    give = lax.dynamic_slice_in_dim(message, (1 - core) * rows, rows, 0)
    summed = jnp.sum(share(keep + swap_cores(give), CHIPS), axis=0)
    other = swap_cores(summed)
    first = core == 0
    return jnp.concatenate([jnp.where(first, summed, other), jnp.where(first, other, summed)], 0)


def up(value):
    return lax.ppermute(value, "y", [(i, (i + 1) % 4) for i in range(4)])


def down(value):
    return lax.ppermute(value, "y", [(i, (i + 3) % 4) for i in range(4)])


def apart(value):
    return lax.ppermute(
        value,
        ("y", "core"),
        [(2 * i + k, 2 * ((i + 1 + 2 * k) % 4) + k) for i in range(4) for k in range(2)],
    )


def apart_z(value):
    moves = []
    for z in range(4):
        for k in range(2):
            to = (z + 1 + 2 * k) % 4
            moves.append((z // 2 * 4 + k * 2 + z % 2, to // 2 * 4 + k * 2 + to % 2))
    return lax.ppermute(value, ("zh", "core", "zl"), moves)


def cross(value):
    return lax.ppermute(value, ("zh", "zl"), [(0, 3), (3, 0), (1, 2), (2, 1)])


def pair_list(count, block_index, core, rows, slabs, arrivals):
    slot = jnp.arange(PAIRS, dtype=jnp.int32)
    rank = jnp.sum(
        jnp.where(slabs[:, None] == arrivals[None, :], jnp.arange(BLOCK_TILES, dtype=jnp.int32), 0), 1
    )
    key = jnp.where(slot < count, rank * PAIRS + slot, BLOCK_TILES * PAIRS + slot)
    place = jnp.sum((key[None, :] < key[:, None]).astype(jnp.int32), axis=1)
    at = place[None, :] == slot[:, None]

    def ordered(value):
        return jnp.sum(jnp.where(at, value[None, :], 0), axis=1)

    ranks = ordered(rank)
    fresh = jnp.concatenate([jnp.zeros(1, bool), ranks[1:] != ranks[:-1]])
    groups = jnp.sum(jnp.where(slot[None, :] <= slot[:, None], fresh[None, :], False).astype(jnp.int32), 1)
    limit = jnp.arange(BLOCK_TILES + 1, dtype=jnp.int32) * PAIRS
    starts = jnp.sum((key[None, :] < limit[:, None]).astype(jnp.int32), axis=1)
    head = jnp.stack([count, block_index, core] + [jnp.int32(0)] * 5)
    return jnp.concatenate([head, ordered(rows), ordered(slabs), ranks, groups, starts]).astype(jnp.int32)


def shards(embeddings, labels, pair_rows, pair_cols, pair_count):
    y, zh, core = (lax.axis_index(a) for a in ROW)
    slab_index = lax.axis_index(ROW)
    block_index = lax.axis_index(COL)
    zero = core == 0
    slab = embeddings.reshape(SLAB_TILES, TILE, WIDTH)

    def of(dy, dz, k):
        return ((y + dy) % 4 * 2 + (zh + dz) % 2) * 2 + k

    side = lambda k: jnp.where(k == 0, 3, 1)
    arrivals = []
    for k in (core, 1 - core):
        arrivals.append(
            [
                of(0, 0, k),
                of(0, 1, k),
                of(3, 0, k),
                of(1, 0, k),
                of(2, 0, k),
                of(side(k), 1, k),
                of(2, 1, k),
                of(4 - side(k), 1, k),
            ]
        )
    first, second = arrivals
    arrivals = [q for both in zip(first[:6], second[:6], strict=True) for q in both]
    arrivals = jnp.stack(arrivals + first[6:] + second[6:])
    info = pair_list(pair_count[0, 0], block_index, core, pair_rows[0, 0], pair_cols[0, 0], arrivals)

    own = lax.dynamic_index_in_dim(slab, block_index, 0, keepdims=False)
    give = lax.dynamic_index_in_dim(slab, block_index ^ 1, 0, keepdims=False)
    across = cross(give)
    below = up(own)
    above = down(own)
    half_rows = 0.5 * jnp.sum(jnp.square(slab.astype(F32)), axis=2)
    column_labels = lax.all_gather(labels, ROW, axis=0)

    def both(*pieces):
        return [each for piece in pieces for each in (piece, swap_cores(piece))]

    def after(made, *pieces):
        tied = lax.optimization_barrier((made[1],) + pieces)
        return (made[0], tied[0]), tied[1:]

    made = build(0, info, slab, half_rows, both(own), ())
    made, (across, below, above) = after(made, across, below, above)
    near = apart(across)
    beyond = apart(jnp.where(zero, below, above))
    other = apart_z(jnp.where(zero, above, below))
    made = build(2, info, slab, half_rows, both(across, below), made)
    made, (near, beyond, other, column_labels) = after(made, near, beyond, other, column_labels)
    far = apart(near)
    other = apart_z(other)
    made = build(6, info, slab, half_rows, both(above, beyond, near), made)
    made, last = after(made, far, other)
    made = build(12, info, slab, half_rows, last, made)
    made = build(14, info, slab, half_rows, [swap_cores(piece) for piece in last], made)
    tiles, partial_degree = made

    spread = jnp.broadcast_to(partial_degree[None, :, None], (8, SLAB_TILES, 1, TILE))
    got = lax.all_to_all(
        spread.reshape(8 * SLAB_TILES, 1, TILE), CHIPS, 0, 0, tiled=True
    )
    mine = jnp.sum(got.reshape(8, SLAB_TILES, TILE), axis=1)
    others = swap_cores(mine)
    column_degree = jnp.where(
        zero, jnp.stack([mine, others], 1), jnp.stack([others, mine], 1)
    ).reshape(BLOCK_TILES, TILE)
    column_inv_root = lax.rsqrt(column_degree)
    degree = lax.dynamic_slice_in_dim(column_degree, slab_index, 1, 0)
    inv_root = lax.rsqrt(degree)
    root = jnp.sqrt(degree)

    scale = 1.0 / (BLOCK_TILES * SLAB_TILES * TILE)
    running = product(info, tiles, column_labels, column_inv_root)
    parts = lax.all_to_all(running, COL, 0, 0, tiled=True)
    weighed = local(weigh_kernel, "weigh", (K + 8, TILE), parts, inv_root, root)
    running = product(info, tiles, *share_row(weighed), column_inv_root)
    parts = lax.all_to_all(running, COL, 0, 0, tiled=True)
    image, message = local(
        functools.partial(middle_kernel, scale), "middle", ((K, TILE), (K // 2, 128)), parts, inv_root, root
    )
    return local(
        functools.partial(last_kernel, scale), "last", (K, TILE), sum_all(message), image, root
    )


def solution(mesh):
    fine = Mesh(np.asarray(mesh.devices).reshape(4, 2, 2, 4, 2), ROW + COL)
    in_specs = (
        P(ROW, None),
        P(ROW + COL),
        P(ROW, COL, None),
        P(ROW, COL, None),
        P(ROW, COL),
    )
    return jax.shard_map(
        shards, mesh=fine, in_specs=in_specs, out_specs=P(None, ROW + COL), check_vma=False
    )
```

```python
import functools

import jax
import jax.numpy as jnp
import numpy as np
from jax import lax
from jax.experimental import pallas as pl
from jax.experimental.pallas import tpu as pltpu
from jax.sharding import Mesh
from jax.sharding import PartitionSpec as P

TILE = 512
K = 64
PAIRS = 24
WIDTH = 1024
KERNEL_SCALE = 0.5
RATE = 2.0 / KERNEL_SCALE * float(np.log2(np.e))
F32 = jnp.float32
BF16 = jnp.bfloat16

ROW = ("y", "zh", "core")
COL = ("x", "zl")
CHIPS = ("y", "zh", "x", "zl")
SLAB_TILES = 8
BLOCK_TILES = 16
VMEM_LIMIT = 10 * 1024 * 1024
ROWS, SLABS, RANKS, GROUPS, STARTS = (8 + PAIRS * i for i in range(5))


def build_kernel(first, arrived, info, slab, half_rows, *refs):
    columns, refs = refs[:arrived], refs[arrived:]
    if first:
        _, old_degree, *refs = refs
    tiles, degree, left, right, made, sem_left, sem_right, sem_out = refs
    block_index = info[1]
    ahead, stores = left.shape[0] - 1, made.shape[0]
    if first:
        degree[...] = old_degree[...]
    else:
        degree[...] = jnp.zeros_like(degree)

    begin, end = info[STARTS + first], info[STARTS + first + arrived]

    def left_copy(entry):
        slot = lax.rem(entry, ahead + 1)
        t = info[ROWS + entry]
        return pltpu.make_async_copy(slab.at[t], left.at[slot], sem_left.at[slot])

    def right_copy(entry, s):
        slot = lax.rem(info[GROUPS + entry], right.shape[0])
        return pltpu.make_async_copy(columns[s], right.at[slot], sem_right.at[slot])

    def fresh(entry):
        return jnp.logical_or(entry == begin, info[GROUPS + entry] != info[GROUPS + entry - 1])

    def fetch(entry):
        left_copy(entry).start()
        for s in range(arrived):

            @pl.when(jnp.logical_and(fresh(entry), info[RANKS + entry] == first + s))
            def _():
                right_copy(entry, s).start()

    def store(entry):
        slot = lax.rem(entry, stores)
        return pltpu.make_async_copy(made.at[slot], tiles.at[entry], sem_out.at[slot])

    for entry in range(ahead):

        @pl.when(begin + entry < end)
        def _():
            fetch(begin + entry)

    def step(entry, carry):
        @pl.when(entry + ahead < end)
        def _():
            fetch(entry + ahead)

        @pl.when(entry - begin >= stores)
        def _():
            store(entry - stores).wait()

        left_copy(entry).wait()

        @pl.when(fresh(entry))
        def _():
            right_copy(entry, 0).wait()

        a_slot = lax.rem(entry, ahead + 1)
        b_slot = lax.rem(info[GROUPS + entry], right.shape[0])
        m_slot = lax.rem(entry, stores)
        t = info[ROWS + entry]
        b = right[b_slot]
        wide = b.astype(F32)
        half_b = 0.5 * jnp.sum(wide * wide, axis=1, keepdims=True)
        sums = []
        for n in range(2):
            lanes = pl.ds(n * 256, 256)
            inner = lax.dot_general(
                b, left[a_slot, lanes, :], (((1,), (1,)), ((), ())), preferred_element_type=F32
            )
            half_a = half_rows[pl.ds(t, 1), lanes]
            w = jnp.exp2(RATE * ((inner - half_a) - half_b)).astype(BF16)
            made[m_slot, :, lanes] = w
            sums.append(jnp.sum(w.astype(F32), axis=0, keepdims=True))
        old = degree[pl.ds(t, 1), :]
        degree[pl.ds(t, 1), :] = old + jnp.concatenate(sums, axis=1)
        if first == 0:
            @pl.when(jnp.logical_and(t == block_index, info[RANKS + entry] == 0))
            def _():
                w = made[m_slot]
                same = lax.broadcasted_iota(jnp.int32, (TILE, TILE), 0) == lax.broadcasted_iota(
                    jnp.int32, (TILE, TILE), 1
                )
                w = jnp.where(same, jnp.zeros_like(w), w)
                made[m_slot] = w
                degree[pl.ds(t, 1), :] = old + jnp.sum(w.astype(F32), axis=0, keepdims=True)

        store(entry).start()
        return carry

    lax.fori_loop(begin, end, step, 0)
    for back in range(stores):

        @pl.when(end - begin > back)
        def _():
            store(end - 1 - back).wait()


def in_hbm(value):
    return pltpu.with_memory_space_constraint(value, pltpu.HBM)


def build(first, info, slab, half_rows, columns, made):
    any_space = pl.BlockSpec(memory_space=pl.ANY)
    hbm = pl.BlockSpec(memory_space=pltpu.HBM)
    vmem = pl.BlockSpec(memory_space=pltpu.VMEM)
    arrived = len(columns)
    pairs = PAIRS * arrived // BLOCK_TILES
    return pl.pallas_call(
        functools.partial(build_kernel, first, arrived),
        out_shape=(
            pltpu.HBM((PAIRS, TILE, TILE), BF16),
            jax.ShapeDtypeStruct((SLAB_TILES, TILE), F32),
        ),
        in_specs=[pl.BlockSpec(memory_space=pltpu.SMEM), hbm, vmem]
        + [any_space] * arrived
        + ([hbm, vmem] if made else []),
        out_specs=(hbm, vmem),
        scratch_shapes=[
            pltpu.VMEM((3, TILE, WIDTH), BF16),
            pltpu.VMEM((3, TILE, WIDTH), BF16),
            pltpu.VMEM((4, TILE, TILE), BF16),
            pltpu.SemaphoreType.DMA((3,)),
            pltpu.SemaphoreType.DMA((3,)),
            pltpu.SemaphoreType.DMA((4,)),
        ],
        input_output_aliases={3 + arrived: 0} if made else {},
        compiler_params=pltpu.CompilerParams(vmem_limit_bytes=20 * 1024 * 1024),
        cost_estimate=pl.CostEstimate(
            flops=pairs * 2 * TILE * TILE * WIDTH,
            bytes_accessed=pairs * 5 * TILE * WIDTH,
            transcendentals=pairs * TILE * TILE,
        ),
        name="build_tiles",
    )(info, in_hbm(slab), half_rows, *columns, *([in_hbm(made[0]), made[1]] if made else []))


def product_kernel(first, info, tiles, *refs):
    if first:
        labels, inv_root, running, held, sem = refs
    else:
        mine, others, inv_root, running, held, sem = refs
    count, core = info[0], info[2]
    depth = held.shape[0]
    running[...] = jnp.zeros_like(running)
    if not first:
        rest = jnp.sum(mine[:, K:, :], axis=0) + jnp.sum(others[:, K:, :], axis=0)
        for t in range(SLAB_TILES):
            running[t, K:, :] = rest

    def fetch(entry):
        slot = lax.rem(entry, depth)
        return pltpu.make_async_copy(tiles.at[entry], held.at[slot], sem.at[slot])

    def piece(entry):
        q = info[SLABS + entry]
        value = inv_root[pl.ds(q, 1), :]
        if first:
            label = labels[pl.ds(q, 1), :]
            value = jnp.where(label < K, value, -value)
            same = (label & (K - 1)) == lax.broadcasted_iota(jnp.int32, (K, TILE), 0)
            return jnp.where(same, jnp.broadcast_to(value, (K, TILE)), 0.0).astype(BF16)
        chip = q // 2
        vectors = jnp.where(q % 2 == core, mine[chip, :K, :], others[chip, :K, :]) * value
        high = vectors.astype(BF16)
        low = (vectors - high.astype(F32)).astype(BF16)
        return jnp.concatenate([high, low], axis=0)

    def term(entry):
        result = jnp.dot(
            piece(entry), held[lax.rem(entry, depth)], preferred_element_type=F32
        )
        return result if first else result[:K] + result[K:]

    for entry in range(depth - 2):

        @pl.when(entry < count)
        def _():
            fetch(jnp.int32(entry)).start()

    def step(pair, carry):
        one = 2 * pair
        two = one + 1
        for entry in (one, two):

            @pl.when(entry + depth - 2 < count)
            def _():
                fetch(entry + depth - 2).start()

        fetch(one).wait()

        @pl.when(two < count)
        def _():
            fetch(two).wait()

        one_term, two_term = term(one), term(two)
        running[info[ROWS + one], :K, :] += one_term
        running[info[ROWS + two], :K, :] += jnp.where(two < count, two_term, 0.0)
        return carry

    lax.fori_loop(0, (count + 1) // 2, step, 0)


def product(info, tiles, *operands):
    vmem = pl.BlockSpec(memory_space=pltpu.VMEM)
    first = len(operands) == 2
    return pl.pallas_call(
        functools.partial(product_kernel, first),
        out_shape=jax.ShapeDtypeStruct((SLAB_TILES, K if first else K + 8, TILE), F32),
        in_specs=[
            pl.BlockSpec(memory_space=pltpu.SMEM),
            pl.BlockSpec(memory_space=pltpu.HBM),
        ]
        + [vmem] * len(operands),
        out_specs=vmem,
        scratch_shapes=[
            pltpu.VMEM((8, TILE, TILE), BF16),
            pltpu.SemaphoreType.DMA((8,)),
        ],
        compiler_params=pltpu.CompilerParams(vmem_limit_bytes=20 * 1024 * 1024),
        name="product",
    )(info, in_hbm(tiles), *operands)


def weights_of(image, root):
    heavy = jnp.concatenate([image, jnp.broadcast_to(root, (8, TILE))], axis=0)
    weights = lax.dot_general(
        heavy,
        heavy,
        (((1,), (1,)), ((), ())),
        precision=lax.Precision.HIGHEST,
        preferred_element_type=F32,
    )
    half = K // 2
    return jnp.concatenate(
        [
            weights[:half, :half],
            weights[half:K, :half],
            weights[half:K, half:K],
            weights[:half, K : K + 8],
            weights[half:K, K : K + 8],
            jnp.broadcast_to(weights[K : K + 1, K : K + 1], (half, 16)),
        ],
        axis=1,
    )


def factor_of(sums, scale):
    half = K // 2
    lower = sums[:, half : 2 * half]
    gram = jnp.concatenate(
        [
            jnp.concatenate([sums[:, :half], lower.T], axis=1),
            jnp.concatenate([lower, sums[:, 2 * half : 3 * half]], axis=1),
        ],
        axis=0,
    )
    top = jnp.concatenate([sums[:, 96:97], sums[:, 104:105]], axis=0)
    total = sums[:1, 112:113]
    rows = lax.broadcasted_iota(jnp.int32, (K, K), 0)
    columns = lax.broadcasted_iota(jnp.int32, (K, K), 1)
    across = jnp.sum(jnp.where(rows == columns, top, 0.0), axis=0, keepdims=True)
    gram = (gram - top * across / total) * scale
    work = jnp.concatenate([gram, (rows == columns).astype(F32)], axis=1)
    index = lax.broadcasted_iota(jnp.int32, (K, 1), 0)
    pivots = jnp.ones((K, 1), F32)
    for j in range(K):
        row = work[j : j + 1, :]
        pivot = work[j : j + 1, j : j + 1]
        column = work[:, j : j + 1]
        pivots = jnp.where(index == j, pivot, pivots)
        if j < K - 1:
            first = j // 8 * 8
            below = jnp.where(index[first:] > j, column[first:], 0.0)
            rest = work[first:] - below * (row / pivot)
            work = jnp.concatenate([work[:first], rest], axis=0) if first else rest
    return work[:, K:] * lax.rsqrt(pivots), top / total


def times(factor, block):
    return jnp.dot(factor, block, precision=lax.Precision.HIGHEST, preferred_element_type=F32)


def weigh_kernel(parts, inv_root, root, out):
    image = jnp.sum(parts[...], axis=0) * inv_root[...]
    out[:K, :] = image
    packed = weights_of(image, root[...])
    out[K:, :] = jnp.concatenate([packed[8 * i : 8 * i + 8] for i in range(4)], axis=1)


def middle_kernel(scale, parts, inv_root, root, image, message):
    sums = jnp.sum(parts[...], axis=0)
    packed = jnp.concatenate([sums[K:, 128 * i : 128 * i + 128] for i in range(4)], axis=0)
    factor, lead = factor_of(packed, scale)
    block = times(factor, sums[:K] * inv_root[...] - lead * root[...])
    image[...] = block
    message[...] = weights_of(block, root[...])


def last_kernel(scale, message, image, root, out):
    factor, lead = factor_of(message[...], scale)
    out[...] = times(factor, image[...] - lead * root[...])


def local(kernel, name, out_shape, *operands):
    vmem = pl.BlockSpec(memory_space=pltpu.VMEM)
    return pl.pallas_call(
        kernel,
        out_shape=jax.tree.map(lambda shape: jax.ShapeDtypeStruct(shape, F32), out_shape, is_leaf=lambda x: isinstance(x[0], int)),
        in_specs=[vmem] * len(operands),
        out_specs=jax.tree.map(lambda shape: vmem, out_shape, is_leaf=lambda x: isinstance(x[0], int)),
        compiler_params=pltpu.CompilerParams(vmem_limit_bytes=VMEM_LIMIT),
        name=name,
    )(*operands)


def swap_cores(value):
    return lax.ppermute(value, "core", [(0, 1), (1, 0)])


def share(value, axes):
    size = lax.axis_size(axes)
    return lax.all_to_all(
        jnp.broadcast_to(value[None], (size,) + value.shape), axes, 0, 0, tiled=True
    )


def share_row(value):
    mine = share(value, ("y", "zh"))
    return mine, swap_cores(mine)


def sum_all(message):
    rows = message.shape[0] // 2
    core = lax.axis_index("core")
    keep = lax.dynamic_slice_in_dim(message, core * rows, rows, 0)
    give = lax.dynamic_slice_in_dim(message, (1 - core) * rows, rows, 0)
    summed = jnp.sum(share(keep + swap_cores(give), CHIPS), axis=0)
    other = swap_cores(summed)
    first = core == 0
    return jnp.concatenate([jnp.where(first, summed, other), jnp.where(first, other, summed)], 0)


def up(value):
    return lax.ppermute(value, "y", [(i, (i + 1) % 4) for i in range(4)])


def down(value):
    return lax.ppermute(value, "y", [(i, (i + 3) % 4) for i in range(4)])


def apart(value):
    return lax.ppermute(
        value,
        ("y", "core"),
        [(2 * i + k, 2 * ((i + 1 + 2 * k) % 4) + k) for i in range(4) for k in range(2)],
    )


def apart_z(value):
    moves = []
    for z in range(4):
        for k in range(2):
            to = (z + 1 + 2 * k) % 4
            moves.append((z // 2 * 4 + k * 2 + z % 2, to // 2 * 4 + k * 2 + to % 2))
    return lax.ppermute(value, ("zh", "core", "zl"), moves)


def cross(value):
    return lax.ppermute(value, ("zh", "zl"), [(0, 3), (3, 0), (1, 2), (2, 1)])


def pair_list(count, block_index, core, rows, slabs, arrivals):
    slot = jnp.arange(PAIRS, dtype=jnp.int32)
    rank = jnp.sum(
        jnp.where(slabs[:, None] == arrivals[None, :], jnp.arange(BLOCK_TILES, dtype=jnp.int32), 0), 1
    )
    key = jnp.where(slot < count, rank * PAIRS + slot, BLOCK_TILES * PAIRS + slot)
    place = jnp.sum((key[None, :] < key[:, None]).astype(jnp.int32), axis=1)
    at = place[None, :] == slot[:, None]

    def ordered(value):
        return jnp.sum(jnp.where(at, value[None, :], 0), axis=1)

    ranks = ordered(rank)
    fresh = jnp.concatenate([jnp.zeros(1, bool), ranks[1:] != ranks[:-1]])
    groups = jnp.sum(jnp.where(slot[None, :] <= slot[:, None], fresh[None, :], False).astype(jnp.int32), 1)
    limit = jnp.arange(BLOCK_TILES + 1, dtype=jnp.int32) * PAIRS
    starts = jnp.sum((key[None, :] < limit[:, None]).astype(jnp.int32), axis=1)
    head = jnp.stack([count, block_index, core] + [jnp.int32(0)] * 5)
    return jnp.concatenate([head, ordered(rows), ordered(slabs), ranks, groups, starts]).astype(jnp.int32)


def shards(embeddings, labels, pair_rows, pair_cols, pair_count):
    y, zh, core = (lax.axis_index(a) for a in ROW)
    slab_index = lax.axis_index(ROW)
    block_index = lax.axis_index(COL)
    zero = core == 0
    slab = embeddings.reshape(SLAB_TILES, TILE, WIDTH)

    def of(dy, dz, k):
        return ((y + dy) % 4 * 2 + (zh + dz) % 2) * 2 + k

    side = lambda k: jnp.where(k == 0, 3, 1)
    arrivals = []
    for k in (core, 1 - core):
        arrivals.append(
            [
                of(0, 0, k),
                of(0, 1, k),
                of(3, 0, k),
                of(1, 0, k),
                of(2, 0, k),
                of(side(k), 1, k),
                of(2, 1, k),
                of(4 - side(k), 1, k),
            ]
        )
    first, second = arrivals
    arrivals = [q for both in zip(first[:6], second[:6], strict=True) for q in both]
    arrivals = jnp.stack(arrivals + first[6:] + second[6:])
    info = pair_list(pair_count[0, 0], block_index, core, pair_rows[0, 0], pair_cols[0, 0], arrivals)

    own = lax.dynamic_index_in_dim(slab, block_index, 0, keepdims=False)
    give = lax.dynamic_index_in_dim(slab, block_index ^ 1, 0, keepdims=False)
    across = cross(give)
    below = up(own)
    above = down(own)
    half_rows = 0.5 * jnp.sum(jnp.square(slab.astype(F32)), axis=2)

    def both(*pieces):
        return [each for piece in pieces for each in (piece, swap_cores(piece))]

    def after(made, *pieces):
        tied = lax.optimization_barrier((made[1],) + pieces)
        return (made[0], tied[0]), tied[1:]

    made = build(0, info, slab, half_rows, both(own), ())
    made, (across, below, above) = after(made, across, below, above)
    near = apart(across)
    beyond = apart(jnp.where(zero, below, above))
    other = apart_z(jnp.where(zero, above, below))
    made = build(2, info, slab, half_rows, both(across, below), made)
    made, (near, beyond, other) = after(made, near, beyond, other)
    far = apart(near)
    other = apart_z(other)
    made = build(6, info, slab, half_rows, both(above, beyond, near), made)
    made, last = after(made, far, other)
    made = build(12, info, slab, half_rows, last, made)
    made = build(14, info, slab, half_rows, [swap_cores(piece) for piece in last], made)
    tiles, partial_degree = made

    in_block = jnp.arange(SLAB_TILES)[:, None] == block_index
    sent = jnp.stack([partial_degree, jnp.where(in_block, labels.astype(F32)[None], 0.0)], axis=1)
    got = lax.all_to_all(
        jnp.broadcast_to(sent[None], (8,) + sent.shape).reshape(8 * SLAB_TILES, 2, TILE), CHIPS, 0, 0, tiled=True
    )
    mine = jnp.sum(got.reshape(8, SLAB_TILES, 2, TILE), axis=1)
    others = swap_cores(mine)
    known = jnp.where(zero, jnp.stack([mine, others], 1), jnp.stack([others, mine], 1)).reshape(BLOCK_TILES, 2, TILE)
    column_degree = known[:, 0]
    column_labels = known[:, 1].astype(jnp.int32)
    column_inv_root = lax.rsqrt(column_degree)
    degree = lax.dynamic_slice_in_dim(column_degree, slab_index, 1, 0)
    inv_root = lax.rsqrt(degree)
    root = jnp.sqrt(degree)

    scale = 1.0 / (BLOCK_TILES * SLAB_TILES * TILE)
    running = product(info, tiles, column_labels, column_inv_root)
    parts = lax.all_to_all(running, COL, 0, 0, tiled=True)
    weighed = local(weigh_kernel, "weigh", (K + 8, TILE), parts, inv_root, root)
    running = product(info, tiles, *share_row(weighed), column_inv_root)
    parts = lax.all_to_all(running, COL, 0, 0, tiled=True)
    image, message = local(
        functools.partial(middle_kernel, scale), "middle", ((K, TILE), (K // 2, 128)), parts, inv_root, root
    )
    return local(
        functools.partial(last_kernel, scale), "last", (K, TILE), sum_all(message), image, root
    )


def solution(mesh):
    fine = Mesh(np.asarray(mesh.devices).reshape(4, 2, 2, 4, 2), ROW + COL)
    in_specs = (
        P(ROW, None),
        P(ROW + COL),
        P(ROW, COL, None),
        P(ROW, COL, None),
        P(ROW, COL),
    )
    return jax.shard_map(
        shards, mesh=fine, in_specs=in_specs, out_specs=P(None, ROW + COL), check_vma=False
    )
```

```python
import functools

import jax
import jax.numpy as jnp
import numpy as np
from jax import lax
from jax.experimental import pallas as pl
from jax.experimental.pallas import tpu as pltpu
from jax.sharding import Mesh
from jax.sharding import PartitionSpec as P

TILE = 512
K = 64
PAIRS = 24
WIDTH = 1024
KERNEL_SCALE = 0.5
RATE = 2.0 / KERNEL_SCALE * float(np.log2(np.e))
F32 = jnp.float32
BF16 = jnp.bfloat16

ROW = ("y", "zh", "core")
COL = ("x", "zl")
CHIPS = ("y", "zh", "x", "zl")
SLAB_TILES = 8
BLOCK_TILES = 16
VMEM_LIMIT = 10 * 1024 * 1024
ROWS, SLABS, RANKS, GROUPS, STARTS = (8 + PAIRS * i for i in range(5))


def build_kernel(first, arrived, info, slab, half_rows, *refs):
    columns, refs = refs[:arrived], refs[arrived:]
    if first:
        _, old_degree, *refs = refs
    tiles, degree, left, right, made, sem_left, sem_right, sem_out = refs
    block_index = info[1]
    ahead, stores = left.shape[0] - 1, made.shape[0]
    if first:
        degree[...] = old_degree[...]
    else:
        degree[...] = jnp.zeros_like(degree)

    begin, end = info[STARTS + first], info[STARTS + first + arrived]

    def left_copy(entry):
        slot = lax.rem(entry, ahead + 1)
        t = info[ROWS + entry]
        return pltpu.make_async_copy(slab.at[t], left.at[slot], sem_left.at[slot])

    def right_copy(entry, s):
        slot = lax.rem(info[GROUPS + entry], right.shape[0])
        return pltpu.make_async_copy(columns[s], right.at[slot], sem_right.at[slot])

    def fresh(entry):
        return jnp.logical_or(entry == begin, info[GROUPS + entry] != info[GROUPS + entry - 1])

    def fetch(entry):
        left_copy(entry).start()
        for s in range(arrived):

            @pl.when(jnp.logical_and(fresh(entry), info[RANKS + entry] == first + s))
            def _():
                right_copy(entry, s).start()

    def store(entry):
        slot = lax.rem(entry, stores)
        return pltpu.make_async_copy(made.at[slot], tiles.at[entry], sem_out.at[slot])

    for entry in range(ahead):

        @pl.when(begin + entry < end)
        def _():
            fetch(begin + entry)

    def step(entry, carry):
        @pl.when(entry + ahead < end)
        def _():
            fetch(entry + ahead)

        @pl.when(entry - begin >= stores)
        def _():
            store(entry - stores).wait()

        left_copy(entry).wait()

        @pl.when(fresh(entry))
        def _():
            right_copy(entry, 0).wait()

        a_slot = lax.rem(entry, ahead + 1)
        b_slot = lax.rem(info[GROUPS + entry], right.shape[0])
        m_slot = lax.rem(entry, stores)
        t = info[ROWS + entry]
        b = right[b_slot]
        wide = b.astype(F32)
        half_b = 0.5 * jnp.sum(wide * wide, axis=1, keepdims=True)
        sums = []
        for n in range(2):
            lanes = pl.ds(n * 256, 256)
            inner = lax.dot_general(
                b, left[a_slot, lanes, :], (((1,), (1,)), ((), ())), preferred_element_type=F32
            )
            half_a = half_rows[pl.ds(t, 1), lanes]
            w = jnp.exp2(RATE * ((inner - half_a) - half_b)).astype(BF16)
            made[m_slot, :, lanes] = w
            sums.append(jnp.sum(w.astype(F32), axis=0, keepdims=True))
        old = degree[pl.ds(t, 1), :]
        degree[pl.ds(t, 1), :] = old + jnp.concatenate(sums, axis=1)
        if first == 0:
            @pl.when(jnp.logical_and(t == block_index, info[RANKS + entry] == 0))
            def _():
                w = made[m_slot]
                same = lax.broadcasted_iota(jnp.int32, (TILE, TILE), 0) == lax.broadcasted_iota(
                    jnp.int32, (TILE, TILE), 1
                )
                w = jnp.where(same, jnp.zeros_like(w), w)
                made[m_slot] = w
                degree[pl.ds(t, 1), :] = old + jnp.sum(w.astype(F32), axis=0, keepdims=True)

        store(entry).start()
        return carry

    lax.fori_loop(begin, end, step, 0)
    for back in range(stores):

        @pl.when(end - begin > back)
        def _():
            store(end - 1 - back).wait()


def in_hbm(value):
    return pltpu.with_memory_space_constraint(value, pltpu.HBM)


def build(first, info, slab, half_rows, columns, made):
    any_space = pl.BlockSpec(memory_space=pl.ANY)
    hbm = pl.BlockSpec(memory_space=pltpu.HBM)
    vmem = pl.BlockSpec(memory_space=pltpu.VMEM)
    arrived = len(columns)
    pairs = PAIRS * arrived // BLOCK_TILES
    return pl.pallas_call(
        functools.partial(build_kernel, first, arrived),
        out_shape=(
            pltpu.HBM((PAIRS, TILE, TILE), BF16),
            jax.ShapeDtypeStruct((SLAB_TILES, TILE), F32),
        ),
        in_specs=[pl.BlockSpec(memory_space=pltpu.SMEM), hbm, vmem]
        + [any_space] * arrived
        + ([hbm, vmem] if made else []),
        out_specs=(hbm, vmem),
        scratch_shapes=[
            pltpu.VMEM((3, TILE, WIDTH), BF16),
            pltpu.VMEM((3, TILE, WIDTH), BF16),
            pltpu.VMEM((4, TILE, TILE), BF16),
            pltpu.SemaphoreType.DMA((3,)),
            pltpu.SemaphoreType.DMA((3,)),
            pltpu.SemaphoreType.DMA((4,)),
        ],
        input_output_aliases={3 + arrived: 0} if made else {},
        compiler_params=pltpu.CompilerParams(vmem_limit_bytes=20 * 1024 * 1024),
        cost_estimate=pl.CostEstimate(
            flops=pairs * 2 * TILE * TILE * WIDTH,
            bytes_accessed=pairs * 5 * TILE * WIDTH,
            transcendentals=pairs * TILE * TILE,
        ),
        name="build_tiles",
    )(info, in_hbm(slab), half_rows, *columns, *([in_hbm(made[0]), made[1]] if made else []))


def product_kernel(first, info, tiles, *refs):
    if first:
        labels, inv_root, out, running, held, sem = refs
    else:
        mine, others, running, held, sem = refs
    count, core = info[0], info[2]
    depth = held.shape[0]
    running[...] = jnp.zeros_like(running)
    if not first:
        rest = jnp.zeros((8, TILE), F32)
        for known in (mine, others):
            terms = jnp.sum(known[:, K:, :].astype(F32), axis=0)
            rest = rest + (terms[:8] + (terms[8:16] + terms[16:24]))
        for t in range(SLAB_TILES):
            running[t, K:, :] = rest

    def fetch(entry):
        slot = lax.rem(entry, depth)
        return pltpu.make_async_copy(tiles.at[entry], held.at[slot], sem.at[slot])

    def piece(entry):
        q = info[SLABS + entry]
        if first:
            value = inv_root[pl.ds(q, 1), :]
            label = labels[pl.ds(q, 1), :]
            value = jnp.where(label < K, value, -value)
            same = (label & (K - 1)) == lax.broadcasted_iota(jnp.int32, (K, TILE), 0)
            return jnp.where(same, jnp.broadcast_to(value, (K, TILE)), 0.0).astype(BF16)
        return jnp.where(q % 2 == core, mine[q // 2, :K, :], others[q // 2, :K, :])

    def term(entry):
        return jnp.dot(piece(entry), held[lax.rem(entry, depth)], preferred_element_type=F32)

    for entry in range(depth - 2):

        @pl.when(entry < count)
        def _():
            fetch(jnp.int32(entry)).start()

    def step(pair, carry):
        one = 2 * pair
        two = one + 1
        for entry in (one, two):

            @pl.when(entry + depth - 2 < count)
            def _():
                fetch(entry + depth - 2).start()

        fetch(one).wait()

        @pl.when(two < count)
        def _():
            fetch(two).wait()

        one_term, two_term = term(one), term(two)
        running[info[ROWS + one], :K, :] += one_term
        running[info[ROWS + two], :K, :] += jnp.where(two < count, two_term, 0.0)
        return carry

    lax.fori_loop(0, (count + 1) // 2, step, 0)
    if first:
        out[...] = running[...].astype(BF16)


def product(info, tiles, *operands):
    vmem = pl.BlockSpec(memory_space=pltpu.VMEM)
    first = operands[0].dtype == jnp.int32
    return pl.pallas_call(
        functools.partial(product_kernel, first),
        out_shape=jax.ShapeDtypeStruct(
            (SLAB_TILES, K if first else K + 8, TILE), BF16 if first else F32
        ),
        in_specs=[
            pl.BlockSpec(memory_space=pltpu.SMEM),
            pl.BlockSpec(memory_space=pltpu.HBM),
        ]
        + [vmem] * len(operands),
        out_specs=vmem,
        scratch_shapes=([pltpu.VMEM((SLAB_TILES, K, TILE), F32)] if first else [])
        + [pltpu.VMEM((8, TILE, TILE), BF16), pltpu.SemaphoreType.DMA((8,))],
        compiler_params=pltpu.CompilerParams(vmem_limit_bytes=20 * 1024 * 1024),
        name="product",
    )(info, in_hbm(tiles), *operands)


def weights_of(image, root):
    heavy = jnp.concatenate([image, jnp.broadcast_to(root, (8, TILE))], axis=0)
    weights = lax.dot_general(
        heavy,
        heavy,
        (((1,), (1,)), ((), ())),
        precision=lax.Precision.HIGHEST,
        preferred_element_type=F32,
    )
    half = K // 2
    return jnp.concatenate(
        [
            weights[:half, :half],
            weights[half:K, :half],
            weights[half:K, half:K],
            weights[:half, K : K + 8],
            weights[half:K, K : K + 8],
            jnp.broadcast_to(weights[K : K + 1, K : K + 1], (half, 16)),
        ],
        axis=1,
    )


def factor_of(sums, scale):
    half = K // 2
    lower = sums[:, half : 2 * half]
    gram = jnp.concatenate(
        [
            jnp.concatenate([sums[:, :half], lower.T], axis=1),
            jnp.concatenate([lower, sums[:, 2 * half : 3 * half]], axis=1),
        ],
        axis=0,
    )
    top = jnp.concatenate([sums[:, 96:97], sums[:, 104:105]], axis=0)
    total = sums[:1, 112:113]
    rows = lax.broadcasted_iota(jnp.int32, (K, K), 0)
    columns = lax.broadcasted_iota(jnp.int32, (K, K), 1)
    across = jnp.sum(jnp.where(rows == columns, top, 0.0), axis=0, keepdims=True)
    gram = (gram - top * across / total) * scale
    work = jnp.concatenate([gram, (rows == columns).astype(F32)], axis=1)
    index = lax.broadcasted_iota(jnp.int32, (K, 2 * K), 0)
    pivots = jnp.ones((K, 2 * K), F32)
    for start in range(0, K, 8):
        index = index[-(K - start) :]
        spread = [
            jnp.broadcast_to(work[start:, j : j + 1], (K - start, 2 * K)) for j in range(start, start + 8)
        ]
        rest = work[start:]
        below = pivots[start:]
        for a in range(8):
            pivot = spread[a][a : a + 1, :]
            below = jnp.where(index == start + a, pivot, below)
            ratio = jnp.where(index > start + a, spread[a] / pivot, 0.0)
            rest = rest - ratio * rest[a : a + 1, :]
            for b in range(a + 1, 8):
                spread[b] = spread[b] - ratio * spread[b][a : a + 1, :]
        work = jnp.concatenate([work[:start], rest], axis=0) if start else rest
        pivots = jnp.concatenate([pivots[:start], below], axis=0) if start else below
    return work[:, K:] * lax.rsqrt(pivots[:, K:]), top / total


def times(factor, block):
    return jnp.dot(factor, block, precision=lax.Precision.HIGHEST, preferred_element_type=F32)


def weigh_kernel(parts, inv_root, root, out):
    image = jnp.sum(parts[...].astype(F32), axis=0) * inv_root[...]
    out[:K, :] = (image * inv_root[...]).astype(BF16)
    packed = weights_of(image, root[...])
    sums = jnp.concatenate([packed[8 * i : 8 * i + 8] for i in range(4)], axis=1)
    high = sums.astype(BF16).astype(F32)
    middle = (sums - high).astype(BF16).astype(F32)
    low = (sums - high) - middle
    out[K:, :] = jnp.concatenate([high, middle, low, jnp.zeros_like(low)], axis=0).astype(BF16)


def middle_kernel(scale, parts, inv_root, root, image, message):
    sums = jnp.sum(parts[...], axis=0)
    packed = jnp.concatenate([sums[K:, 128 * i : 128 * i + 128] for i in range(4)], axis=0)
    factor, lead = factor_of(packed, scale)
    block = times(factor, sums[:K] * inv_root[...] - lead * root[...])
    image[...] = block
    message[...] = weights_of(block, root[...])


def last_kernel(scale, message, image, root, out):
    factor, lead = factor_of(message[...], scale)
    out[...] = times(factor, image[...] - lead * root[...])


def local(kernel, name, out_shape, *operands):
    vmem = pl.BlockSpec(memory_space=pltpu.VMEM)
    return pl.pallas_call(
        kernel,
        out_shape=out_shape,
        in_specs=[vmem] * len(operands),
        out_specs=jax.tree.map(lambda _: vmem, out_shape),
        compiler_params=pltpu.CompilerParams(vmem_limit_bytes=VMEM_LIMIT),
        name=name,
    )(*operands)


def swap_cores(value):
    return lax.ppermute(value, "core", [(0, 1), (1, 0)])


def share(value, axes):
    size = lax.axis_size(axes)
    return lax.all_to_all(
        jnp.broadcast_to(value[None], (size,) + value.shape), axes, 0, 0, tiled=True
    )


def share_row(value):
    mine = share(value, ("y", "zh"))
    return mine, swap_cores(mine)


def sum_all(message):
    rows = message.shape[0] // 2
    core = lax.axis_index("core")
    keep = lax.dynamic_slice_in_dim(message, core * rows, rows, 0)
    give = lax.dynamic_slice_in_dim(message, (1 - core) * rows, rows, 0)
    summed = jnp.sum(share(keep + swap_cores(give), CHIPS), axis=0)
    other = swap_cores(summed)
    first = core == 0
    return jnp.concatenate([jnp.where(first, summed, other), jnp.where(first, other, summed)], 0)


def up(value):
    return lax.ppermute(value, "y", [(i, (i + 1) % 4) for i in range(4)])


def down(value):
    return lax.ppermute(value, "y", [(i, (i + 3) % 4) for i in range(4)])


def apart(value):
    return lax.ppermute(
        value,
        ("y", "core"),
        [(2 * i + k, 2 * ((i + 1 + 2 * k) % 4) + k) for i in range(4) for k in range(2)],
    )


def apart_z(value):
    moves = []
    for z in range(4):
        for k in range(2):
            to = (z + 1 + 2 * k) % 4
            moves.append((z // 2 * 4 + k * 2 + z % 2, to // 2 * 4 + k * 2 + to % 2))
    return lax.ppermute(value, ("zh", "core", "zl"), moves)


def cross(value):
    return lax.ppermute(value, ("zh", "zl"), [(0, 3), (3, 0), (1, 2), (2, 1)])


def pair_list(count, block_index, core, rows, slabs, arrivals):
    slot = jnp.arange(PAIRS, dtype=jnp.int32)
    rank = jnp.sum(
        jnp.where(slabs[:, None] == arrivals[None, :], jnp.arange(BLOCK_TILES, dtype=jnp.int32), 0), 1
    )
    key = jnp.where(slot < count, rank * PAIRS + slot, BLOCK_TILES * PAIRS + slot)
    place = jnp.sum((key[None, :] < key[:, None]).astype(jnp.int32), axis=1)
    at = place[None, :] == slot[:, None]

    def ordered(value):
        return jnp.sum(jnp.where(at, value[None, :], 0), axis=1)

    ranks = ordered(rank)
    fresh = jnp.concatenate([jnp.zeros(1, bool), ranks[1:] != ranks[:-1]])
    groups = jnp.sum(jnp.where(slot[None, :] <= slot[:, None], fresh[None, :], False).astype(jnp.int32), 1)
    limit = jnp.arange(BLOCK_TILES + 1, dtype=jnp.int32) * PAIRS
    starts = jnp.sum((key[None, :] < limit[:, None]).astype(jnp.int32), axis=1)
    head = jnp.stack([count, block_index, core] + [jnp.int32(0)] * 5)
    return jnp.concatenate([head, ordered(rows), ordered(slabs), ranks, groups, starts]).astype(jnp.int32)


def shards(embeddings, labels, pair_rows, pair_cols, pair_count):
    y, zh, core = (lax.axis_index(a) for a in ROW)
    slab_index = lax.axis_index(ROW)
    block_index = lax.axis_index(COL)
    zero = core == 0
    slab = embeddings.reshape(SLAB_TILES, TILE, WIDTH)

    def of(dy, dz, k):
        return ((y + dy) % 4 * 2 + (zh + dz) % 2) * 2 + k

    side = lambda k: jnp.where(k == 0, 3, 1)
    arrivals = []
    for k in (core, 1 - core):
        arrivals.append(
            [
                of(0, 0, k),
                of(0, 1, k),
                of(3, 0, k),
                of(1, 0, k),
                of(2, 0, k),
                of(side(k), 1, k),
                of(2, 1, k),
                of(4 - side(k), 1, k),
            ]
        )
    first, second = arrivals
    arrivals = [q for both in zip(first[:6], second[:6], strict=True) for q in both]
    arrivals = jnp.stack(arrivals + first[6:] + second[6:])
    info = pair_list(pair_count[0, 0], block_index, core, pair_rows[0, 0], pair_cols[0, 0], arrivals)

    own = lax.dynamic_index_in_dim(slab, block_index, 0, keepdims=False)
    give = lax.dynamic_index_in_dim(slab, block_index ^ 1, 0, keepdims=False)
    across = cross(give)
    below = up(own)
    above = down(own)
    half_rows = 0.5 * jnp.sum(jnp.square(slab.astype(F32)), axis=2)

    def both(*pieces):
        return [each for piece in pieces for each in (piece, swap_cores(piece))]

    def after(made, *pieces):
        tied = lax.optimization_barrier((made[1],) + pieces)
        return (made[0], tied[0]), tied[1:]

    made = build(0, info, slab, half_rows, both(own), ())
    made, (across, below, above) = after(made, across, below, above)
    near = apart(across)
    beyond = apart(jnp.where(zero, below, above))
    other = apart_z(jnp.where(zero, above, below))
    made = build(2, info, slab, half_rows, both(across, below), made)
    made, (near, beyond, other) = after(made, near, beyond, other)
    far = apart(near)
    other = apart_z(other)
    made = build(6, info, slab, half_rows, both(above, beyond, near), made)
    made, last = after(made, far, other)
    made = build(12, info, slab, half_rows, last, made)
    made = build(14, info, slab, half_rows, [swap_cores(piece) for piece in last], made)
    tiles, partial_degree = made

    in_block = jnp.arange(SLAB_TILES)[:, None] == block_index
    sent = jnp.stack([partial_degree, jnp.where(in_block, labels.astype(F32)[None], 0.0)], axis=1)
    got = lax.all_to_all(
        jnp.broadcast_to(sent[None], (8,) + sent.shape).reshape(8 * SLAB_TILES, 2, TILE), CHIPS, 0, 0, tiled=True
    )
    mine = jnp.sum(got.reshape(8, SLAB_TILES, 2, TILE), axis=1)
    others = swap_cores(mine)
    known = jnp.where(zero, jnp.stack([mine, others], 1), jnp.stack([others, mine], 1)).reshape(BLOCK_TILES, 2, TILE)
    column_degree = known[:, 0]
    column_labels = known[:, 1].astype(jnp.int32)
    column_inv_root = lax.rsqrt(column_degree)
    degree = lax.dynamic_slice_in_dim(column_degree, slab_index, 1, 0)
    inv_root = lax.rsqrt(degree)
    root = jnp.sqrt(degree)

    scale = 1.0 / (BLOCK_TILES * SLAB_TILES * TILE)
    running = product(info, tiles, column_labels, column_inv_root)
    parts = lax.all_to_all(running, COL, 0, 0, tiled=True)
    weighed = local(
        weigh_kernel, "weigh", jax.ShapeDtypeStruct((K + 32, TILE), BF16), parts, inv_root, root
    )
    running = product(info, tiles, *share_row(weighed))
    parts = lax.all_to_all(running, COL, 0, 0, tiled=True)
    block = jax.ShapeDtypeStruct((K, TILE), F32)
    packed = jax.ShapeDtypeStruct((K // 2, 128), F32)
    image, message = local(
        functools.partial(middle_kernel, scale), "middle", (block, packed), parts, inv_root, root
    )
    return local(functools.partial(last_kernel, scale), "last", block, sum_all(message), image, root)


def solution(mesh):
    fine = Mesh(np.asarray(mesh.devices).reshape(4, 2, 2, 4, 2), ROW + COL)
    in_specs = (
        P(ROW, None),
        P(ROW + COL),
        P(ROW, COL, None),
        P(ROW, COL, None),
        P(ROW, COL),
    )
    return jax.shard_map(
        shards, mesh=fine, in_specs=in_specs, out_specs=P(None, ROW + COL), check_vma=False
    )
```

```python
import functools

import jax
import jax.numpy as jnp
import numpy as np
from jax import lax
from jax.experimental import pallas as pl
from jax.experimental.pallas import tpu as pltpu
from jax.sharding import Mesh
from jax.sharding import PartitionSpec as P

TILE = 512
K = 64
PAIRS = 24
WIDTH = 1024
KERNEL_SCALE = 0.5
RATE = 2.0 / KERNEL_SCALE * float(np.log2(np.e))
F32 = jnp.float32
BF16 = jnp.bfloat16

ROW = ("y", "zh", "core")
COL = ("x", "zl")
CHIPS = ("y", "zh", "x", "zl")
SLAB_TILES = 8
BLOCK_TILES = 16
VMEM_LIMIT = 10 * 1024 * 1024
ROWS, SLABS, RANKS, GROUPS, STARTS = (8 + PAIRS * i for i in range(5))


def build_kernel(first, arrived, info, slab, half_rows, *refs):
    columns, refs = refs[:arrived], refs[arrived:]
    if first:
        _, old_degree, *refs = refs
    tiles, degree, left, right, made, sem_left, sem_right, sem_out = refs
    block_index = info[1]
    ahead, stores = left.shape[0] - 1, made.shape[0]
    if first:
        degree[...] = old_degree[...]
    else:
        degree[...] = jnp.zeros_like(degree)

    begin, end = info[STARTS + first], info[STARTS + first + arrived]

    def left_copy(entry):
        slot = lax.rem(entry, ahead + 1)
        t = info[ROWS + entry]
        return pltpu.make_async_copy(slab.at[t], left.at[slot], sem_left.at[slot])

    def right_copy(entry, s):
        slot = lax.rem(info[GROUPS + entry], right.shape[0])
        return pltpu.make_async_copy(columns[s], right.at[slot], sem_right.at[slot])

    def fresh(entry):
        return jnp.logical_or(entry == begin, info[GROUPS + entry] != info[GROUPS + entry - 1])

    def fetch(entry):
        left_copy(entry).start()
        for s in range(arrived):

            @pl.when(jnp.logical_and(fresh(entry), info[RANKS + entry] == first + s))
            def _():
                right_copy(entry, s).start()

    def store(entry):
        slot = lax.rem(entry, stores)
        return pltpu.make_async_copy(made.at[slot], tiles.at[entry], sem_out.at[slot])

    for entry in range(ahead):

        @pl.when(begin + entry < end)
        def _():
            fetch(begin + entry)

    def step(entry, carry):
        @pl.when(entry + ahead < end)
        def _():
            fetch(entry + ahead)

        @pl.when(entry - begin >= stores)
        def _():
            store(entry - stores).wait()

        left_copy(entry).wait()

        @pl.when(fresh(entry))
        def _():
            right_copy(entry, 0).wait()

        a_slot = lax.rem(entry, ahead + 1)
        b_slot = lax.rem(info[GROUPS + entry], right.shape[0])
        m_slot = lax.rem(entry, stores)
        t = info[ROWS + entry]
        b = right[b_slot]
        wide = b.astype(F32)
        half_b = 0.5 * jnp.sum(wide * wide, axis=1, keepdims=True)
        sums = []
        for n in range(2):
            lanes = pl.ds(n * 256, 256)
            inner = lax.dot_general(
                b, left[a_slot, lanes, :], (((1,), (1,)), ((), ())), preferred_element_type=F32
            )
            half_a = half_rows[pl.ds(t, 1), lanes]
            w = jnp.exp2(RATE * ((inner - half_a) - half_b)).astype(BF16)
            made[m_slot, :, lanes] = w
            sums.append(jnp.sum(w.astype(F32), axis=0, keepdims=True))
        old = degree[pl.ds(t, 1), :]
        degree[pl.ds(t, 1), :] = old + jnp.concatenate(sums, axis=1)
        if first == 0:
            @pl.when(jnp.logical_and(t == block_index, info[RANKS + entry] == 0))
            def _():
                w = made[m_slot]
                same = lax.broadcasted_iota(jnp.int32, (TILE, TILE), 0) == lax.broadcasted_iota(
                    jnp.int32, (TILE, TILE), 1
                )
                w = jnp.where(same, jnp.zeros_like(w), w)
                made[m_slot] = w
                degree[pl.ds(t, 1), :] = old + jnp.sum(w.astype(F32), axis=0, keepdims=True)

        store(entry).start()
        return carry

    lax.fori_loop(begin, end, step, 0)
    for back in range(stores):

        @pl.when(end - begin > back)
        def _():
            store(end - 1 - back).wait()


def in_hbm(value):
    return pltpu.with_memory_space_constraint(value, pltpu.HBM)


def build(first, info, slab, half_rows, columns, made):
    any_space = pl.BlockSpec(memory_space=pl.ANY)
    hbm = pl.BlockSpec(memory_space=pltpu.HBM)
    vmem = pl.BlockSpec(memory_space=pltpu.VMEM)
    arrived = len(columns)
    pairs = PAIRS * arrived // BLOCK_TILES
    return pl.pallas_call(
        functools.partial(build_kernel, first, arrived),
        out_shape=(
            pltpu.HBM((PAIRS, TILE, TILE), BF16),
            jax.ShapeDtypeStruct((SLAB_TILES, TILE), F32),
        ),
        in_specs=[pl.BlockSpec(memory_space=pltpu.SMEM), hbm, vmem]
        + [any_space] * arrived
        + ([hbm, vmem] if made else []),
        out_specs=(hbm, vmem),
        scratch_shapes=[
            pltpu.VMEM((3, TILE, WIDTH), BF16),
            pltpu.VMEM((3, TILE, WIDTH), BF16),
            pltpu.VMEM((4, TILE, TILE), BF16),
            pltpu.SemaphoreType.DMA((3,)),
            pltpu.SemaphoreType.DMA((3,)),
            pltpu.SemaphoreType.DMA((4,)),
        ],
        input_output_aliases={3 + arrived: 0} if made else {},
        compiler_params=pltpu.CompilerParams(vmem_limit_bytes=20 * 1024 * 1024),
        cost_estimate=pl.CostEstimate(
            flops=pairs * 2 * TILE * TILE * WIDTH,
            bytes_accessed=pairs * 5 * TILE * WIDTH,
            transcendentals=pairs * TILE * TILE,
        ),
        name="build_tiles",
    )(info, in_hbm(slab), half_rows, *columns, *([in_hbm(made[0]), made[1]] if made else []))


def terms_of(value):
    high = value.astype(BF16).astype(F32)
    middle = (value - high).astype(BF16).astype(F32)
    low = (value - high) - middle
    return jnp.concatenate([high, middle, low, jnp.zeros_like(low)], axis=0).astype(BF16)


def sum_of(terms):
    total = jnp.sum(terms.astype(F32), axis=0)
    return total[:8] + (total[8:16] + total[16:24])


def product_kernel(first, info, tiles, *refs):
    if first:
        labels, inv_root, degree, shift, out, running, held, sem = refs
    else:
        mine, others, out, running, held, sem = refs
    count, core = info[0], info[2]
    depth = held.shape[0]
    running[...] = jnp.zeros_like(running)
    if not first:
        rest = jnp.zeros((8, TILE), F32)
        for known in (mine, others):
            rest = rest + sum_of(known[:, K:, :])
        for t in range(SLAB_TILES):
            out[t, K:, :] = terms_of(rest)

    def fetch(entry):
        slot = lax.rem(entry, depth)
        return pltpu.make_async_copy(tiles.at[entry], held.at[slot], sem.at[slot])

    def piece(entry):
        q = info[SLABS + entry]
        if first:
            value = inv_root[pl.ds(q, 1), :]
            label = labels[pl.ds(q, 1), :]
            value = jnp.where(label < K, value, -value)
            same = (label & (K - 1)) == lax.broadcasted_iota(jnp.int32, (K, TILE), 0)
            return jnp.where(same, jnp.broadcast_to(value, (K, TILE)), 0.0).astype(BF16)
        return jnp.where(q % 2 == core, mine[q // 2, :K, :], others[q // 2, :K, :])

    def term(entry):
        return jnp.dot(piece(entry), held[lax.rem(entry, depth)], preferred_element_type=F32)

    for entry in range(depth - 2):

        @pl.when(entry < count)
        def _():
            fetch(jnp.int32(entry)).start()

    def step(pair, carry):
        one = 2 * pair
        two = one + 1
        for entry in (one, two):

            @pl.when(entry + depth - 2 < count)
            def _():
                fetch(entry + depth - 2).start()

        fetch(one).wait()

        @pl.when(two < count)
        def _():
            fetch(two).wait()

        one_term, two_term = term(one), term(two)
        running[info[ROWS + one]] += one_term
        running[info[ROWS + two]] += jnp.where(two < count, two_term, 0.0)
        return carry

    lax.fori_loop(0, (count + 1) // 2, step, 0)
    for t in range(SLAB_TILES):
        total = running[t]
        if first:
            total = total - shift[...] * degree[t : t + 1, :]
        out[t, :K, :] = total.astype(BF16)


def product(info, tiles, *operands):
    vmem = pl.BlockSpec(memory_space=pltpu.VMEM)
    first = operands[0].dtype == jnp.int32
    return pl.pallas_call(
        functools.partial(product_kernel, first),
        out_shape=jax.ShapeDtypeStruct(
            (SLAB_TILES, K if first else K + 32, TILE), BF16
        ),
        in_specs=[
            pl.BlockSpec(memory_space=pltpu.SMEM),
            pl.BlockSpec(memory_space=pltpu.HBM),
        ]
        + [vmem] * len(operands),
        out_specs=vmem,
        scratch_shapes=[
            pltpu.VMEM((SLAB_TILES, K, TILE), F32),
            pltpu.VMEM((8, TILE, TILE), BF16),
            pltpu.SemaphoreType.DMA((8,)),
        ],
        compiler_params=pltpu.CompilerParams(vmem_limit_bytes=20 * 1024 * 1024),
        name="product",
    )(info, in_hbm(tiles), *operands)


def weights_of(image, root):
    heavy = jnp.concatenate([image, jnp.broadcast_to(root, (8, TILE))], axis=0)
    weights = lax.dot_general(
        heavy,
        heavy,
        (((1,), (1,)), ((), ())),
        precision=lax.Precision.HIGHEST,
        preferred_element_type=F32,
    )
    half = K // 2
    return jnp.concatenate(
        [
            weights[:half, :half],
            weights[half:K, :half],
            weights[half:K, half:K],
            weights[:half, K : K + 8],
            weights[half:K, K : K + 8],
            jnp.broadcast_to(weights[K : K + 1, K : K + 1], (half, 16)),
        ],
        axis=1,
    )


def factor_of(sums, scale):
    half = K // 2
    lower = sums[:, half : 2 * half]
    gram = jnp.concatenate(
        [
            jnp.concatenate([sums[:, :half], lower.T], axis=1),
            jnp.concatenate([lower, sums[:, 2 * half : 3 * half]], axis=1),
        ],
        axis=0,
    )
    top = jnp.concatenate([sums[:, 96:97], sums[:, 104:105]], axis=0)
    total = sums[:1, 112:113]
    rows = lax.broadcasted_iota(jnp.int32, (K, K), 0)
    columns = lax.broadcasted_iota(jnp.int32, (K, K), 1)
    across = jnp.sum(jnp.where(rows == columns, top, 0.0), axis=0, keepdims=True)
    gram = (gram - top * across / total) * scale
    work = jnp.concatenate([gram, (rows == columns).astype(F32)], axis=1)
    index = lax.broadcasted_iota(jnp.int32, (K, 2 * K), 0)
    pivots = jnp.ones((K, 2 * K), F32)
    for start in range(0, K, 8):
        index = index[-(K - start) :]
        spread = [
            jnp.broadcast_to(work[start:, j : j + 1], (K - start, 2 * K)) for j in range(start, start + 8)
        ]
        rest = work[start:]
        below = pivots[start:]
        for a in range(8):
            pivot = spread[a][a : a + 1, :]
            below = jnp.where(index == start + a, pivot, below)
            ratio = jnp.where(index > start + a, spread[a] / pivot, 0.0)
            rest = rest - ratio * rest[a : a + 1, :]
            for b in range(a + 1, 8):
                spread[b] = spread[b] - ratio * spread[b][a : a + 1, :]
        work = jnp.concatenate([work[:start], rest], axis=0) if start else rest
        pivots = jnp.concatenate([pivots[:start], below], axis=0) if start else below
    return work[:, K:] * lax.rsqrt(pivots[:, K:]), top / total


def times(factor, block):
    return jnp.dot(factor, block, precision=lax.Precision.HIGHEST, preferred_element_type=F32)


def weigh_kernel(parts, inv_root, root, out):
    image = jnp.sum(parts[...].astype(F32), axis=0) * inv_root[...]
    out[:K, :] = (image * inv_root[...]).astype(BF16)
    packed = weights_of(image, root[...])
    sums = jnp.concatenate([packed[8 * i : 8 * i + 8] for i in range(4)], axis=1)
    out[K:, :] = terms_of(sums)


def middle_kernel(scale, parts, inv_root, root, image, message):
    sums = sum_of(parts[:, K:, :])
    packed = jnp.concatenate([sums[:, 128 * i : 128 * i + 128] for i in range(4)], axis=0)
    factor, lead = factor_of(packed, scale)
    whole = jnp.sum(parts[:, :K, :].astype(F32), axis=0)
    block = times(factor, whole * inv_root[...] - lead * root[...])
    image[...] = block
    message[...] = weights_of(block, root[...])


def last_kernel(scale, message, image, root, out):
    factor, lead = factor_of(message[...], scale)
    out[...] = times(factor, image[...] - lead * root[...])


def local(kernel, name, out_shape, *operands):
    vmem = pl.BlockSpec(memory_space=pltpu.VMEM)
    return pl.pallas_call(
        kernel,
        out_shape=out_shape,
        in_specs=[vmem] * len(operands),
        out_specs=jax.tree.map(lambda _: vmem, out_shape),
        compiler_params=pltpu.CompilerParams(vmem_limit_bytes=VMEM_LIMIT),
        name=name,
    )(*operands)


def swap_cores(value):
    return lax.ppermute(value, "core", [(0, 1), (1, 0)])


def share(value, axes):
    size = lax.axis_size(axes)
    return lax.all_to_all(
        jnp.broadcast_to(value[None], (size,) + value.shape), axes, 0, 0, tiled=True
    )


def share_row(value):
    mine = share(value, ("y", "zh"))
    return mine, swap_cores(mine)


def sum_all(message):
    rows = message.shape[0] // 2
    core = lax.axis_index("core")
    keep = lax.dynamic_slice_in_dim(message, core * rows, rows, 0)
    give = lax.dynamic_slice_in_dim(message, (1 - core) * rows, rows, 0)
    summed = jnp.sum(share(keep + swap_cores(give), CHIPS), axis=0)
    other = swap_cores(summed)
    first = core == 0
    return jnp.concatenate([jnp.where(first, summed, other), jnp.where(first, other, summed)], 0)


def up(value):
    return lax.ppermute(value, "y", [(i, (i + 1) % 4) for i in range(4)])


def down(value):
    return lax.ppermute(value, "y", [(i, (i + 3) % 4) for i in range(4)])


def apart(value):
    return lax.ppermute(
        value,
        ("y", "core"),
        [(2 * i + k, 2 * ((i + 1 + 2 * k) % 4) + k) for i in range(4) for k in range(2)],
    )


def apart_z(value):
    moves = []
    for z in range(4):
        for k in range(2):
            to = (z + 1 + 2 * k) % 4
            moves.append((z // 2 * 4 + k * 2 + z % 2, to // 2 * 4 + k * 2 + to % 2))
    return lax.ppermute(value, ("zh", "core", "zl"), moves)


def cross(value):
    return lax.ppermute(value, ("zh", "zl"), [(0, 3), (3, 0), (1, 2), (2, 1)])


def pair_list(count, block_index, core, rows, slabs, arrivals):
    slot = jnp.arange(PAIRS, dtype=jnp.int32)
    rank = jnp.sum(
        jnp.where(slabs[:, None] == arrivals[None, :], jnp.arange(BLOCK_TILES, dtype=jnp.int32), 0), 1
    )
    key = jnp.where(slot < count, rank * PAIRS + slot, BLOCK_TILES * PAIRS + slot)
    place = jnp.sum((key[None, :] < key[:, None]).astype(jnp.int32), axis=1)
    at = place[None, :] == slot[:, None]

    def ordered(value):
        return jnp.sum(jnp.where(at, value[None, :], 0), axis=1)

    ranks = ordered(rank)
    fresh = jnp.concatenate([jnp.zeros(1, bool), ranks[1:] != ranks[:-1]])
    groups = jnp.sum(jnp.where(slot[None, :] <= slot[:, None], fresh[None, :], False).astype(jnp.int32), 1)
    limit = jnp.arange(BLOCK_TILES + 1, dtype=jnp.int32) * PAIRS
    starts = jnp.sum((key[None, :] < limit[:, None]).astype(jnp.int32), axis=1)
    head = jnp.stack([count, block_index, core] + [jnp.int32(0)] * 5)
    return jnp.concatenate([head, ordered(rows), ordered(slabs), ranks, groups, starts]).astype(jnp.int32)


def shards(embeddings, labels, pair_rows, pair_cols, pair_count):
    y, zh, core = (lax.axis_index(a) for a in ROW)
    slab_index = lax.axis_index(ROW)
    block_index = lax.axis_index(COL)
    zero = core == 0
    slab = embeddings.reshape(SLAB_TILES, TILE, WIDTH)

    def of(dy, dz, k):
        return ((y + dy) % 4 * 2 + (zh + dz) % 2) * 2 + k

    def side(k):
        return jnp.where(k == 0, 3, 1)

    def both_of(dy, dz):
        return [of(dy, dz, core), of(dy, dz, 1 - core)]

    near_q, other_q = (
        [of(side(k ^ way), 1, k) for k in (core, 1 - core)] for way in (0, 1)
    )
    beyond_q, far_q = both_of(2, 0), both_of(2, 1)
    arrivals = both_of(0, 0) + both_of(0, 1) + both_of(3, 0) + both_of(1, 0) + near_q
    arrivals += [beyond_q[0], other_q[0], beyond_q[1], other_q[1], far_q[0], far_q[1]]
    arrivals = jnp.stack(arrivals)
    info = pair_list(pair_count[0, 0], block_index, core, pair_rows[0, 0], pair_cols[0, 0], arrivals)

    own = lax.dynamic_index_in_dim(slab, block_index, 0, keepdims=False)
    later, own = lax.optimization_barrier((slab, own))
    below = up(own)
    above = down(own)
    give = lax.dynamic_index_in_dim(later, block_index ^ 1, 0, keepdims=False)
    across = cross(give)
    half_rows = 0.5 * jnp.sum(jnp.square(slab.astype(F32)), axis=2)

    def both(*pieces):
        return [each for piece in pieces for each in (piece, swap_cores(piece))]

    def after(made, *pieces):
        tied = lax.optimization_barrier((made[1],) + pieces)
        return (made[0], tied[0]), tied[1:]

    made = build(0, info, slab, half_rows, both(own), ())
    made, (across, below, above) = after(made, across, below, above)
    near = apart(across)
    other = apart_z(jnp.where(zero, above, below))
    made = build(2, info, slab, half_rows, both(across, below, above), made)
    made, (near, other, below, above) = after(made, near, other, below, above)
    beyond = apart(jnp.where(zero, below, above))
    other = apart_z(other)
    made = build(8, info, slab, half_rows, [near], made)
    made, (passed,) = after(made, near)
    far = apart(passed)
    made = build(9, info, slab, half_rows, [swap_cores(near), beyond, other], made)
    made, (far,) = after(made, far)
    made = build(12, info, slab, half_rows, [swap_cores(beyond), swap_cores(other), far], made)
    made = build(15, info, slab, half_rows, [swap_cores(far)], made)
    tiles, partial_degree = made

    in_block = jnp.arange(SLAB_TILES)[:, None] == block_index
    counted = jnp.where(labels % K == jnp.arange(K)[:, None], jnp.where(labels < K, 1.0, -1.0), 0.0)
    facts = jnp.concatenate(
        [jnp.sum(counted, axis=1), jnp.sum(partial_degree)[None], jnp.zeros(TILE - K - 1, F32)]
    )
    sent = jnp.stack(
        [
            partial_degree,
            jnp.where(in_block, labels.astype(F32)[None], 0.0),
            jnp.broadcast_to(facts[None], (SLAB_TILES, TILE)),
        ],
        axis=1,
    )
    got = lax.all_to_all(
        jnp.broadcast_to(sent[None], (8,) + sent.shape).reshape(8 * SLAB_TILES, 3, TILE), CHIPS, 0, 0, tiled=True
    )
    mine = jnp.sum(got.reshape(8, SLAB_TILES, 3, TILE), axis=1)
    others = swap_cores(mine)
    known = jnp.where(zero, jnp.stack([mine, others], 1), jnp.stack([others, mine], 1)).reshape(BLOCK_TILES, 3, TILE)
    column_degree = known[:, 0]
    column_labels = known[:, 1].astype(jnp.int32)
    facts = jnp.sum(mine[:, 2], axis=0) + jnp.sum(others[:, 2], axis=0)
    documents = BLOCK_TILES * SLAB_TILES * TILE
    shift = facts[:K, None] * lax.rsqrt(facts[K] * documents)
    column_inv_root = lax.rsqrt(column_degree)
    degree = lax.dynamic_slice_in_dim(column_degree, slab_index, 1, 0)
    inv_root = lax.rsqrt(degree)
    root = jnp.sqrt(degree)

    scale = 1.0 / documents
    running = product(info, tiles, column_labels, column_inv_root, partial_degree, shift)
    parts = lax.all_to_all(running, COL, 0, 0, tiled=True)
    weighed = local(
        weigh_kernel, "weigh", jax.ShapeDtypeStruct((K + 32, TILE), BF16), parts, inv_root, root
    )
    running = product(info, tiles, *share_row(weighed))
    parts = lax.all_to_all(running, COL, 0, 0, tiled=True)
    block = jax.ShapeDtypeStruct((K, TILE), F32)
    packed = jax.ShapeDtypeStruct((K // 2, 128), F32)
    image, message = local(
        functools.partial(middle_kernel, scale), "middle", (block, packed), parts, inv_root, root
    )
    return local(functools.partial(last_kernel, scale), "last", block, sum_all(message), image, root)


def solution(mesh):
    fine = Mesh(np.asarray(mesh.devices).reshape(4, 2, 2, 4, 2), ROW + COL)
    in_specs = (
        P(ROW, None),
        P(ROW + COL),
        P(ROW, COL, None),
        P(ROW, COL, None),
        P(ROW, COL),
    )
    return jax.shard_map(
        shards, mesh=fine, in_specs=in_specs, out_specs=P(None, ROW + COL), check_vma=False
    )
```

```python
import functools

import jax
import jax.numpy as jnp
import numpy as np
from jax import lax
from jax.experimental import pallas as pl
from jax.experimental.pallas import tpu as pltpu
from jax.sharding import Mesh
from jax.sharding import PartitionSpec as P

TILE = 512
K = 64
PAIRS = 24
WIDTH = 1024
KERNEL_SCALE = 0.5
RATE = 2.0 / KERNEL_SCALE * float(np.log2(np.e))
F32 = jnp.float32
BF16 = jnp.bfloat16

ROW = ("y", "zh", "core")
COL = ("x", "zl")
CHIPS = ("y", "zh", "x", "zl")
SLAB_TILES = 8
BLOCK_TILES = 16
VMEM_LIMIT = 10 * 1024 * 1024
ROWS, SLABS, RANKS, GROUPS, STARTS = (8 + PAIRS * i for i in range(5))


def build_kernel(first, arrived, info, slab, half_rows, *refs):
    columns, refs = refs[:arrived], refs[arrived:]
    if first:
        _, old_degree, *refs = refs
    tiles, degree, left, right, made, sem_left, sem_right, sem_out = refs
    block_index = info[1]
    ahead, stores = left.shape[0] - 1, made.shape[0]
    if first:
        degree[...] = old_degree[...]
    else:
        degree[...] = jnp.zeros_like(degree)

    begin, end = info[STARTS + first], info[STARTS + first + arrived]

    def left_copy(entry):
        slot = lax.rem(entry, ahead + 1)
        t = info[ROWS + entry]
        return pltpu.make_async_copy(slab.at[t], left.at[slot], sem_left.at[slot])

    def right_copy(entry, s):
        slot = lax.rem(info[GROUPS + entry], right.shape[0])
        return pltpu.make_async_copy(columns[s], right.at[slot], sem_right.at[slot])

    def fresh(entry):
        return jnp.logical_or(entry == begin, info[GROUPS + entry] != info[GROUPS + entry - 1])

    def fetch(entry):
        left_copy(entry).start()
        for s in range(arrived):

            @pl.when(jnp.logical_and(fresh(entry), info[RANKS + entry] == first + s))
            def _():
                right_copy(entry, s).start()

    def store(entry):
        slot = lax.rem(entry, stores)
        return pltpu.make_async_copy(made.at[slot], tiles.at[entry], sem_out.at[slot])

    for entry in range(ahead):

        @pl.when(begin + entry < end)
        def _():
            fetch(begin + entry)

    def step(entry, carry):
        @pl.when(entry + ahead < end)
        def _():
            fetch(entry + ahead)

        @pl.when(entry - begin >= stores)
        def _():
            store(entry - stores).wait()

        left_copy(entry).wait()

        @pl.when(fresh(entry))
        def _():
            right_copy(entry, 0).wait()

        a_slot = lax.rem(entry, ahead + 1)
        b_slot = lax.rem(info[GROUPS + entry], right.shape[0])
        m_slot = lax.rem(entry, stores)
        t = info[ROWS + entry]
        b = right[b_slot]
        wide = b.astype(F32)
        half_b = 0.5 * jnp.sum(wide * wide, axis=1, keepdims=True)
        sums = []
        for n in range(2):
            lanes = pl.ds(n * 256, 256)
            inner = lax.dot_general(
                b, left[a_slot, lanes, :], (((1,), (1,)), ((), ())), preferred_element_type=F32
            )
            half_a = half_rows[pl.ds(t, 1), lanes]
            w = jnp.exp2(RATE * ((inner - half_a) - half_b)).astype(BF16)
            made[m_slot, :, lanes] = w
            sums.append(jnp.sum(w.astype(F32), axis=0, keepdims=True))
        old = degree[pl.ds(t, 1), :]
        degree[pl.ds(t, 1), :] = old + jnp.concatenate(sums, axis=1)
        if first == 0:
            @pl.when(jnp.logical_and(t == block_index, info[RANKS + entry] == 0))
            def _():
                w = made[m_slot]
                same = lax.broadcasted_iota(jnp.int32, (TILE, TILE), 0) == lax.broadcasted_iota(
                    jnp.int32, (TILE, TILE), 1
                )
                w = jnp.where(same, jnp.zeros_like(w), w)
                made[m_slot] = w
                degree[pl.ds(t, 1), :] = old + jnp.sum(w.astype(F32), axis=0, keepdims=True)

        store(entry).start()
        return carry

    lax.fori_loop(begin, end, step, 0)
    for back in range(stores):

        @pl.when(end - begin > back)
        def _():
            store(end - 1 - back).wait()


def in_hbm(value):
    return pltpu.with_memory_space_constraint(value, pltpu.HBM)


def build(first, info, slab, half_rows, columns, made):
    any_space = pl.BlockSpec(memory_space=pl.ANY)
    hbm = pl.BlockSpec(memory_space=pltpu.HBM)
    vmem = pl.BlockSpec(memory_space=pltpu.VMEM)
    arrived = len(columns)
    pairs = PAIRS * arrived // BLOCK_TILES
    return pl.pallas_call(
        functools.partial(build_kernel, first, arrived),
        out_shape=(
            pltpu.HBM((PAIRS, TILE, TILE), BF16),
            jax.ShapeDtypeStruct((SLAB_TILES, TILE), F32),
        ),
        in_specs=[pl.BlockSpec(memory_space=pltpu.SMEM), hbm, vmem]
        + [any_space] * arrived
        + ([hbm, vmem] if made else []),
        out_specs=(hbm, vmem),
        scratch_shapes=[
            pltpu.VMEM((3, TILE, WIDTH), BF16),
            pltpu.VMEM((3, TILE, WIDTH), BF16),
            pltpu.VMEM((4, TILE, TILE), BF16),
            pltpu.SemaphoreType.DMA((3,)),
            pltpu.SemaphoreType.DMA((3,)),
            pltpu.SemaphoreType.DMA((4,)),
        ],
        input_output_aliases={3 + arrived: 0} if made else {},
        compiler_params=pltpu.CompilerParams(vmem_limit_bytes=20 * 1024 * 1024),
        cost_estimate=pl.CostEstimate(
            flops=pairs * 2 * TILE * TILE * WIDTH,
            bytes_accessed=pairs * 5 * TILE * WIDTH,
            transcendentals=pairs * TILE * TILE,
        ),
        name="build_tiles",
    )(info, in_hbm(slab), half_rows, *columns, *([in_hbm(made[0]), made[1]] if made else []))


def terms_of(value):
    high = value.astype(BF16).astype(F32)
    middle = (value - high).astype(BF16).astype(F32)
    low = (value - high) - middle
    wide = jnp.concatenate([high, middle, low, jnp.zeros((32, 16), F32)], axis=1)
    return jnp.concatenate([wide[:16], wide[16:]], axis=1).astype(BF16)


def value_of(terms):
    wide = jnp.concatenate([terms[:, :256], terms[:, 256:]], axis=0)
    return wide[:, :80] + (wide[:, 80:160] + wide[:, 160:240])


def lead_of(sums):
    total = sums[:1, 67:68]
    return jnp.concatenate([sums[:, 65:66], sums[:, 66:67]], axis=0) / total, total


def product_kernel(first, info, tiles, *refs):
    if first:
        labels, mine, others, out, running, held, sem = refs
    else:
        mine, others, degree, out, running, held, sem = refs
    count = info[0]
    core, zh, y = info[2], info[3], info[4]
    depth = held.shape[0]
    running[...] = jnp.zeros_like(running)

    def fetch(entry):
        slot = lax.rem(entry, depth)
        return pltpu.make_async_copy(tiles.at[entry], held.at[slot], sem.at[slot])

    def piece(entry):
        q = info[SLABS + entry]
        own = q % 2 == core
        if first:
            index = (q % 2 ^ core) * 8 + ((q // 4 + 4 - y) % 4) * 2 + (q // 2 % 2 ^ zh)
            label = labels[pl.ds(index, 1), :]
            chip = pl.ds(q // 2, 1)
            value = lax.rsqrt(jnp.where(own, mine[chip, :], others[chip, :]))
            value = jnp.where(label < K, value, -value)
            label = jnp.where(label < K, label, label - K)
            same = label == lax.broadcasted_iota(jnp.int32, (K, TILE), 0).astype(F32)
            return jnp.where(same, jnp.broadcast_to(value, (K, TILE)), 0.0).astype(BF16)
        return jnp.where(own, mine[q // 2, :K, :], others[q // 2, :K, :])

    def term(entry):
        return jnp.dot(piece(entry), held[lax.rem(entry, depth)], preferred_element_type=F32)

    for entry in range(depth - 2):

        @pl.when(entry < count)
        def _():
            fetch(jnp.int32(entry)).start()

    def step(pair, carry):
        one = 2 * pair
        two = one + 1
        for entry in (one, two):

            @pl.when(entry + depth - 2 < count)
            def _():
                fetch(entry + depth - 2).start()

        fetch(one).wait()

        @pl.when(two < count)
        def _():
            fetch(two).wait()

        one_term, two_term = term(one), term(two)
        running[info[ROWS + one]] += one_term
        running[info[ROWS + two]] += jnp.where(two < count, two_term, 0.0)
        return carry

    lax.fori_loop(0, (count + 1) // 2, step, 0)
    if first:
        out[...] = running[...].astype(BF16)
    else:
        sums = jnp.sum(mine[:, K:, :].astype(F32), axis=0) + jnp.sum(others[:, K:, :].astype(F32), axis=0)
        sums = value_of(sums)
        lead, _ = lead_of(sums)
        terms = terms_of(sums)
        for t in range(SLAB_TILES):
            out[t, :K, :] = (running[t] - lead * degree[t : t + 1, :]).astype(BF16)
            out[t, K:, :] = terms


def product(info, tiles, *operands):
    vmem = pl.BlockSpec(memory_space=pltpu.VMEM)
    first = operands[0].dtype == F32
    return pl.pallas_call(
        functools.partial(product_kernel, first),
        out_shape=jax.ShapeDtypeStruct(
            (SLAB_TILES, K if first else K + 16, TILE), BF16
        ),
        in_specs=[
            pl.BlockSpec(memory_space=pltpu.SMEM),
            pl.BlockSpec(memory_space=pltpu.HBM),
        ]
        + [vmem] * len(operands),
        out_specs=vmem,
        scratch_shapes=[
            pltpu.VMEM((SLAB_TILES, K, TILE), F32),
            pltpu.VMEM((8, TILE, TILE), BF16),
            pltpu.SemaphoreType.DMA((8,)),
        ],
        compiler_params=pltpu.CompilerParams(vmem_limit_bytes=20 * 1024 * 1024),
        name="product",
    )(info, in_hbm(tiles), *operands)


def weights_of(image, root):
    heavy = jnp.concatenate([image, jnp.broadcast_to(root, (8, TILE))], axis=0)
    weights = lax.dot_general(
        heavy,
        heavy,
        (((1,), (1,)), ((), ())),
        precision=lax.Precision.HIGHEST,
        preferred_element_type=F32,
    )
    half = K // 2
    rows = lax.broadcasted_iota(jnp.int32, (half, half), 0)
    columns = lax.broadcasted_iota(jnp.int32, (half, half), 1)
    corner = weights[half:K, half:K]
    return jnp.concatenate(
        [
            weights[half:K, :half],
            jnp.where(rows >= columns, weights[:half, :half], corner),
            jnp.sum(jnp.where(rows == columns, corner, 0.0), axis=1, keepdims=True),
            weights[:half, K : K + 1],
            weights[half:K, K : K + 1],
            jnp.broadcast_to(weights[K : K + 1, K : K + 1], (half, 1)),
            jnp.zeros((half, 12), F32),
        ],
        axis=1,
    )


def factor_of(sums, scale):
    half = K // 2
    rows = lax.broadcasted_iota(jnp.int32, (half, half), 0)
    columns = lax.broadcasted_iota(jnp.int32, (half, half), 1)
    lower, mixed = sums[:, :half], sums[:, half:K]
    strict = jnp.where(rows > columns, mixed, 0.0)
    upper = jnp.where(rows < columns, mixed, 0.0)
    diagonal = rows == columns
    left = strict + strict.T + jnp.where(diagonal, mixed, 0.0)
    right = upper + upper.T + jnp.where(diagonal, sums[:, K : K + 1], 0.0)
    gram = jnp.concatenate(
        [jnp.concatenate([left, lower.T], axis=1), jnp.concatenate([lower, right], axis=1)], axis=0
    )
    lead, total = lead_of(sums)
    rows = lax.broadcasted_iota(jnp.int32, (K, K), 0)
    columns = lax.broadcasted_iota(jnp.int32, (K, K), 1)
    across = jnp.sum(jnp.where(rows == columns, lead, 0.0), axis=0, keepdims=True)
    gram = (gram - lead * across * total) * scale
    work = jnp.concatenate([gram, (rows == columns).astype(F32)], axis=1)
    index = lax.broadcasted_iota(jnp.int32, (K, 2 * K), 0)
    pivots = jnp.ones((K, 2 * K), F32)
    for start in range(0, K, 8):
        index = index[-(K - start) :]
        spread = [
            jnp.broadcast_to(work[start:, j : j + 1], (K - start, 2 * K)) for j in range(start, start + 8)
        ]
        rest = work[start:]
        below = pivots[start:]
        for a in range(8):
            pivot = spread[a][a : a + 1, :]
            below = jnp.where(index == start + a, pivot, below)
            ratio = jnp.where(index > start + a, spread[a] / pivot, 0.0)
            rest = rest - ratio * rest[a : a + 1, :]
            for b in range(a + 1, 8):
                spread[b] = spread[b] - ratio * spread[b][a : a + 1, :]
        work = jnp.concatenate([work[:start], rest], axis=0) if start else rest
        pivots = jnp.concatenate([pivots[:start], below], axis=0) if start else below
    return work[:, K:] * lax.rsqrt(pivots[:, K:]), lead


def times(factor, block):
    return jnp.dot(factor, block, precision=lax.Precision.HIGHEST, preferred_element_type=F32)


def roots_of(info, degrees):
    degree = degrees[pl.ds(info[5], 1), :]
    return lax.rsqrt(degree), jnp.sqrt(degree)


def weigh_kernel(info, parts, degrees, out):
    inv_root, root = roots_of(info, degrees)
    image = jnp.sum(parts[...].astype(F32), axis=0) * inv_root
    out[:K, :] = (image * inv_root).astype(BF16)
    out[K:, :] = terms_of(weights_of(image, root))


def middle_kernel(scale, info, parts, degrees, by_column, image, message):
    inv_root, root = roots_of(info, degrees)
    own = by_column[info[5]]
    columns = [value_of(parts[c, K:, :].astype(F32)) for c in range(SLAB_TILES)]
    factor, lead = factor_of(sum(columns), scale)
    whole = jnp.sum(parts[:, :K, :].astype(F32), axis=0)
    for c in range(SLAB_TILES):
        whole = whole + (lead_of(columns[c])[0] - lead) * own[c : c + 1, :]
    block = times(factor, whole * inv_root)
    image[...] = block
    message[:, :80] = weights_of(block, root)
    message[:, 80:] = jnp.zeros((K // 2, 48), F32)


def last_kernel(scale, info, message, image, degrees, out):
    _, root = roots_of(info, degrees)
    factor, lead = factor_of(message[:, :80], scale)
    out[...] = times(factor, image[...] - lead * root)


def local(kernel, name, out_shape, info, *operands):
    vmem = pl.BlockSpec(memory_space=pltpu.VMEM)
    return pl.pallas_call(
        kernel,
        out_shape=out_shape,
        in_specs=[pl.BlockSpec(memory_space=pltpu.SMEM)] + [vmem] * len(operands),
        out_specs=jax.tree.map(lambda _: vmem, out_shape),
        compiler_params=pltpu.CompilerParams(vmem_limit_bytes=VMEM_LIMIT),
        name=name,
    )(info, *operands)


def swap_cores(value):
    return lax.ppermute(value, "core", [(0, 1), (1, 0)])


def share(value, axes):
    size = lax.axis_size(axes)
    return lax.all_to_all(
        jnp.broadcast_to(value[None], (size,) + value.shape), axes, 0, 0, tiled=True
    )


def share_row(value):
    mine = share(value, ("y", "zh"))
    return mine, swap_cores(mine)


def sum_all(message):
    rows = message.shape[0] // 2
    core = lax.axis_index("core")
    keep = lax.dynamic_slice_in_dim(message, core * rows, rows, 0)
    give = lax.dynamic_slice_in_dim(message, (1 - core) * rows, rows, 0)
    summed = jnp.sum(share(keep + swap_cores(give), CHIPS), axis=0)
    other = swap_cores(summed)
    first = core == 0
    return jnp.concatenate([jnp.where(first, summed, other), jnp.where(first, other, summed)], 0)


def up(value):
    return lax.ppermute(value, "y", [(i, (i + 1) % 4) for i in range(4)])


def down(value):
    return lax.ppermute(value, "y", [(i, (i + 3) % 4) for i in range(4)])


def apart(value):
    return lax.ppermute(
        value,
        ("y", "core"),
        [(2 * i + k, 2 * ((i + 1 + 2 * k) % 4) + k) for i in range(4) for k in range(2)],
    )


def apart_z(value):
    moves = []
    for z in range(4):
        for k in range(2):
            to = (z + 1 + 2 * k) % 4
            moves.append((z // 2 * 4 + k * 2 + z % 2, to // 2 * 4 + k * 2 + to % 2))
    return lax.ppermute(value, ("zh", "core", "zl"), moves)


def cross(value):
    return lax.ppermute(value, ("zh", "zl"), [(0, 3), (3, 0), (1, 2), (2, 1)])


def pair_list(head, rows, slabs, arrivals):
    count = head[0]
    slot = jnp.arange(PAIRS, dtype=jnp.int32)
    rank = jnp.sum(
        jnp.where(slabs[:, None] == arrivals[None, :], jnp.arange(BLOCK_TILES, dtype=jnp.int32), 0), 1
    )
    key = jnp.where(slot < count, rank * PAIRS + slot, BLOCK_TILES * PAIRS + slot)
    place = jnp.sum((key[None, :] < key[:, None]).astype(jnp.int32), axis=1)
    at = place[None, :] == slot[:, None]

    def ordered(value):
        return jnp.sum(jnp.where(at, value[None, :], 0), axis=1)

    ranks = ordered(rank)
    fresh = jnp.concatenate([jnp.zeros(1, bool), ranks[1:] != ranks[:-1]])
    groups = jnp.sum(jnp.where(slot[None, :] <= slot[:, None], fresh[None, :], False).astype(jnp.int32), 1)
    limit = jnp.arange(BLOCK_TILES + 1, dtype=jnp.int32) * PAIRS
    starts = jnp.sum((key[None, :] < limit[:, None]).astype(jnp.int32), axis=1)
    head = jnp.stack(head + [jnp.int32(0)] * (8 - len(head)))
    return jnp.concatenate([head, ordered(rows), ordered(slabs), ranks, groups, starts]).astype(jnp.int32)


def shards(embeddings, labels, pair_rows, pair_cols, pair_count):
    y, zh, core = (lax.axis_index(a) for a in ROW)
    slab_index = lax.axis_index(ROW)
    block_index = lax.axis_index(COL)
    zero = core == 0
    slab = embeddings.reshape(SLAB_TILES, TILE, WIDTH)

    def of(dy, dz, k):
        return ((y + dy) % 4 * 2 + (zh + dz) % 2) * 2 + k

    def side(k):
        return jnp.where(k == 0, 3, 1)

    def both_of(dy, dz):
        return [of(dy, dz, core), of(dy, dz, 1 - core)]

    near_q, other_q = (
        [of(side(k ^ way), 1, k) for k in (core, 1 - core)] for way in (0, 1)
    )
    beyond_q, far_q = both_of(2, 0), both_of(2, 1)
    arrivals = both_of(0, 0)
    arrivals += [near_by[k] for k in (0, 1) for near_by in (both_of(0, 1), both_of(3, 0), both_of(1, 0))]
    arrivals += near_q
    arrivals += [beyond_q[0], other_q[0], beyond_q[1], other_q[1], far_q[0], far_q[1]]
    arrivals = jnp.stack(arrivals)
    head = [pair_count[0, 0], block_index, core, zh, y, slab_index // 2]
    info = pair_list(head, pair_rows[0, 0], pair_cols[0, 0], arrivals)

    own = lax.dynamic_index_in_dim(slab, block_index, 0, keepdims=False)
    later, own = lax.optimization_barrier((slab, own))
    below = up(own)
    above = down(own)
    give = lax.dynamic_index_in_dim(later, block_index ^ 1, 0, keepdims=False)
    across = cross(give)
    half_rows = 0.5 * jnp.sum(jnp.square(slab.astype(F32)), axis=2)
    seeds = labels.astype(F32)[None]
    seeds = jnp.concatenate([seeds, lax.ppermute(seeds, "zh", [(0, 1), (1, 0)])], axis=0)

    def both(*pieces):
        return [each for piece in pieces for each in (piece, swap_cores(piece))]

    def after(made, *pieces):
        tied = lax.optimization_barrier((made[1],) + pieces)
        return (made[0], tied[0]), tied[1:]

    made = build(0, info, slab, half_rows, both(own), ())
    made, (across, below, above, seeds) = after(made, across, below, above, seeds)
    near = apart(across)
    other = apart_z(jnp.where(zero, above, below))
    seeds = [seeds, down(seeds), lax.ppermute(seeds, "y", [(i, (i + 2) % 4) for i in range(4)]), up(seeds)]
    made = build(2, info, slab, half_rows, [across, below, above], made)
    made, seeds = after(made, *seeds)
    seeds = jnp.concatenate(seeds, axis=0)
    seeds = jnp.concatenate([seeds, swap_cores(seeds)], axis=0)
    made = build(5, info, slab, half_rows, [swap_cores(piece) for piece in (across, below, above)], made)
    made, (near, other, below, above) = after(made, near, other, below, above)
    beyond = apart(jnp.where(zero, below, above))
    other = apart_z(other)
    made = build(8, info, slab, half_rows, [near], made)
    made, (passed,) = after(made, near)
    far = apart(passed)
    made = build(9, info, slab, half_rows, [swap_cores(near), beyond, other], made)
    made, (far, seeds) = after(made, far, seeds)
    made = build(12, info, slab, half_rows, [swap_cores(beyond), swap_cores(other), far], made)
    made = build(15, info, slab, half_rows, [swap_cores(far)], made)
    tiles, partial_degree = made

    by_column = lax.all_to_all(
        jnp.broadcast_to(partial_degree[None, :, None], (8, SLAB_TILES, 1, TILE)).reshape(8 * SLAB_TILES, 1, TILE),
        CHIPS,
        0,
        0,
        tiled=True,
    ).reshape(8, SLAB_TILES, TILE)
    degrees = jnp.sum(by_column, axis=1)

    scale = 1.0 / (BLOCK_TILES * SLAB_TILES * TILE)
    block = jax.ShapeDtypeStruct((K, TILE), F32)
    running = product(info, tiles, seeds, degrees, swap_cores(degrees))
    parts = lax.all_to_all(running, COL, 0, 0, tiled=True)
    weighed = local(
        weigh_kernel, "weigh", jax.ShapeDtypeStruct((K + 16, TILE), BF16), info, parts, degrees
    )
    running = product(info, tiles, *share_row(weighed), partial_degree)
    parts = lax.all_to_all(running, COL, 0, 0, tiled=True)
    image, message = local(
        functools.partial(middle_kernel, scale),
        "middle",
        (block, jax.ShapeDtypeStruct((K // 2, 128), F32)),
        info,
        parts,
        degrees,
        by_column,
    )
    return local(
        functools.partial(last_kernel, scale), "last", block, info, sum_all(message), image, degrees
    )


def solution(mesh):
    fine = Mesh(np.asarray(mesh.devices).reshape(4, 2, 2, 4, 2), ROW + COL)
    in_specs = (
        P(ROW, None),
        P(ROW + COL),
        P(ROW, COL, None),
        P(ROW, COL, None),
        P(ROW, COL),
    )
    return jax.shard_map(
        shards, mesh=fine, in_specs=in_specs, out_specs=P(None, ROW + COL), check_vma=False
    )
```

```python
import functools

import jax
import jax.numpy as jnp
import numpy as np
from jax import lax
from jax.experimental import pallas as pl
from jax.experimental.pallas import tpu as pltpu
from jax.sharding import Mesh
from jax.sharding import PartitionSpec as P

TILE = 512
K = 64
PAIRS = 24
WIDTH = 1024
KERNEL_SCALE = 0.5
RATE = 2.0 / KERNEL_SCALE * float(np.log2(np.e))
F32 = jnp.float32
BF16 = jnp.bfloat16

ROW = ("y", "zh", "core")
COL = ("x", "zl")
CHIPS = ("y", "zh", "x", "zl")
SLAB_TILES = 8
BLOCK_TILES = 16
VMEM_LIMIT = 10 * 1024 * 1024
ROWS, SLABS, RANKS, GROUPS, STARTS = (8 + PAIRS * i for i in range(5))


def build_kernel(first, arrived, info, slab, half_rows, *refs):
    columns, refs = refs[:arrived], refs[arrived:]
    if first:
        _, old_degree, *refs = refs
    tiles, degree, half_column, made, sem_out = refs
    block_index = info[1]
    stores = made.shape[0]
    if first:
        degree[...] = old_degree[...]
    else:
        degree[...] = jnp.zeros_like(degree)

    begin, end = info[STARTS + first], info[STARTS + first + arrived]

    def store(entry):
        slot = lax.rem(entry, stores)
        return pltpu.make_async_copy(made.at[slot], tiles.at[entry], sem_out.at[slot])

    def step(column, own, entry, carry):
        @pl.when(entry - begin >= stores)
        def _():
            store(entry - stores).wait()

        slot = lax.rem(entry, stores)
        t = info[ROWS + entry]
        sums = []
        for n in range(2):
            lanes = pl.ds(n * 256, 256)
            inner = lax.dot_general(
                column[...], slab[t, lanes, :], (((1,), (1,)), ((), ())), preferred_element_type=F32
            )
            half_row = half_rows[pl.ds(t, 1), lanes]
            w = jnp.exp2(RATE * ((inner - half_row) - half_column[...])).astype(BF16)
            made[slot, :, lanes] = w
            sums.append(jnp.sum(w.astype(F32), axis=0, keepdims=True))
        old = degree[pl.ds(t, 1), :]
        degree[pl.ds(t, 1), :] = old + jnp.concatenate(sums, axis=1)
        if own:
            @pl.when(t == block_index)
            def _():
                w = made[slot]
                same = lax.broadcasted_iota(jnp.int32, (TILE, TILE), 0) == lax.broadcasted_iota(
                    jnp.int32, (TILE, TILE), 1
                )
                w = jnp.where(same, jnp.zeros_like(w), w)
                made[slot] = w
                degree[pl.ds(t, 1), :] = old + jnp.sum(w.astype(F32), axis=0, keepdims=True)

        store(entry).start()
        return carry

    for s, column in enumerate(columns):
        low, high = info[STARTS + first + s], info[STARTS + first + s + 1]

        @pl.when(low < high)
        def _(column=column):
            wide = column[...].astype(F32)
            half_column[...] = jnp.broadcast_to(
                0.5 * jnp.sum(wide * wide, axis=1, keepdims=True), half_column.shape
            )

        lax.fori_loop(low, high, functools.partial(step, column, first + s == 0), 0)
    for back in range(stores):

        @pl.when(end - begin > back)
        def _():
            store(end - 1 - back).wait()


def in_hbm(value):
    return pltpu.with_memory_space_constraint(value, pltpu.HBM)


def in_vmem(value):
    return pltpu.with_memory_space_constraint(value, pltpu.VMEM)


def build(first, info, slab, half_rows, columns, made):
    hbm = pl.BlockSpec(memory_space=pltpu.HBM)
    vmem = pl.BlockSpec(memory_space=pltpu.VMEM)
    arrived = len(columns)
    pairs = max(1, PAIRS * arrived // BLOCK_TILES)
    return pl.pallas_call(
        functools.partial(build_kernel, first, arrived),
        out_shape=(
            pltpu.HBM((PAIRS, TILE, TILE), BF16),
            jax.ShapeDtypeStruct((SLAB_TILES, TILE), F32),
        ),
        in_specs=[pl.BlockSpec(memory_space=pltpu.SMEM), vmem, vmem]
        + [vmem] * arrived
        + ([hbm, vmem] if made else []),
        out_specs=(hbm, vmem),
        scratch_shapes=[
            pltpu.VMEM((TILE, 256), F32),
            pltpu.VMEM((4, TILE, TILE), BF16),
            pltpu.SemaphoreType.DMA((4,)),
        ],
        input_output_aliases={3 + arrived: 0} if made else {},
        compiler_params=pltpu.CompilerParams(vmem_limit_bytes=16 * 1024 * 1024),
        cost_estimate=pl.CostEstimate(
            flops=pairs * 2 * TILE * TILE * WIDTH,
            bytes_accessed=pairs * 5 * TILE * WIDTH,
            transcendentals=pairs * TILE * TILE,
        ),
        name="build_tiles",
    )(
        info,
        in_vmem(slab),
        half_rows,
        *(in_vmem(column) for column in columns),
        *([in_hbm(made[0]), made[1]] if made else []),
    )


def terms_of(value):
    high = value.astype(BF16).astype(F32)
    middle = (value - high).astype(BF16).astype(F32)
    low = (value - high) - middle
    wide = jnp.concatenate([high, middle, low, jnp.zeros((32, 16), F32)], axis=1)
    return jnp.concatenate([wide[:16], wide[16:]], axis=1).astype(BF16)


def value_of(terms):
    wide = jnp.concatenate([terms[:, :256], terms[:, 256:]], axis=0)
    return wide[:, :80] + (wide[:, 80:160] + wide[:, 160:240])


def lead_of(sums):
    total = sums[:1, 67:68]
    return jnp.concatenate([sums[:, 65:66], sums[:, 66:67]], axis=0) / total, total


def row_of(rows, start):
    return jnp.concatenate([rows[start + i : start + i + 1] for i in range(4)], axis=1)


def product_kernel(first, info, tiles, *refs):
    if first:
        mine, others, out, running, held, sem = refs
    else:
        mine, others, degree, out, running, held, sem = refs
    count = info[0]
    core = info[2]
    depth = held.shape[0]
    running[...] = jnp.zeros_like(running)

    def fetch(entry):
        slot = lax.rem(entry, depth)
        return pltpu.make_async_copy(tiles.at[entry], held.at[slot], sem.at[slot])

    def piece(entry):
        q = info[SLABS + entry]
        own = q % 2 == core
        if first:
            known = jnp.where(own, mine[q // 2], others[q // 2])
            value, label = lax.rsqrt(row_of(known, 0)), row_of(known, 4)
            value = jnp.where(label < K, value, -value)
            label = jnp.where(label < K, label, label - K)
            same = label == lax.broadcasted_iota(jnp.int32, (K, TILE), 0).astype(F32)
            return jnp.where(same, jnp.broadcast_to(value, (K, TILE)), 0.0).astype(BF16)
        return jnp.where(own, mine[q // 2, :K, :], others[q // 2, :K, :])

    def term(entry):
        return jnp.dot(piece(entry), held[lax.rem(entry, depth)], preferred_element_type=F32)

    for entry in range(depth - 2):

        @pl.when(entry < count)
        def _():
            fetch(jnp.int32(entry)).start()

    def step(pair, carry):
        one = 2 * pair
        two = one + 1
        for entry in (one, two):

            @pl.when(entry + depth - 2 < count)
            def _():
                fetch(entry + depth - 2).start()

        fetch(one).wait()

        @pl.when(two < count)
        def _():
            fetch(two).wait()

        one_term, two_term = term(one), term(two)
        running[info[ROWS + one]] += one_term
        running[info[ROWS + two]] += jnp.where(two < count, two_term, 0.0)
        return carry

    lax.fori_loop(0, (count + 1) // 2, step, 0)
    if first:
        out[...] = running[...].astype(BF16)
    else:
        sums = jnp.sum(mine[:, K:, :].astype(F32), axis=0) + jnp.sum(others[:, K:, :].astype(F32), axis=0)
        sums = value_of(sums)
        lead, _ = lead_of(sums)
        terms = terms_of(sums)
        for t in range(SLAB_TILES):
            out[t, :K, :] = (running[t] - lead * degree[t : t + 1, :]).astype(BF16)
            out[t, K:, :] = terms


def product(info, tiles, *operands):
    vmem = pl.BlockSpec(memory_space=pltpu.VMEM)
    first = len(operands) == 2
    return pl.pallas_call(
        functools.partial(product_kernel, first),
        out_shape=jax.ShapeDtypeStruct(
            (SLAB_TILES, K if first else K + 16, TILE), BF16
        ),
        in_specs=[
            pl.BlockSpec(memory_space=pltpu.SMEM),
            pl.BlockSpec(memory_space=pltpu.HBM),
        ]
        + [vmem] * len(operands),
        out_specs=vmem,
        scratch_shapes=[
            pltpu.VMEM((SLAB_TILES, K, TILE), F32),
            pltpu.VMEM((8, TILE, TILE), BF16),
            pltpu.SemaphoreType.DMA((8,)),
        ],
        compiler_params=pltpu.CompilerParams(vmem_limit_bytes=20 * 1024 * 1024),
        name="product",
    )(info, in_hbm(tiles), *operands)


def weights_of(image, root):
    heavy = jnp.concatenate([image, jnp.broadcast_to(root, (8, TILE))], axis=0)
    weights = lax.dot_general(
        heavy,
        heavy,
        (((1,), (1,)), ((), ())),
        precision=lax.Precision.HIGHEST,
        preferred_element_type=F32,
    )
    half = K // 2
    rows = lax.broadcasted_iota(jnp.int32, (half, half), 0)
    columns = lax.broadcasted_iota(jnp.int32, (half, half), 1)
    corner = weights[half:K, half:K]
    return jnp.concatenate(
        [
            weights[half:K, :half],
            jnp.where(rows >= columns, weights[:half, :half], corner),
            jnp.sum(jnp.where(rows == columns, corner, 0.0), axis=1, keepdims=True),
            weights[:half, K : K + 1],
            weights[half:K, K : K + 1],
            jnp.broadcast_to(weights[K : K + 1, K : K + 1], (half, 1)),
            jnp.zeros((half, 12), F32),
        ],
        axis=1,
    )


def factor_of(sums, scale):
    half = K // 2
    rows = lax.broadcasted_iota(jnp.int32, (half, half), 0)
    columns = lax.broadcasted_iota(jnp.int32, (half, half), 1)
    lower, mixed = sums[:, :half], sums[:, half:K]
    strict = jnp.where(rows > columns, mixed, 0.0)
    upper = jnp.where(rows < columns, mixed, 0.0)
    diagonal = rows == columns
    left = strict + strict.T + jnp.where(diagonal, mixed, 0.0)
    right = upper + upper.T + jnp.where(diagonal, sums[:, K : K + 1], 0.0)
    gram = jnp.concatenate(
        [jnp.concatenate([left, lower.T], axis=1), jnp.concatenate([lower, right], axis=1)], axis=0
    )
    lead, total = lead_of(sums)
    rows = lax.broadcasted_iota(jnp.int32, (K, K), 0)
    columns = lax.broadcasted_iota(jnp.int32, (K, K), 1)
    across = jnp.sum(jnp.where(rows == columns, lead, 0.0), axis=0, keepdims=True)
    gram = (gram - lead * across * total) * scale
    work = jnp.concatenate([gram, (rows == columns).astype(F32)], axis=1)
    index = lax.broadcasted_iota(jnp.int32, (K, 2 * K), 0)
    pivots = jnp.ones((K, 2 * K), F32)
    for start in range(0, K, 8):
        index = index[-(K - start) :]
        spread = [
            jnp.broadcast_to(work[start:, j : j + 1], (K - start, 2 * K)) for j in range(start, start + 8)
        ]
        rest = work[start:]
        below = pivots[start:]
        for a in range(8):
            pivot = spread[a][a : a + 1, :]
            below = jnp.where(index == start + a, pivot, below)
            ratio = jnp.where(index > start + a, spread[a] / pivot, 0.0)
            rest = rest - ratio * rest[a : a + 1, :]
            for b in range(a + 1, 8):
                spread[b] = spread[b] - ratio * spread[b][a : a + 1, :]
        work = jnp.concatenate([work[:start], rest], axis=0) if start else rest
        pivots = jnp.concatenate([pivots[:start], below], axis=0) if start else below
    return work[:, K:] * lax.rsqrt(pivots[:, K:]), lead


def times(factor, block):
    return jnp.dot(factor, block, precision=lax.Precision.HIGHEST, preferred_element_type=F32)


def roots_of(info, known):
    degree = row_of(known[info[3]], 0)
    return lax.rsqrt(degree), jnp.sqrt(degree)


def weigh_kernel(info, parts, known, out):
    inv_root, root = roots_of(info, known)
    image = jnp.sum(parts[...].astype(F32), axis=0) * inv_root
    out[:K, :] = (image * inv_root).astype(BF16)
    out[K:, :] = terms_of(weights_of(image, root))


def middle_kernel(scale, info, parts, known, by_column, image, message):
    inv_root, root = roots_of(info, known)
    own = by_column[info[3]]
    columns = [value_of(parts[c, K:, :].astype(F32)) for c in range(SLAB_TILES)]
    factor, lead = factor_of(sum(columns), scale)
    whole = jnp.sum(parts[:, :K, :].astype(F32), axis=0)
    for c in range(SLAB_TILES):
        whole = whole + (lead_of(columns[c])[0] - lead) * row_of(own[c], 0)
    block = times(factor, whole * inv_root)
    image[...] = block
    message[:, :80] = weights_of(block, root)
    message[:, 80:] = jnp.zeros((K // 2, 48), F32)


def last_kernel(scale, info, message, image, known, out):
    _, root = roots_of(info, known)
    factor, lead = factor_of(message[:, :80], scale)
    out[...] = times(factor, image[...] - lead * root)


def local(kernel, name, out_shape, info, *operands):
    vmem = pl.BlockSpec(memory_space=pltpu.VMEM)
    return pl.pallas_call(
        kernel,
        out_shape=out_shape,
        in_specs=[pl.BlockSpec(memory_space=pltpu.SMEM)] + [vmem] * len(operands),
        out_specs=jax.tree.map(lambda _: vmem, out_shape),
        compiler_params=pltpu.CompilerParams(vmem_limit_bytes=VMEM_LIMIT),
        name=name,
    )(info, *operands)


def swap_cores(value):
    return lax.ppermute(value, "core", [(0, 1), (1, 0)])


def share(value, axes):
    size = lax.axis_size(axes)
    return lax.all_to_all(
        jnp.broadcast_to(value[None], (size,) + value.shape), axes, 0, 0, tiled=True
    )


def share_row(value):
    mine = share(value, ("y", "zh"))
    return mine, swap_cores(mine)


def sum_all(message):
    rows = message.shape[0] // 2
    core = lax.axis_index("core")
    keep = lax.dynamic_slice_in_dim(message, core * rows, rows, 0)
    give = lax.dynamic_slice_in_dim(message, (1 - core) * rows, rows, 0)
    summed = jnp.sum(share(keep + swap_cores(give), CHIPS), axis=0)
    other = swap_cores(summed)
    first = core == 0
    return jnp.concatenate([jnp.where(first, summed, other), jnp.where(first, other, summed)], 0)


def up(value):
    return lax.ppermute(value, "y", [(i, (i + 1) % 4) for i in range(4)])


def down(value):
    return lax.ppermute(value, "y", [(i, (i + 3) % 4) for i in range(4)])


def apart(value):
    return lax.ppermute(
        value,
        ("y", "core"),
        [(2 * i + k, 2 * ((i + 1 + 2 * k) % 4) + k) for i in range(4) for k in range(2)],
    )


def apart_z(value):
    moves = []
    for z in range(4):
        for k in range(2):
            to = (z + 1 + 2 * k) % 4
            moves.append((z // 2 * 4 + k * 2 + z % 2, to // 2 * 4 + k * 2 + to % 2))
    return lax.ppermute(value, ("zh", "core", "zl"), moves)


def cross(value):
    return lax.ppermute(value, ("zh", "zl"), [(0, 3), (3, 0), (1, 2), (2, 1)])


def pair_list(head, rows, slabs, arrivals):
    count = head[0]
    slot = jnp.arange(PAIRS, dtype=jnp.int32)
    rank = jnp.sum(
        jnp.where(slabs[:, None] == arrivals[None, :], jnp.arange(BLOCK_TILES, dtype=jnp.int32), 0), 1
    )
    key = jnp.where(slot < count, rank * PAIRS + slot, BLOCK_TILES * PAIRS + slot)
    place = jnp.sum((key[None, :] < key[:, None]).astype(jnp.int32), axis=1)
    at = place[None, :] == slot[:, None]

    def ordered(value):
        return jnp.sum(jnp.where(at, value[None, :], 0), axis=1)

    ranks = ordered(rank)
    fresh = jnp.concatenate([jnp.zeros(1, bool), ranks[1:] != ranks[:-1]])
    groups = jnp.sum(jnp.where(slot[None, :] <= slot[:, None], fresh[None, :], False).astype(jnp.int32), 1)
    limit = jnp.arange(BLOCK_TILES + 1, dtype=jnp.int32) * PAIRS
    starts = jnp.sum((key[None, :] < limit[:, None]).astype(jnp.int32), axis=1)
    head = jnp.stack(head + [jnp.int32(0)] * (8 - len(head)))
    return jnp.concatenate([head, ordered(rows), ordered(slabs), ranks, groups, starts]).astype(jnp.int32)


def shards(embeddings, labels, pair_rows, pair_cols, pair_count):
    y, zh, core = (lax.axis_index(a) for a in ROW)
    slab_index = lax.axis_index(ROW)
    block_index = lax.axis_index(COL)
    zero = core == 0
    slab = embeddings.reshape(SLAB_TILES, TILE, WIDTH)

    def of(dy, dz, k):
        return ((y + dy) % 4 * 2 + (zh + dz) % 2) * 2 + k

    def side(k):
        return jnp.where(k == 0, 3, 1)

    def both_of(dy, dz):
        return [of(dy, dz, core), of(dy, dz, 1 - core)]

    near_q, other_q = (
        [of(side(k ^ way), 1, k) for k in (core, 1 - core)] for way in (0, 1)
    )
    beyond_q, far_q = both_of(2, 0), both_of(2, 1)
    arrivals = both_of(0, 0)
    arrivals += [near_by[k] for k in (0, 1) for near_by in (both_of(0, 1), both_of(3, 0), both_of(1, 0))]
    arrivals += near_q
    arrivals += [beyond_q[0], other_q[0], beyond_q[1], other_q[1], far_q[0], far_q[1]]
    arrivals = jnp.stack(arrivals)
    head = [pair_count[0, 0], block_index, core, slab_index // 2]
    info = pair_list(head, pair_rows[0, 0], pair_cols[0, 0], arrivals)

    own = lax.dynamic_index_in_dim(slab, block_index, 0, keepdims=False)
    later, own = lax.optimization_barrier((slab, own))
    below = up(own)
    above = down(own)
    give = lax.dynamic_index_in_dim(later, block_index ^ 1, 0, keepdims=False)
    across = cross(give)
    half_rows = 0.5 * jnp.sum(jnp.square(slab.astype(F32)), axis=2)
    def both(*pieces):
        return [each for piece in pieces for each in (piece, swap_cores(piece))]

    def after(made, *pieces):
        tied = lax.optimization_barrier((made[1],) + pieces)
        return (made[0], tied[0]), tied[1:]

    made = build(0, info, slab, half_rows, both(own), ())
    made, (across, below, above) = after(made, across, below, above)
    near = apart(across)
    other = apart_z(jnp.where(zero, above, below))
    made = build(2, info, slab, half_rows, [across, below, above], made)
    made = build(5, info, slab, half_rows, [swap_cores(piece) for piece in (across, below, above)], made)
    made, (near, other, below, above) = after(made, near, other, below, above)
    beyond = apart(jnp.where(zero, below, above))
    other = apart_z(other)
    made = build(8, info, slab, half_rows, [near], made)
    made, (passed,) = after(made, near)
    far = apart(passed)
    made = build(9, info, slab, half_rows, [swap_cores(near), beyond, other], made)
    made, (far,) = after(made, far)
    made = build(12, info, slab, half_rows, [swap_cores(beyond), swap_cores(other), far], made)
    made = build(15, info, slab, half_rows, [swap_cores(far)], made)
    tiles, partial_degree = made

    in_block = (jnp.arange(SLAB_TILES) == block_index)[:, None, None]
    seeds = jnp.where(in_block, labels.astype(F32).reshape(1, 4, 128), 0.0)
    sent = jnp.concatenate([partial_degree.reshape(SLAB_TILES, 4, 128), seeds], axis=1)
    by_column = lax.all_to_all(
        jnp.broadcast_to(sent[None], (8,) + sent.shape).reshape(8 * SLAB_TILES, 8, 128), CHIPS, 0, 0, tiled=True
    ).reshape(8, SLAB_TILES, 8, 128)
    known = jnp.sum(by_column, axis=1)

    scale = 1.0 / (BLOCK_TILES * SLAB_TILES * TILE)
    block = jax.ShapeDtypeStruct((K, TILE), F32)
    running = product(info, tiles, known, swap_cores(known))
    parts = lax.all_to_all(running, COL, 0, 0, tiled=True)
    weighed = local(
        weigh_kernel, "weigh", jax.ShapeDtypeStruct((K + 16, TILE), BF16), info, parts, known
    )
    running = product(info, tiles, *share_row(weighed), partial_degree)
    parts = lax.all_to_all(running, COL, 0, 0, tiled=True)
    image, message = local(
        functools.partial(middle_kernel, scale),
        "middle",
        (block, jax.ShapeDtypeStruct((K // 2, 128), F32)),
        info,
        parts,
        known,
        by_column,
    )
    return local(
        functools.partial(last_kernel, scale), "last", block, info, sum_all(message), image, known
    )


def solution(mesh):
    fine = Mesh(np.asarray(mesh.devices).reshape(4, 2, 2, 4, 2), ROW + COL)
    in_specs = (
        P(ROW, None),
        P(ROW + COL),
        P(ROW, COL, None),
        P(ROW, COL, None),
        P(ROW, COL),
    )
    return jax.shard_map(
        shards, mesh=fine, in_specs=in_specs, out_specs=P(None, ROW + COL), check_vma=False
    )
```

```python
import functools

import jax
import jax.numpy as jnp
import numpy as np
from jax import lax
from jax.experimental import pallas as pl
from jax.experimental.pallas import tpu as pltpu
from jax.sharding import Mesh
from jax.sharding import PartitionSpec as P

TILE = 512
K = 64
PAIRS = 24
WIDTH = 1024
KERNEL_SCALE = 0.5
RATE = 2.0 / KERNEL_SCALE * float(np.log2(np.e))
F32 = jnp.float32
BF16 = jnp.bfloat16

ROW = ("y", "zh", "core")
COL = ("x", "zl")
CHIPS = ("y", "zh", "x", "zl")
SLAB_TILES = 8
BLOCK_TILES = 16
VMEM_LIMIT = 10 * 1024 * 1024
ROWS, SLABS, RANKS, GROUPS, STARTS = (8 + PAIRS * i for i in range(5))


def build_kernel(first, arrived, info, slab, half_rows, *refs):
    columns, refs = refs[:arrived], refs[arrived:]
    if first:
        _, old_degree, *refs = refs
    tiles, degree, half_column, made, sem_out = refs
    block_index = info[1]
    stores = made.shape[0]
    if first:
        degree[...] = old_degree[...]
    else:
        degree[...] = jnp.zeros_like(degree)

    begin, end = info[STARTS + first], info[STARTS + first + arrived]

    def store(entry):
        slot = lax.rem(entry, stores)
        return pltpu.make_async_copy(made.at[slot], tiles.at[entry], sem_out.at[slot])

    def step(column, own, entry, carry):
        @pl.when(entry - begin >= stores)
        def _():
            store(entry - stores).wait()

        slot = lax.rem(entry, stores)
        t = info[ROWS + entry]
        sums = []
        for n in range(2):
            lanes = pl.ds(n * 256, 256)
            inner = lax.dot_general(
                column[...], slab[t, lanes, :], (((1,), (1,)), ((), ())), preferred_element_type=F32
            )
            half_row = half_rows[pl.ds(t, 1), lanes]
            w = jnp.exp2(RATE * ((inner - half_row) - half_column[...])).astype(BF16)
            made[slot, :, lanes] = w
            sums.append(jnp.sum(w.astype(F32), axis=0, keepdims=True))
        old = degree[pl.ds(t, 1), :]
        degree[pl.ds(t, 1), :] = old + jnp.concatenate(sums, axis=1)
        if own:
            @pl.when(t == block_index)
            def _():
                w = made[slot]
                same = lax.broadcasted_iota(jnp.int32, (TILE, TILE), 0) == lax.broadcasted_iota(
                    jnp.int32, (TILE, TILE), 1
                )
                w = jnp.where(same, jnp.zeros_like(w), w)
                made[slot] = w
                degree[pl.ds(t, 1), :] = old + jnp.sum(w.astype(F32), axis=0, keepdims=True)

        store(entry).start()
        return carry

    for s, column in enumerate(columns):
        low, high = info[STARTS + first + s], info[STARTS + first + s + 1]

        @pl.when(low < high)
        def _(column=column):
            wide = column[...].astype(F32)
            half_column[...] = jnp.broadcast_to(
                0.5 * jnp.sum(wide * wide, axis=1, keepdims=True), half_column.shape
            )

        lax.fori_loop(low, high, functools.partial(step, column, first + s == 0), 0)
    for back in range(stores):

        @pl.when(end - begin > back)
        def _():
            store(end - 1 - back).wait()


def in_hbm(value):
    return pltpu.with_memory_space_constraint(value, pltpu.HBM)


def in_vmem(value):
    return pltpu.with_memory_space_constraint(value, pltpu.VMEM)


def build(first, info, slab, half_rows, columns, made):
    hbm = pl.BlockSpec(memory_space=pltpu.HBM)
    vmem = pl.BlockSpec(memory_space=pltpu.VMEM)
    arrived = len(columns)
    pairs = max(1, PAIRS * arrived // BLOCK_TILES)
    return pl.pallas_call(
        functools.partial(build_kernel, first, arrived),
        out_shape=(
            pltpu.HBM((PAIRS, TILE, TILE), BF16),
            jax.ShapeDtypeStruct((SLAB_TILES, TILE), F32),
        ),
        in_specs=[pl.BlockSpec(memory_space=pltpu.SMEM), vmem, vmem]
        + [vmem] * arrived
        + ([hbm, vmem] if made else []),
        out_specs=(hbm, vmem),
        scratch_shapes=[
            pltpu.VMEM((TILE, 256), F32),
            pltpu.VMEM((4, TILE, TILE), BF16),
            pltpu.SemaphoreType.DMA((4,)),
        ],
        input_output_aliases={3 + arrived: 0} if made else {},
        compiler_params=pltpu.CompilerParams(vmem_limit_bytes=16 * 1024 * 1024),
        cost_estimate=pl.CostEstimate(
            flops=pairs * 2 * TILE * TILE * WIDTH,
            bytes_accessed=pairs * 5 * TILE * WIDTH,
            transcendentals=pairs * TILE * TILE,
        ),
        name="build_tiles",
    )(
        info,
        in_vmem(slab),
        half_rows,
        *(in_vmem(column) for column in columns),
        *([in_hbm(made[0]), made[1]] if made else []),
    )


def terms_of(value):
    high = value.astype(BF16).astype(F32)
    middle = (value - high).astype(BF16).astype(F32)
    low = (value - high) - middle
    wide = jnp.concatenate([high, middle, low, jnp.zeros((32, 16), F32)], axis=1)
    return jnp.concatenate([wide[:16], wide[16:]], axis=1).astype(BF16)


def value_of(terms):
    wide = jnp.concatenate([terms[:, :256], terms[:, 256:]], axis=0)
    return wide[:, :80] + (wide[:, 80:160] + wide[:, 160:240])


def lead_of(sums):
    total = sums[:1, 67:68]
    return jnp.concatenate([sums[:, 65:66], sums[:, 66:67]], axis=0) / total, total


def row_of(rows, start):
    return jnp.concatenate([rows[start + i : start + i + 1] for i in range(4)], axis=1)


def product_kernel(first, info, tiles, *refs):
    if first:
        mine, others, out, running, held, sem = refs
    else:
        mine, others, degree, out, running, held, sem = refs
    count = info[0]
    core = info[2]
    depth = held.shape[0]
    running[...] = jnp.zeros_like(running)

    def fetch(entry):
        slot = lax.rem(entry, depth)
        return pltpu.make_async_copy(tiles.at[entry], held.at[slot], sem.at[slot])

    def piece(entry):
        q = info[SLABS + entry]
        own = q % 2 == core
        if first:
            known = jnp.where(own, mine[q // 2], others[q // 2])
            value, label = lax.rsqrt(row_of(known, 0)), row_of(known, 4)
            value = jnp.where(label < K, value, -value)
            label = jnp.where(label < K, label, label - K)
            same = label == lax.broadcasted_iota(jnp.int32, (K, TILE), 0).astype(F32)
            return jnp.where(same, jnp.broadcast_to(value, (K, TILE)), 0.0).astype(BF16)
        return jnp.where(own, mine[q // 2, :K, :], others[q // 2, :K, :])

    def term(entry):
        return jnp.dot(piece(entry), held[lax.rem(entry, depth)], preferred_element_type=F32)

    for entry in range(depth - 2):

        @pl.when(entry < count)
        def _():
            fetch(jnp.int32(entry)).start()

    def step(pair, carry):
        one = 2 * pair
        two = one + 1
        for entry in (one, two):

            @pl.when(entry + depth - 2 < count)
            def _():
                fetch(entry + depth - 2).start()

        fetch(one).wait()

        @pl.when(two < count)
        def _():
            fetch(two).wait()

        one_term, two_term = term(one), term(two)
        running[info[ROWS + one]] += one_term
        running[info[ROWS + two]] += jnp.where(two < count, two_term, 0.0)
        return carry

    lax.fori_loop(0, (count + 1) // 2, step, 0)
    if first:
        out[...] = running[...].astype(BF16)
    else:
        sums = jnp.sum(mine[:, K:, :].astype(F32), axis=0) + jnp.sum(others[:, K:, :].astype(F32), axis=0)
        sums = value_of(sums)
        lead, _ = lead_of(sums)
        terms = terms_of(sums)
        for t in range(SLAB_TILES):
            out[t, :K, :] = (running[t] - lead * degree[t : t + 1, :]).astype(BF16)
            out[t, K:, :] = terms


def product(info, tiles, *operands):
    vmem = pl.BlockSpec(memory_space=pltpu.VMEM)
    first = len(operands) == 2
    return pl.pallas_call(
        functools.partial(product_kernel, first),
        out_shape=jax.ShapeDtypeStruct(
            (SLAB_TILES, K if first else K + 16, TILE), BF16
        ),
        in_specs=[
            pl.BlockSpec(memory_space=pltpu.SMEM),
            pl.BlockSpec(memory_space=pltpu.HBM),
        ]
        + [vmem] * len(operands),
        out_specs=vmem,
        scratch_shapes=[
            pltpu.VMEM((SLAB_TILES, K, TILE), F32),
            pltpu.VMEM((8, TILE, TILE), BF16),
            pltpu.SemaphoreType.DMA((8,)),
        ],
        compiler_params=pltpu.CompilerParams(vmem_limit_bytes=20 * 1024 * 1024),
        name="product",
    )(info, in_hbm(tiles), *operands)


def weights_of(image, root):
    heavy = jnp.concatenate([image, jnp.broadcast_to(root, (8, TILE))], axis=0)
    weights = lax.dot_general(
        heavy,
        heavy,
        (((1,), (1,)), ((), ())),
        precision=lax.Precision.HIGHEST,
        preferred_element_type=F32,
    )
    half = K // 2
    rows = lax.broadcasted_iota(jnp.int32, (half, half), 0)
    columns = lax.broadcasted_iota(jnp.int32, (half, half), 1)
    corner = weights[half:K, half:K]
    return jnp.concatenate(
        [
            weights[half:K, :half],
            jnp.where(rows >= columns, weights[:half, :half], corner),
            jnp.sum(jnp.where(rows == columns, corner, 0.0), axis=1, keepdims=True),
            weights[:half, K : K + 1],
            weights[half:K, K : K + 1],
            jnp.broadcast_to(weights[K : K + 1, K : K + 1], (half, 1)),
            jnp.zeros((half, 12), F32),
        ],
        axis=1,
    )


def factor_of(sums, scale):
    half = K // 2
    rows = lax.broadcasted_iota(jnp.int32, (half, half), 0)
    columns = lax.broadcasted_iota(jnp.int32, (half, half), 1)
    lower, mixed = sums[:, :half], sums[:, half:K]
    strict = jnp.where(rows > columns, mixed, 0.0)
    upper = jnp.where(rows < columns, mixed, 0.0)
    diagonal = rows == columns
    left = strict + strict.T + jnp.where(diagonal, mixed, 0.0)
    right = upper + upper.T + jnp.where(diagonal, sums[:, K : K + 1], 0.0)
    gram = jnp.concatenate(
        [jnp.concatenate([left, lower.T], axis=1), jnp.concatenate([lower, right], axis=1)], axis=0
    )
    lead, total = lead_of(sums)
    rows = lax.broadcasted_iota(jnp.int32, (K, K), 0)
    columns = lax.broadcasted_iota(jnp.int32, (K, K), 1)
    across = jnp.sum(jnp.where(rows == columns, lead, 0.0), axis=0, keepdims=True)
    gram = (gram - lead * across * total) * scale
    work = jnp.concatenate([gram, (rows == columns).astype(F32)], axis=1)
    index = lax.broadcasted_iota(jnp.int32, (K, 2 * K), 0)
    pivots = jnp.ones((K, 2 * K), F32)
    for start in range(0, K, 8):
        index = index[-(K - start) :]
        spread = [
            jnp.broadcast_to(work[start:, j : j + 1], (K - start, 2 * K)) for j in range(start, start + 8)
        ]
        rest = work[start:]
        below = pivots[start:]
        for a in range(8):
            pivot = spread[a][a : a + 1, :]
            below = jnp.where(index == start + a, pivot, below)
            ratio = jnp.where(index > start + a, spread[a] / pivot, 0.0)
            rest = rest - ratio * rest[a : a + 1, :]
            for b in range(a + 1, 8):
                spread[b] = spread[b] - ratio * spread[b][a : a + 1, :]
        work = jnp.concatenate([work[:start], rest], axis=0) if start else rest
        pivots = jnp.concatenate([pivots[:start], below], axis=0) if start else below
    return work[:, K:] * lax.rsqrt(pivots[:, K:]), lead


def times(factor, block):
    return jnp.dot(factor, block, precision=lax.Precision.HIGHEST, preferred_element_type=F32)


def roots_of(info, known):
    degree = row_of(known[info[3]], 0)
    return lax.rsqrt(degree), jnp.sqrt(degree)


def weigh_kernel(info, parts, known, out):
    inv_root, root = roots_of(info, known)
    image = jnp.sum(parts[...].astype(F32), axis=0) * inv_root
    out[:K, :] = (image * inv_root).astype(BF16)
    out[K:, :] = terms_of(weights_of(image, root))


def middle_kernel(scale, info, parts, known, by_column, image, message):
    inv_root, root = roots_of(info, known)
    own = by_column[info[3]]
    columns = [value_of(parts[c, K:, :].astype(F32)) for c in range(SLAB_TILES)]
    factor, lead = factor_of(sum(columns), scale)
    whole = jnp.sum(parts[:, :K, :].astype(F32), axis=0)
    for c in range(SLAB_TILES):
        whole = whole + (lead_of(columns[c])[0] - lead) * row_of(own[c], 0)
    block = times(factor, whole * inv_root)
    image[...] = block
    message[:, :80] = weights_of(block, root)
    message[:, 80:] = jnp.zeros((K // 2, 48), F32)


def last_kernel(scale, info, message, image, known, out):
    _, root = roots_of(info, known)
    factor, lead = factor_of(message[:, :80], scale)
    out[...] = times(factor, image[...] - lead * root)


def local(kernel, name, out_shape, info, *operands):
    vmem = pl.BlockSpec(memory_space=pltpu.VMEM)
    return pl.pallas_call(
        kernel,
        out_shape=out_shape,
        in_specs=[pl.BlockSpec(memory_space=pltpu.SMEM)] + [vmem] * len(operands),
        out_specs=jax.tree.map(lambda _: vmem, out_shape),
        compiler_params=pltpu.CompilerParams(vmem_limit_bytes=VMEM_LIMIT),
        name=name,
    )(info, *operands)


def swap_cores(value):
    return lax.ppermute(value, "core", [(0, 1), (1, 0)])


def share(value, axes):
    size = lax.axis_size(axes)
    return lax.all_to_all(
        jnp.broadcast_to(value[None], (size,) + value.shape), axes, 0, 0, tiled=True
    )


def share_row(value):
    mine = share(value, ("y", "zh"))
    return mine, swap_cores(mine)


def sum_all(message):
    rows = message.shape[0] // 2
    core = lax.axis_index("core")
    keep = lax.dynamic_slice_in_dim(message, core * rows, rows, 0)
    give = lax.dynamic_slice_in_dim(message, (1 - core) * rows, rows, 0)
    summed = jnp.sum(share(keep + swap_cores(give), CHIPS), axis=0)
    other = swap_cores(summed)
    first = core == 0
    return jnp.concatenate([jnp.where(first, summed, other), jnp.where(first, other, summed)], 0)


def up(value):
    return lax.ppermute(value, "y", [(i, (i + 1) % 4) for i in range(4)])


def down(value):
    return lax.ppermute(value, "y", [(i, (i + 3) % 4) for i in range(4)])


def apart(value):
    return lax.ppermute(
        value,
        ("y", "core"),
        [(2 * i + k, 2 * ((i + 1 + 2 * k) % 4) + k) for i in range(4) for k in range(2)],
    )


def apart_z(value):
    moves = []
    for z in range(4):
        for k in range(2):
            to = (z + 1 + 2 * k) % 4
            moves.append((z // 2 * 4 + k * 2 + z % 2, to // 2 * 4 + k * 2 + to % 2))
    return lax.ppermute(value, ("zh", "core", "zl"), moves)


def cross(value):
    return lax.ppermute(value, ("zh", "zl"), [(0, 3), (3, 0), (1, 2), (2, 1)])


def pair_list(head, rows, slabs, arrivals):
    count = head[0]
    slot = jnp.arange(PAIRS, dtype=jnp.int32)
    rank = jnp.sum(
        jnp.where(slabs[:, None] == arrivals[None, :], jnp.arange(BLOCK_TILES, dtype=jnp.int32), 0), 1
    )
    key = jnp.where(slot < count, rank * PAIRS + slot, BLOCK_TILES * PAIRS + slot)
    place = jnp.sum((key[None, :] < key[:, None]).astype(jnp.int32), axis=1)
    at = place[None, :] == slot[:, None]

    def ordered(value):
        return jnp.sum(jnp.where(at, value[None, :], 0), axis=1)

    ranks = ordered(rank)
    fresh = jnp.concatenate([jnp.zeros(1, bool), ranks[1:] != ranks[:-1]])
    groups = jnp.sum(jnp.where(slot[None, :] <= slot[:, None], fresh[None, :], False).astype(jnp.int32), 1)
    limit = jnp.arange(BLOCK_TILES + 1, dtype=jnp.int32) * PAIRS
    starts = jnp.sum((key[None, :] < limit[:, None]).astype(jnp.int32), axis=1)
    head = jnp.stack(head + [jnp.int32(0)] * (8 - len(head)))
    return jnp.concatenate([head, ordered(rows), ordered(slabs), ranks, groups, starts]).astype(jnp.int32)


def shards(embeddings, labels, pair_rows, pair_cols, pair_count):
    y, zh, core = (lax.axis_index(a) for a in ROW)
    slab_index = lax.axis_index(ROW)
    block_index = lax.axis_index(COL)
    zero = core == 0
    slab = embeddings.reshape(SLAB_TILES, TILE, WIDTH)

    def of(dy, dz, k):
        return ((y + dy) % 4 * 2 + (zh + dz) % 2) * 2 + k

    def side(k):
        return jnp.where(k == 0, 3, 1)

    def both_of(dy, dz):
        return [of(dy, dz, core), of(dy, dz, 1 - core)]

    near_q, other_q = (
        [of(side(k ^ way), 1, k) for k in (core, 1 - core)] for way in (0, 1)
    )
    beyond_q, far_q = both_of(2, 0), both_of(2, 1)
    arrivals = both_of(0, 0)
    arrivals += [near_by[k] for k in (0, 1) for near_by in (both_of(0, 1), both_of(3, 0), both_of(1, 0))]
    arrivals += near_q
    arrivals += [beyond_q[0], other_q[0], beyond_q[1], other_q[1], far_q[0], far_q[1]]
    arrivals = jnp.stack(arrivals)
    head = [pair_count[0, 0], block_index, core, slab_index // 2]
    info = pair_list(head, pair_rows[0, 0], pair_cols[0, 0], arrivals)

    own = lax.dynamic_index_in_dim(slab, block_index, 0, keepdims=False)
    later, own = lax.optimization_barrier((slab, own))
    below = up(own)
    above = down(own)
    give = lax.dynamic_index_in_dim(later, block_index ^ 1, 0, keepdims=False)
    across = cross(give)
    half_rows = 0.5 * jnp.sum(jnp.square(slab.astype(F32)), axis=2)
    def both(*pieces):
        return [each for piece in pieces for each in (piece, swap_cores(piece))]

    def after(made, *pieces):
        tied = lax.optimization_barrier((made[1],) + pieces)
        return (made[0], tied[0]), tied[1:]

    made = build(0, info, slab, half_rows, both(own), ())
    made, (across, below, above) = after(made, across, below, above)
    near = apart(across)
    other = apart_z(jnp.where(zero, above, below))
    made = build(2, info, slab, half_rows, [across, below, above], made)
    made, (passed,) = after(made, jnp.where(zero, below, above))
    beyond = apart(passed)
    made = build(5, info, slab, half_rows, [swap_cores(piece) for piece in (across, below, above)], made)
    made, (near, other) = after(made, near, other)
    far = apart(near)
    other = apart_z(other)
    made = build(8, info, slab, half_rows, [near, swap_cores(near), beyond, other], made)
    made, (far,) = after(made, far)
    made = build(12, info, slab, half_rows, [swap_cores(beyond), swap_cores(other), far], made)
    made = build(15, info, slab, half_rows, [swap_cores(far)], made)
    tiles, partial_degree = made

    in_block = (jnp.arange(SLAB_TILES) == block_index)[:, None, None]
    seeds = jnp.where(in_block, labels.astype(F32).reshape(1, 4, 128), 0.0)
    sent = jnp.concatenate([partial_degree.reshape(SLAB_TILES, 4, 128), seeds], axis=1)
    by_column = lax.all_to_all(
        jnp.broadcast_to(sent[None], (8,) + sent.shape).reshape(8 * SLAB_TILES, 8, 128), CHIPS, 0, 0, tiled=True
    ).reshape(8, SLAB_TILES, 8, 128)
    known = jnp.sum(by_column, axis=1)

    scale = 1.0 / (BLOCK_TILES * SLAB_TILES * TILE)
    block = jax.ShapeDtypeStruct((K, TILE), F32)
    running = product(info, tiles, known, swap_cores(known))
    parts = lax.all_to_all(running, COL, 0, 0, tiled=True)
    weighed = local(
        weigh_kernel, "weigh", jax.ShapeDtypeStruct((K + 16, TILE), BF16), info, parts, known
    )
    running = product(info, tiles, *share_row(weighed), partial_degree)
    parts = lax.all_to_all(running, COL, 0, 0, tiled=True)
    image, message = local(
        functools.partial(middle_kernel, scale),
        "middle",
        (block, jax.ShapeDtypeStruct((K // 2, 128), F32)),
        info,
        parts,
        known,
        by_column,
    )
    return local(
        functools.partial(last_kernel, scale), "last", block, info, sum_all(message), image, known
    )


def solution(mesh):
    fine = Mesh(np.asarray(mesh.devices).reshape(4, 2, 2, 4, 2), ROW + COL)
    in_specs = (
        P(ROW, None),
        P(ROW + COL),
        P(ROW, COL, None),
        P(ROW, COL, None),
        P(ROW, COL),
    )
    return jax.shard_map(
        shards, mesh=fine, in_specs=in_specs, out_specs=P(None, ROW + COL), check_vma=False
    )
```

```python
import functools

import jax
import jax.numpy as jnp
import numpy as np
from jax import lax
from jax.experimental import pallas as pl
from jax.experimental.pallas import tpu as pltpu
from jax.sharding import Mesh
from jax.sharding import PartitionSpec as P

TILE = 512
K = 64
PAIRS = 24
WIDTH = 1024
KERNEL_SCALE = 0.5
RATE = 2.0 / KERNEL_SCALE * float(np.log2(np.e))
F32 = jnp.float32
BF16 = jnp.bfloat16

ROW = ("y", "zh", "core")
COL = ("x", "zl")
CHIPS = ("y", "zh", "x", "zl")
SLAB_TILES = 8
BLOCK_TILES = 16
VMEM_LIMIT = 10 * 1024 * 1024
ROWS, SLABS, RANKS, GROUPS, STARTS = (8 + PAIRS * i for i in range(5))


def build_kernel(first, arrived, info, slab, half_rows, *refs):
    columns, refs = refs[:arrived], refs[arrived:]
    if first:
        _, old_degree, *refs = refs
    tiles, degree, half_column, made, sem_out = refs
    block_index = info[1]
    stores = made.shape[0]
    if first:
        degree[...] = old_degree[...]
    else:
        degree[...] = jnp.zeros_like(degree)

    begin, end = info[STARTS + first], info[STARTS + first + arrived]

    def store(entry):
        slot = lax.rem(entry, stores)
        return pltpu.make_async_copy(made.at[slot], tiles.at[entry], sem_out.at[slot])

    def step(column, own, entry, carry):
        @pl.when(entry - begin >= stores)
        def _():
            store(entry - stores).wait()

        slot = lax.rem(entry, stores)
        t = info[ROWS + entry]
        sums = []
        for n in range(2):
            lanes = pl.ds(n * 256, 256)
            inner = lax.dot_general(
                column[...], slab[t, lanes, :], (((1,), (1,)), ((), ())), preferred_element_type=F32
            )
            half_row = half_rows[pl.ds(t, 1), lanes]
            w = jnp.exp2(RATE * ((inner - half_row) - half_column[...])).astype(BF16)
            made[slot, :, lanes] = w
            sums.append(jnp.sum(w.astype(F32), axis=0, keepdims=True))
        old = degree[pl.ds(t, 1), :]
        degree[pl.ds(t, 1), :] = old + jnp.concatenate(sums, axis=1)
        if own:
            @pl.when(t == block_index)
            def _():
                w = made[slot]
                same = lax.broadcasted_iota(jnp.int32, (TILE, TILE), 0) == lax.broadcasted_iota(
                    jnp.int32, (TILE, TILE), 1
                )
                w = jnp.where(same, jnp.zeros_like(w), w)
                made[slot] = w
                degree[pl.ds(t, 1), :] = old + jnp.sum(w.astype(F32), axis=0, keepdims=True)

        store(entry).start()
        return carry

    for s, column in enumerate(columns):
        low, high = info[STARTS + first + s], info[STARTS + first + s + 1]

        @pl.when(low < high)
        def _(column=column):
            wide = column[...].astype(F32)
            half_column[...] = jnp.broadcast_to(
                0.5 * jnp.sum(wide * wide, axis=1, keepdims=True), half_column.shape
            )

        lax.fori_loop(low, high, functools.partial(step, column, first + s == 0), 0)
    for back in range(stores):

        @pl.when(end - begin > back)
        def _():
            store(end - 1 - back).wait()


def in_hbm(value):
    return pltpu.with_memory_space_constraint(value, pltpu.HBM)


def in_vmem(value):
    return pltpu.with_memory_space_constraint(value, pltpu.VMEM)


def build(first, info, slab, half_rows, columns, made):
    hbm = pl.BlockSpec(memory_space=pltpu.HBM)
    vmem = pl.BlockSpec(memory_space=pltpu.VMEM)
    arrived = len(columns)
    pairs = max(1, PAIRS * arrived // BLOCK_TILES)
    return pl.pallas_call(
        functools.partial(build_kernel, first, arrived),
        out_shape=(
            pltpu.HBM((PAIRS, TILE, TILE), BF16),
            jax.ShapeDtypeStruct((SLAB_TILES, TILE), F32),
        ),
        in_specs=[pl.BlockSpec(memory_space=pltpu.SMEM), vmem, vmem]
        + [vmem] * arrived
        + ([hbm, vmem] if made else []),
        out_specs=(hbm, vmem),
        scratch_shapes=[
            pltpu.VMEM((TILE, 256), F32),
            pltpu.VMEM((4, TILE, TILE), BF16),
            pltpu.SemaphoreType.DMA((4,)),
        ],
        input_output_aliases={3 + arrived: 0} if made else {},
        compiler_params=pltpu.CompilerParams(vmem_limit_bytes=16 * 1024 * 1024),
        cost_estimate=pl.CostEstimate(
            flops=pairs * 2 * TILE * TILE * WIDTH,
            bytes_accessed=pairs * 5 * TILE * WIDTH,
            transcendentals=pairs * TILE * TILE,
        ),
        name="build_tiles",
    )(
        info,
        in_vmem(slab),
        half_rows,
        *(in_vmem(column) for column in columns),
        *([in_hbm(made[0]), made[1]] if made else []),
    )


def terms_of(value):
    high = value.astype(BF16).astype(F32)
    middle = (value - high).astype(BF16).astype(F32)
    low = (value - high) - middle
    wide = jnp.concatenate([high, middle, low, jnp.zeros((32, 16), F32)], axis=1)
    return jnp.concatenate([wide[:16], wide[16:]], axis=1).astype(BF16)


def value_of(terms):
    wide = jnp.concatenate([terms[:, :256], terms[:, 256:]], axis=0)
    return wide[:, :80] + (wide[:, 80:160] + wide[:, 160:240])


def lead_of(sums):
    total = sums[:1, 67:68]
    return jnp.concatenate([sums[:, 65:66], sums[:, 66:67]], axis=0) / total, total


def row_of(rows, start):
    return jnp.concatenate([rows[start + i : start + i + 1] for i in range(4)], axis=1)


def product_kernel(first, info, tiles, *refs):
    if first:
        mine, others, out, running, held, sem = refs
    else:
        mine, others, degree, out, running, held, sem = refs
    count = info[0]
    core = info[2]
    depth = held.shape[0]
    running[...] = jnp.zeros_like(running)

    def fetch(entry):
        slot = lax.rem(entry, depth)
        return pltpu.make_async_copy(tiles.at[entry], held.at[slot], sem.at[slot])

    def piece(entry):
        q = info[SLABS + entry]
        own = q % 2 == core
        if first:
            known = jnp.where(own, mine[q // 2], others[q // 2])
            value, label = lax.rsqrt(row_of(known, 0)), row_of(known, 4)
            value = jnp.where(label < K, value, -value)
            label = jnp.where(label < K, label, label - K)
            same = label == lax.broadcasted_iota(jnp.int32, (K, TILE), 0).astype(F32)
            return jnp.where(same, jnp.broadcast_to(value, (K, TILE)), 0.0).astype(BF16)
        return jnp.where(own, mine[q // 2, :K, :], others[q // 2, :K, :])

    def term(entry):
        return jnp.dot(piece(entry), held[lax.rem(entry, depth)], preferred_element_type=F32)

    for entry in range(depth - 4):

        @pl.when(entry < count)
        def _():
            fetch(jnp.int32(entry)).start()

    def step(turn, carry):
        entries = [4 * turn + i for i in range(4)]
        for entry in entries:

            @pl.when(entry + depth - 4 < count)
            def _(entry=entry):
                fetch(entry + depth - 4).start()

        for entry in entries:

            @pl.when(entry < count)
            def _(entry=entry):
                fetch(entry).wait()

        terms = [term(entry) for entry in entries]
        for entry, value in zip(entries, terms, strict=True):
            running[info[ROWS + entry]] += jnp.where(entry < count, value, 0.0)
        return carry

    lax.fori_loop(0, (count + 3) // 4, step, 0)
    if first:
        out[...] = running[...].astype(BF16)
    else:
        sums = jnp.sum(mine[:, K:, :].astype(F32), axis=0) + jnp.sum(others[:, K:, :].astype(F32), axis=0)
        sums = value_of(sums)
        lead, _ = lead_of(sums)
        terms = terms_of(sums)
        for t in range(SLAB_TILES):
            out[t, :K, :] = (running[t] - lead * degree[t : t + 1, :]).astype(BF16)
            out[t, K:, :] = terms


def product(info, tiles, *operands):
    vmem = pl.BlockSpec(memory_space=pltpu.VMEM)
    first = len(operands) == 2
    return pl.pallas_call(
        functools.partial(product_kernel, first),
        out_shape=jax.ShapeDtypeStruct(
            (SLAB_TILES, K if first else K + 16, TILE), BF16
        ),
        in_specs=[
            pl.BlockSpec(memory_space=pltpu.SMEM),
            pl.BlockSpec(memory_space=pltpu.HBM),
        ]
        + [vmem] * len(operands),
        out_specs=vmem,
        scratch_shapes=[
            pltpu.VMEM((SLAB_TILES, K, TILE), F32),
            pltpu.VMEM((PAIRS, TILE, TILE), BF16),
            pltpu.SemaphoreType.DMA((PAIRS,)),
        ],
        compiler_params=pltpu.CompilerParams(vmem_limit_bytes=20 * 1024 * 1024),
        name="product",
    )(info, in_hbm(tiles), *operands)


def weights_of(image, root):
    heavy = jnp.concatenate([image, jnp.broadcast_to(root, (8, TILE))], axis=0)
    weights = lax.dot_general(
        heavy,
        heavy,
        (((1,), (1,)), ((), ())),
        precision=lax.Precision.HIGHEST,
        preferred_element_type=F32,
    )
    half = K // 2
    rows = lax.broadcasted_iota(jnp.int32, (half, half), 0)
    columns = lax.broadcasted_iota(jnp.int32, (half, half), 1)
    corner = weights[half:K, half:K]
    return jnp.concatenate(
        [
            weights[half:K, :half],
            jnp.where(rows >= columns, weights[:half, :half], corner),
            jnp.sum(jnp.where(rows == columns, corner, 0.0), axis=1, keepdims=True),
            weights[:half, K : K + 1],
            weights[half:K, K : K + 1],
            jnp.broadcast_to(weights[K : K + 1, K : K + 1], (half, 1)),
            jnp.zeros((half, 12), F32),
        ],
        axis=1,
    )


def factor_of(sums, scale):
    half = K // 2
    rows = lax.broadcasted_iota(jnp.int32, (half, half), 0)
    columns = lax.broadcasted_iota(jnp.int32, (half, half), 1)
    lower, mixed = sums[:, :half], sums[:, half:K]
    strict = jnp.where(rows > columns, mixed, 0.0)
    upper = jnp.where(rows < columns, mixed, 0.0)
    diagonal = rows == columns
    left = strict + strict.T + jnp.where(diagonal, mixed, 0.0)
    right = upper + upper.T + jnp.where(diagonal, sums[:, K : K + 1], 0.0)
    gram = jnp.concatenate(
        [jnp.concatenate([left, lower.T], axis=1), jnp.concatenate([lower, right], axis=1)], axis=0
    )
    lead, total = lead_of(sums)
    rows = lax.broadcasted_iota(jnp.int32, (K, K), 0)
    columns = lax.broadcasted_iota(jnp.int32, (K, K), 1)
    across = jnp.sum(jnp.where(rows == columns, lead, 0.0), axis=0, keepdims=True)
    gram = (gram - lead * across * total) * scale
    work = jnp.concatenate([gram, (rows == columns).astype(F32)], axis=1)
    index = lax.broadcasted_iota(jnp.int32, (K, 2 * K), 0)
    pivots = jnp.ones((K, 2 * K), F32)
    for start in range(0, K, 8):
        index = index[-(K - start) :]
        spread = [
            jnp.broadcast_to(work[start:, j : j + 1], (K - start, 2 * K)) for j in range(start, start + 8)
        ]
        rest = work[start:]
        below = pivots[start:]
        for a in range(8):
            pivot = spread[a][a : a + 1, :]
            below = jnp.where(index == start + a, pivot, below)
            ratio = jnp.where(index > start + a, spread[a] * (1.0 / pivot), 0.0)
            rest = rest - ratio * rest[a : a + 1, :]
            for b in range(a + 1, 8):
                spread[b] = spread[b] - ratio * spread[b][a : a + 1, :]
        work = jnp.concatenate([work[:start], rest], axis=0) if start else rest
        pivots = jnp.concatenate([pivots[:start], below], axis=0) if start else below
    return work[:, K:] * lax.rsqrt(pivots[:, K:]), lead


def times(factor, block):
    return jnp.dot(factor, block, precision=lax.Precision.HIGHEST, preferred_element_type=F32)


def roots_of(info, known):
    degree = row_of(known[info[3]], 0)
    return lax.rsqrt(degree), jnp.sqrt(degree)


def weigh_kernel(info, parts, known, out):
    inv_root, root = roots_of(info, known)
    image = jnp.sum(parts[...].astype(F32), axis=0) * inv_root
    out[:K, :] = (image * inv_root).astype(BF16)
    out[K:, :] = terms_of(weights_of(image, root))


def middle_kernel(scale, info, parts, known, by_column, image, message):
    inv_root, root = roots_of(info, known)
    own = by_column[info[3]]
    columns = [value_of(parts[c, K:, :].astype(F32)) for c in range(SLAB_TILES)]
    factor, lead = factor_of(sum(columns), scale)
    whole = jnp.sum(parts[:, :K, :].astype(F32), axis=0)
    for c in range(SLAB_TILES):
        whole = whole + (lead_of(columns[c])[0] - lead) * row_of(own[c], 0)
    block = times(factor, whole * inv_root)
    image[...] = block
    message[:, :80] = weights_of(block, root)
    message[:, 80:] = jnp.zeros((K // 2, 48), F32)


def last_kernel(scale, info, message, image, known, out):
    _, root = roots_of(info, known)
    factor, lead = factor_of(message[:, :80], scale)
    out[...] = times(factor, image[...] - lead * root)


def local(kernel, name, out_shape, info, *operands):
    vmem = pl.BlockSpec(memory_space=pltpu.VMEM)
    return pl.pallas_call(
        kernel,
        out_shape=out_shape,
        in_specs=[pl.BlockSpec(memory_space=pltpu.SMEM)] + [vmem] * len(operands),
        out_specs=jax.tree.map(lambda _: vmem, out_shape),
        compiler_params=pltpu.CompilerParams(vmem_limit_bytes=VMEM_LIMIT),
        name=name,
    )(info, *operands)


def swap_cores(value):
    return lax.ppermute(value, "core", [(0, 1), (1, 0)])


def share(value, axes):
    size = lax.axis_size(axes)
    return lax.all_to_all(
        jnp.broadcast_to(value[None], (size,) + value.shape), axes, 0, 0, tiled=True
    )


def share_row(value):
    mine = share(value, ("y", "zh"))
    return mine, swap_cores(mine)


def sum_all(message):
    rows = message.shape[0] // 2
    core = lax.axis_index("core")
    keep = lax.dynamic_slice_in_dim(message, core * rows, rows, 0)
    give = lax.dynamic_slice_in_dim(message, (1 - core) * rows, rows, 0)
    summed = jnp.sum(share(keep + swap_cores(give), CHIPS), axis=0)
    other = swap_cores(summed)
    first = core == 0
    return jnp.concatenate([jnp.where(first, summed, other), jnp.where(first, other, summed)], 0)


def up(value):
    return lax.ppermute(value, "y", [(i, (i + 1) % 4) for i in range(4)])


def down(value):
    return lax.ppermute(value, "y", [(i, (i + 3) % 4) for i in range(4)])


def apart(value):
    return lax.ppermute(
        value,
        ("y", "core"),
        [(2 * i + k, 2 * ((i + 1 + 2 * k) % 4) + k) for i in range(4) for k in range(2)],
    )


def apart_z(value):
    moves = []
    for z in range(4):
        for k in range(2):
            to = (z + 1 + 2 * k) % 4
            moves.append((z // 2 * 4 + k * 2 + z % 2, to // 2 * 4 + k * 2 + to % 2))
    return lax.ppermute(value, ("zh", "core", "zl"), moves)


def cross(value):
    return lax.ppermute(value, ("zh", "zl"), [(0, 3), (3, 0), (1, 2), (2, 1)])


def pair_list(head, rows, slabs, arrivals):
    count = head[0]
    slot = jnp.arange(PAIRS, dtype=jnp.int32)
    rank = jnp.sum(
        jnp.where(slabs[:, None] == arrivals[None, :], jnp.arange(BLOCK_TILES, dtype=jnp.int32), 0), 1
    )
    key = jnp.where(slot < count, rank * PAIRS + slot, BLOCK_TILES * PAIRS + slot)
    place = jnp.sum((key[None, :] < key[:, None]).astype(jnp.int32), axis=1)
    at = place[None, :] == slot[:, None]

    def ordered(value):
        return jnp.sum(jnp.where(at, value[None, :], 0), axis=1)

    ranks = ordered(rank)
    fresh = jnp.concatenate([jnp.zeros(1, bool), ranks[1:] != ranks[:-1]])
    groups = jnp.sum(jnp.where(slot[None, :] <= slot[:, None], fresh[None, :], False).astype(jnp.int32), 1)
    limit = jnp.arange(BLOCK_TILES + 1, dtype=jnp.int32) * PAIRS
    starts = jnp.sum((key[None, :] < limit[:, None]).astype(jnp.int32), axis=1)
    head = jnp.stack(head + [jnp.int32(0)] * (8 - len(head)))
    return jnp.concatenate([head, ordered(rows), ordered(slabs), ranks, groups, starts]).astype(jnp.int32)


def shards(embeddings, labels, pair_rows, pair_cols, pair_count):
    y, zh, core = (lax.axis_index(a) for a in ROW)
    slab_index = lax.axis_index(ROW)
    block_index = lax.axis_index(COL)
    zero = core == 0
    slab = embeddings.reshape(SLAB_TILES, TILE, WIDTH)

    def of(dy, dz, k):
        return ((y + dy) % 4 * 2 + (zh + dz) % 2) * 2 + k

    def side(k):
        return jnp.where(k == 0, 3, 1)

    def both_of(dy, dz):
        return [of(dy, dz, core), of(dy, dz, 1 - core)]

    near_q, other_q = (
        [of(side(k ^ way), 1, k) for k in (core, 1 - core)] for way in (0, 1)
    )
    beyond_q, far_q = both_of(2, 0), both_of(2, 1)
    arrivals = both_of(0, 0)
    arrivals += [near_by[k] for k in (0, 1) for near_by in (both_of(0, 1), both_of(3, 0), both_of(1, 0))]
    arrivals += near_q
    arrivals += [beyond_q[0], other_q[0], beyond_q[1], other_q[1], far_q[0], far_q[1]]
    arrivals = jnp.stack(arrivals)
    head = [pair_count[0, 0], block_index, core, slab_index // 2]
    info = pair_list(head, pair_rows[0, 0], pair_cols[0, 0], arrivals)

    own = lax.dynamic_index_in_dim(slab, block_index, 0, keepdims=False)
    later, own = lax.optimization_barrier((slab, own))
    below = up(own)
    above = down(own)
    give = lax.dynamic_index_in_dim(later, block_index ^ 1, 0, keepdims=False)
    across = cross(give)
    half_rows = 0.5 * jnp.sum(jnp.square(slab.astype(F32)), axis=2)
    def both(*pieces):
        return [each for piece in pieces for each in (piece, swap_cores(piece))]

    def after(made, *pieces):
        tied = lax.optimization_barrier((made[1],) + pieces)
        return (made[0], tied[0]), tied[1:]

    made = build(0, info, slab, half_rows, both(own), ())
    made, (across, below, above) = after(made, across, below, above)
    near = apart(across)
    other = apart_z(jnp.where(zero, above, below))
    made = build(2, info, slab, half_rows, [across, below, above], made)
    made, (passed,) = after(made, jnp.where(zero, below, above))
    beyond = apart(passed)
    made = build(5, info, slab, half_rows, [swap_cores(piece) for piece in (across, below, above)], made)
    made, (near, other) = after(made, near, other)
    far = apart(near)
    other = apart_z(other)
    made = build(8, info, slab, half_rows, [near, swap_cores(near), beyond, other], made)
    made, (far,) = after(made, far)
    made = build(12, info, slab, half_rows, [swap_cores(beyond), swap_cores(other), far], made)
    made = build(15, info, slab, half_rows, [swap_cores(far)], made)
    tiles, partial_degree = made

    in_block = (jnp.arange(SLAB_TILES) == block_index)[:, None, None]
    seeds = jnp.where(in_block, labels.astype(F32).reshape(1, 4, 128), 0.0)
    sent = jnp.concatenate([partial_degree.reshape(SLAB_TILES, 4, 128), seeds], axis=1)
    by_column = lax.all_to_all(
        jnp.broadcast_to(sent[None], (8,) + sent.shape).reshape(8 * SLAB_TILES, 8, 128), CHIPS, 0, 0, tiled=True
    ).reshape(8, SLAB_TILES, 8, 128)
    known = jnp.sum(by_column, axis=1)

    scale = 1.0 / (BLOCK_TILES * SLAB_TILES * TILE)
    block = jax.ShapeDtypeStruct((K, TILE), F32)
    running = product(info, tiles, known, swap_cores(known))
    parts = lax.all_to_all(running, COL, 0, 0, tiled=True)
    weighed = local(
        weigh_kernel, "weigh", jax.ShapeDtypeStruct((K + 16, TILE), BF16), info, parts, known
    )
    running = product(info, tiles, *share_row(weighed), partial_degree)
    parts = lax.all_to_all(running, COL, 0, 0, tiled=True)
    image, message = local(
        functools.partial(middle_kernel, scale),
        "middle",
        (block, jax.ShapeDtypeStruct((K // 2, 128), F32)),
        info,
        parts,
        known,
        by_column,
    )
    return local(
        functools.partial(last_kernel, scale), "last", block, info, sum_all(message), image, known
    )


def solution(mesh):
    fine = Mesh(np.asarray(mesh.devices).reshape(4, 2, 2, 4, 2), ROW + COL)
    in_specs = (
        P(ROW, None),
        P(ROW + COL),
        P(ROW, COL, None),
        P(ROW, COL, None),
        P(ROW, COL),
    )
    return jax.shard_map(
        shards, mesh=fine, in_specs=in_specs, out_specs=P(None, ROW + COL), check_vma=False
    )
```

```python
import functools

import jax
import jax.numpy as jnp
import numpy as np
from jax import lax
from jax.experimental import pallas as pl
from jax.experimental.pallas import tpu as pltpu
from jax.sharding import Mesh
from jax.sharding import PartitionSpec as P

TILE = 512
K = 64
PAIRS = 24
WIDTH = 1024
KERNEL_SCALE = 0.5
RATE = 2.0 / KERNEL_SCALE * float(np.log2(np.e))
F32 = jnp.float32
BF16 = jnp.bfloat16

ROW = ("y", "zh", "core")
COL = ("x", "zl")
CHIPS = ("y", "zh", "x", "zl")
SLAB_TILES = 8
BLOCK_TILES = 16
VMEM_LIMIT = 10 * 1024 * 1024
ROWS, SLABS, RANKS, GROUPS, STARTS = (8 + PAIRS * i for i in range(5))


def build_kernel(first, arrived, info, slab, half_rows, *refs):
    columns, refs = refs[:arrived], refs[arrived:]
    if first:
        _, old_degree, *refs = refs
    tiles, degree, made, sem_out = refs
    block_index = info[1]
    stores = made.shape[0]
    if first:
        degree[...] = old_degree[...]
    else:
        degree[...] = jnp.zeros_like(degree)

    begin, end = info[STARTS + first], info[STARTS + first + arrived]

    def store(entry):
        slot = lax.rem(entry, stores)
        return pltpu.make_async_copy(made.at[slot], tiles.at[entry], sem_out.at[slot])

    def step(column, own, entry, carry):
        @pl.when(entry - begin >= stores)
        def _():
            store(entry - stores).wait()

        slot = lax.rem(entry, stores)
        t = info[ROWS + entry]
        wide = column[...].astype(F32)
        half_column = 0.5 * jnp.sum(wide * wide, axis=1, keepdims=True)
        sums = []
        for n in range(2):
            lanes = pl.ds(n * 256, 256)
            inner = lax.dot_general(
                column[...], slab[t, lanes, :], (((1,), (1,)), ((), ())), preferred_element_type=F32
            )
            half_row = half_rows[pl.ds(t, 1), lanes]
            w = jnp.exp2(RATE * ((inner - half_row) - half_column)).astype(BF16)
            made[slot, :, lanes] = w
            sums.append(jnp.sum(w.astype(F32), axis=0, keepdims=True))
        old = degree[pl.ds(t, 1), :]
        degree[pl.ds(t, 1), :] = old + jnp.concatenate(sums, axis=1)
        if own:
            @pl.when(t == block_index)
            def _():
                w = made[slot]
                same = lax.broadcasted_iota(jnp.int32, (TILE, TILE), 0) == lax.broadcasted_iota(
                    jnp.int32, (TILE, TILE), 1
                )
                w = jnp.where(same, jnp.zeros_like(w), w)
                made[slot] = w
                degree[pl.ds(t, 1), :] = old + jnp.sum(w.astype(F32), axis=0, keepdims=True)

        store(entry).start()
        return carry

    for s, column in enumerate(columns):
        low, high = info[STARTS + first + s], info[STARTS + first + s + 1]
        lax.fori_loop(low, high, functools.partial(step, column, first + s == 0), 0)
    for back in range(stores):

        @pl.when(end - begin > back)
        def _():
            store(end - 1 - back).wait()


def in_hbm(value):
    return pltpu.with_memory_space_constraint(value, pltpu.HBM)


def in_vmem(value):
    return pltpu.with_memory_space_constraint(value, pltpu.VMEM)


def build(first, info, slab, half_rows, columns, made):
    hbm = pl.BlockSpec(memory_space=pltpu.HBM)
    vmem = pl.BlockSpec(memory_space=pltpu.VMEM)
    arrived = len(columns)
    pairs = max(1, PAIRS * arrived // BLOCK_TILES)
    return pl.pallas_call(
        functools.partial(build_kernel, first, arrived),
        out_shape=(
            pltpu.HBM((PAIRS, TILE, TILE), BF16),
            jax.ShapeDtypeStruct((SLAB_TILES, TILE), F32),
        ),
        in_specs=[pl.BlockSpec(memory_space=pltpu.SMEM), vmem, vmem]
        + [vmem] * arrived
        + ([hbm, vmem] if made else []),
        out_specs=(hbm, vmem),
        scratch_shapes=[
            pltpu.VMEM((4, TILE, TILE), BF16),
            pltpu.SemaphoreType.DMA((4,)),
        ],
        input_output_aliases={3 + arrived: 0} if made else {},
        compiler_params=pltpu.CompilerParams(vmem_limit_bytes=16 * 1024 * 1024),
        cost_estimate=pl.CostEstimate(
            flops=pairs * 2 * TILE * TILE * WIDTH,
            bytes_accessed=pairs * 5 * TILE * WIDTH,
            transcendentals=pairs * TILE * TILE,
        ),
        name="build_tiles",
    )(
        info,
        in_vmem(slab),
        half_rows,
        *(in_vmem(column) for column in columns),
        *([in_hbm(made[0]), made[1]] if made else []),
    )


def terms_of(value):
    high = value.astype(BF16).astype(F32)
    middle = (value - high).astype(BF16).astype(F32)
    low = (value - high) - middle
    wide = jnp.concatenate([high, middle, low, jnp.zeros((32, 16), F32)], axis=1)
    return jnp.concatenate([wide[:16], wide[16:]], axis=1).astype(BF16)


def value_of(terms):
    wide = jnp.concatenate([terms[:, :256], terms[:, 256:]], axis=0)
    return wide[:, :80] + (wide[:, 80:160] + wide[:, 160:240])


def lead_of(sums):
    total = sums[:1, 67:68]
    return jnp.concatenate([sums[:, 65:66], sums[:, 66:67]], axis=0) / total, total


def row_of(rows, start):
    return jnp.concatenate([rows[start + i : start + i + 1] for i in range(4)], axis=1)


def product_kernel(first, info, tiles, *refs):
    if first:
        mine, others, out, running, held, sem = refs
    else:
        mine, others, degree, out, running, held, sem = refs
    count = info[0]
    core = info[2]
    depth = held.shape[0]

    def fetch(entry):
        slot = lax.rem(entry, depth)
        return pltpu.make_async_copy(tiles.at[entry], held.at[slot], sem.at[slot])

    def piece(entry):
        q = info[SLABS + entry]
        own = q % 2 == core
        if first:
            known = jnp.where(own, mine[q // 2], others[q // 2])
            value, label = lax.rsqrt(row_of(known, 0)), row_of(known, 4)
            value = jnp.where(label < K, value, -value)
            label = jnp.where(label < K, label, label - K)
            same = label == lax.broadcasted_iota(jnp.int32, (K, TILE), 0).astype(F32)
            return jnp.where(same, jnp.broadcast_to(value, (K, TILE)), 0.0).astype(BF16)
        return jnp.where(own, mine[q // 2, :K, :], others[q // 2, :K, :])

    def term(entry):
        return jnp.dot(piece(entry), held[lax.rem(entry, depth)], preferred_element_type=F32)

    for entry in range(depth - 4):

        @pl.when(entry < count)
        def _():
            fetch(jnp.int32(entry)).start()

    running[...] = jnp.zeros_like(running)
    if not first:
        sums = jnp.sum(mine[:, K:, :].astype(F32), axis=0) + jnp.sum(others[:, K:, :].astype(F32), axis=0)
        sums = value_of(sums)
        terms = terms_of(sums)
        for t in range(SLAB_TILES):
            out[t, K:, :] = terms

    def step(turn, carry):
        entries = [4 * turn + i for i in range(4)]
        for entry in entries:

            @pl.when(entry + depth - 4 < count)
            def _(entry=entry):
                fetch(entry + depth - 4).start()

        for entry in entries:

            @pl.when(entry < count)
            def _(entry=entry):
                fetch(entry).wait()

        terms = [term(entry) for entry in entries]
        for entry, value in zip(entries, terms, strict=True):
            running[info[ROWS + entry]] += jnp.where(entry < count, value, 0.0)
        return carry

    lax.fori_loop(0, (count + 3) // 4, step, 0)
    if first:
        out[...] = running[...].astype(BF16)
    else:
        lead, _ = lead_of(sums)
        for t in range(SLAB_TILES):
            out[t, :K, :] = (running[t] - lead * degree[t : t + 1, :]).astype(BF16)


def product(info, tiles, *operands):
    vmem = pl.BlockSpec(memory_space=pltpu.VMEM)
    first = len(operands) == 2
    return pl.pallas_call(
        functools.partial(product_kernel, first),
        out_shape=jax.ShapeDtypeStruct(
            (SLAB_TILES, K if first else K + 16, TILE), BF16
        ),
        in_specs=[
            pl.BlockSpec(memory_space=pltpu.SMEM),
            pl.BlockSpec(memory_space=pltpu.HBM),
        ]
        + [vmem] * len(operands),
        out_specs=vmem,
        scratch_shapes=[
            pltpu.VMEM((SLAB_TILES, K, TILE), F32),
            pltpu.VMEM((PAIRS, TILE, TILE), BF16),
            pltpu.SemaphoreType.DMA((PAIRS,)),
        ],
        compiler_params=pltpu.CompilerParams(vmem_limit_bytes=20 * 1024 * 1024),
        name="product",
    )(info, in_hbm(tiles), *operands)


def weights_of(image, root):
    heavy = jnp.concatenate([image, jnp.broadcast_to(root, (8, TILE))], axis=0)
    weights = lax.dot_general(
        heavy,
        heavy,
        (((1,), (1,)), ((), ())),
        precision=lax.Precision.HIGHEST,
        preferred_element_type=F32,
    )
    half = K // 2
    rows = lax.broadcasted_iota(jnp.int32, (half, half), 0)
    columns = lax.broadcasted_iota(jnp.int32, (half, half), 1)
    corner = weights[half:K, half:K]
    return jnp.concatenate(
        [
            weights[half:K, :half],
            jnp.where(rows >= columns, weights[:half, :half], corner),
            jnp.sum(jnp.where(rows == columns, corner, 0.0), axis=1, keepdims=True),
            weights[:half, K : K + 1],
            weights[half:K, K : K + 1],
            jnp.broadcast_to(weights[K : K + 1, K : K + 1], (half, 1)),
            jnp.zeros((half, 12), F32),
        ],
        axis=1,
    )


def factor_of(sums, scale):
    half = K // 2
    rows = lax.broadcasted_iota(jnp.int32, (half, half), 0)
    columns = lax.broadcasted_iota(jnp.int32, (half, half), 1)
    lower, mixed = sums[:, :half], sums[:, half:K]
    strict = jnp.where(rows > columns, mixed, 0.0)
    upper = jnp.where(rows < columns, mixed, 0.0)
    diagonal = rows == columns
    left = strict + strict.T + jnp.where(diagonal, mixed, 0.0)
    right = upper + upper.T + jnp.where(diagonal, sums[:, K : K + 1], 0.0)
    gram = jnp.concatenate(
        [jnp.concatenate([left, lower.T], axis=1), jnp.concatenate([lower, right], axis=1)], axis=0
    )
    lead, total = lead_of(sums)
    rows = lax.broadcasted_iota(jnp.int32, (K, K), 0)
    columns = lax.broadcasted_iota(jnp.int32, (K, K), 1)
    across = jnp.sum(jnp.where(rows == columns, lead, 0.0), axis=0, keepdims=True)
    gram = (gram - lead * across * total) * scale
    work = jnp.concatenate([gram, (rows == columns).astype(F32)], axis=1)
    index = lax.broadcasted_iota(jnp.int32, (K, 2 * K), 0)
    pivots = jnp.ones((K, 2 * K), F32)
    for start in range(0, K, 8):
        index = index[-(K - start) :]
        spread = [
            jnp.broadcast_to(work[start:, j : j + 1], (K - start, 2 * K)) for j in range(start, start + 8)
        ]
        rest = work[start:]
        below = pivots[start:]
        for a in range(8):
            pivot = spread[a][a : a + 1, :]
            below = jnp.where(index == start + a, pivot, below)
            ratio = jnp.where(index > start + a, spread[a] * (1.0 / pivot), 0.0)
            rest = rest - ratio * rest[a : a + 1, :]
            for b in range(a + 1, 8):
                spread[b] = spread[b] - ratio * spread[b][a : a + 1, :]
        work = jnp.concatenate([work[:start], rest], axis=0) if start else rest
        pivots = jnp.concatenate([pivots[:start], below], axis=0) if start else below
    return work[:, K:] * lax.rsqrt(pivots[:, K:]), lead


def times(factor, block):
    return jnp.dot(factor, block, precision=lax.Precision.HIGHEST, preferred_element_type=F32)


def roots_of(info, known):
    degree = row_of(known[info[3]], 0)
    return lax.rsqrt(degree), jnp.sqrt(degree)


def weigh_kernel(info, parts, known, out):
    inv_root, root = roots_of(info, known)
    image = jnp.sum(parts[...].astype(F32), axis=0) * inv_root
    out[:K, :] = (image * inv_root).astype(BF16)
    out[K:, :] = terms_of(weights_of(image, root))


def middle_kernel(scale, info, parts, known, by_column, image, message):
    inv_root, root = roots_of(info, known)
    own = by_column[info[3]]
    columns = [value_of(parts[c, K:, :].astype(F32)) for c in range(SLAB_TILES)]
    factor, lead = factor_of(sum(columns), scale)
    whole = jnp.sum(parts[:, :K, :].astype(F32), axis=0)
    for c in range(SLAB_TILES):
        whole = whole + (lead_of(columns[c])[0] - lead) * row_of(own[c], 0)
    block = times(factor, whole * inv_root)
    image[...] = block
    message[:, :80] = weights_of(block, root)
    message[:, 80:] = jnp.zeros((K // 2, 48), F32)


def last_kernel(scale, info, message, image, known, out):
    _, root = roots_of(info, known)
    factor, lead = factor_of(message[:, :80], scale)
    out[...] = times(factor, image[...] - lead * root)


def local(kernel, name, out_shape, info, *operands):
    vmem = pl.BlockSpec(memory_space=pltpu.VMEM)
    return pl.pallas_call(
        kernel,
        out_shape=out_shape,
        in_specs=[pl.BlockSpec(memory_space=pltpu.SMEM)] + [vmem] * len(operands),
        out_specs=jax.tree.map(lambda _: vmem, out_shape),
        compiler_params=pltpu.CompilerParams(vmem_limit_bytes=VMEM_LIMIT),
        name=name,
    )(info, *operands)


def swap_cores(value):
    return lax.ppermute(value, "core", [(0, 1), (1, 0)])


def share(value, axes):
    size = lax.axis_size(axes)
    return lax.all_to_all(
        jnp.broadcast_to(value[None], (size,) + value.shape), axes, 0, 0, tiled=True
    )


def share_row(value):
    mine = share(value, ("y", "zh"))
    return mine, swap_cores(mine)


def sum_all(message):
    rows = message.shape[0] // 2
    core = lax.axis_index("core")
    keep = lax.dynamic_slice_in_dim(message, core * rows, rows, 0)
    give = lax.dynamic_slice_in_dim(message, (1 - core) * rows, rows, 0)
    summed = jnp.sum(share(keep + swap_cores(give), CHIPS), axis=0)
    other = swap_cores(summed)
    first = core == 0
    return jnp.concatenate([jnp.where(first, summed, other), jnp.where(first, other, summed)], 0)


def up(value):
    return lax.ppermute(value, "y", [(i, (i + 1) % 4) for i in range(4)])


def down(value):
    return lax.ppermute(value, "y", [(i, (i + 3) % 4) for i in range(4)])


def apart(value):
    return lax.ppermute(
        value,
        ("y", "core"),
        [(2 * i + k, 2 * ((i + 1 + 2 * k) % 4) + k) for i in range(4) for k in range(2)],
    )


def apart_z(value):
    moves = []
    for z in range(4):
        for k in range(2):
            to = (z + 1 + 2 * k) % 4
            moves.append((z // 2 * 4 + k * 2 + z % 2, to // 2 * 4 + k * 2 + to % 2))
    return lax.ppermute(value, ("zh", "core", "zl"), moves)


def cross(value):
    return lax.ppermute(value, ("zh", "zl"), [(0, 3), (3, 0), (1, 2), (2, 1)])


def pair_list(head, rows, slabs, arrivals):
    count = head[0]
    slot = jnp.arange(PAIRS, dtype=jnp.int32)
    rank = jnp.sum(
        jnp.where(slabs[:, None] == arrivals[None, :], jnp.arange(BLOCK_TILES, dtype=jnp.int32), 0), 1
    )
    key = jnp.where(slot < count, rank * PAIRS + slot, BLOCK_TILES * PAIRS + slot)
    place = jnp.sum((key[None, :] < key[:, None]).astype(jnp.int32), axis=1)
    at = place[None, :] == slot[:, None]

    def ordered(value):
        return jnp.sum(jnp.where(at, value[None, :], 0), axis=1)

    ranks = ordered(rank)
    fresh = jnp.concatenate([jnp.zeros(1, bool), ranks[1:] != ranks[:-1]])
    groups = jnp.sum(jnp.where(slot[None, :] <= slot[:, None], fresh[None, :], False).astype(jnp.int32), 1)
    limit = jnp.arange(BLOCK_TILES + 1, dtype=jnp.int32) * PAIRS
    starts = jnp.sum((key[None, :] < limit[:, None]).astype(jnp.int32), axis=1)
    head = jnp.stack(head + [jnp.int32(0)] * (8 - len(head)))
    return jnp.concatenate([head, ordered(rows), ordered(slabs), ranks, groups, starts]).astype(jnp.int32)


def shards(embeddings, labels, pair_rows, pair_cols, pair_count):
    y, zh, core = (lax.axis_index(a) for a in ROW)
    slab_index = lax.axis_index(ROW)
    block_index = lax.axis_index(COL)
    zero = core == 0
    slab = embeddings.reshape(SLAB_TILES, TILE, WIDTH)

    def of(dy, dz, k):
        return ((y + dy) % 4 * 2 + (zh + dz) % 2) * 2 + k

    def side(k):
        return jnp.where(k == 0, 3, 1)

    def both_of(dy, dz):
        return [of(dy, dz, core), of(dy, dz, 1 - core)]

    near_q, other_q = (
        [of(side(k ^ way), 1, k) for k in (core, 1 - core)] for way in (0, 1)
    )
    beyond_q, far_q = both_of(2, 0), both_of(2, 1)
    arrivals = both_of(0, 0)
    arrivals += [near_by[k] for k in (0, 1) for near_by in (both_of(0, 1), both_of(3, 0), both_of(1, 0))]
    arrivals += near_q
    arrivals += [beyond_q[0], other_q[0], beyond_q[1], other_q[1], far_q[0], far_q[1]]
    arrivals = jnp.stack(arrivals)
    head = [pair_count[0, 0], block_index, core, slab_index // 2]
    info = pair_list(head, pair_rows[0, 0], pair_cols[0, 0], arrivals)

    own = lax.dynamic_index_in_dim(slab, block_index, 0, keepdims=False)
    later, own = lax.optimization_barrier((slab, own))
    below = up(own)
    above = down(own)
    give = lax.dynamic_index_in_dim(later, block_index ^ 1, 0, keepdims=False)
    across = cross(give)
    half_rows = 0.5 * jnp.sum(jnp.square(slab.astype(F32)), axis=2)
    def both(*pieces):
        return [each for piece in pieces for each in (piece, swap_cores(piece))]

    def after(made, *pieces):
        tied = lax.optimization_barrier((made[1],) + pieces)
        return (made[0], tied[0]), tied[1:]

    made = build(0, info, slab, half_rows, both(own), ())
    made, (across, below, above) = after(made, across, below, above)
    near = apart(across)
    other = apart_z(jnp.where(zero, above, below))
    made = build(2, info, slab, half_rows, [across, below, above], made)
    made, (passed,) = after(made, jnp.where(zero, below, above))
    beyond = apart(passed)
    made = build(5, info, slab, half_rows, [swap_cores(piece) for piece in (across, below, above)], made)
    made, (near, other) = after(made, near, other)
    far = apart(near)
    other = apart_z(other)
    made = build(8, info, slab, half_rows, [near, swap_cores(near), beyond, other], made)
    made, (far,) = after(made, far)
    made = build(12, info, slab, half_rows, [swap_cores(beyond), swap_cores(other), far], made)
    made = build(15, info, slab, half_rows, [swap_cores(far)], made)
    tiles, partial_degree = made

    in_block = (jnp.arange(SLAB_TILES) == block_index)[:, None, None]
    seeds = jnp.where(in_block, labels.astype(F32).reshape(1, 4, 128), 0.0)
    sent = jnp.concatenate([partial_degree.reshape(SLAB_TILES, 4, 128), seeds], axis=1)
    by_column = lax.all_to_all(
        jnp.broadcast_to(sent[None], (8,) + sent.shape).reshape(8 * SLAB_TILES, 8, 128), CHIPS, 0, 0, tiled=True
    ).reshape(8, SLAB_TILES, 8, 128)
    known = jnp.sum(by_column, axis=1)

    scale = 1.0 / (BLOCK_TILES * SLAB_TILES * TILE)
    block = jax.ShapeDtypeStruct((K, TILE), F32)
    running = product(info, tiles, known, swap_cores(known))
    parts = lax.all_to_all(running, COL, 0, 0, tiled=True)
    weighed = local(
        weigh_kernel, "weigh", jax.ShapeDtypeStruct((K + 16, TILE), BF16), info, parts, known
    )
    running = product(info, tiles, *share_row(weighed), partial_degree)
    parts = lax.all_to_all(running, COL, 0, 0, tiled=True)
    image, message = local(
        functools.partial(middle_kernel, scale),
        "middle",
        (block, jax.ShapeDtypeStruct((K // 2, 128), F32)),
        info,
        parts,
        known,
        by_column,
    )
    return local(
        functools.partial(last_kernel, scale), "last", block, info, sum_all(message), image, known
    )


def solution(mesh):
    fine = Mesh(np.asarray(mesh.devices).reshape(4, 2, 2, 4, 2), ROW + COL)
    in_specs = (
        P(ROW, None),
        P(ROW + COL),
        P(ROW, COL, None),
        P(ROW, COL, None),
        P(ROW, COL),
    )
    return jax.shard_map(
        shards, mesh=fine, in_specs=in_specs, out_specs=P(None, ROW + COL), check_vma=False
    )
```

```python
import functools

import jax
import jax.numpy as jnp
import numpy as np
from jax import lax
from jax.experimental import pallas as pl
from jax.experimental.pallas import tpu as pltpu
from jax.sharding import Mesh
from jax.sharding import PartitionSpec as P

TILE = 512
K = 64
PAIRS = 24
WIDTH = 1024
KERNEL_SCALE = 0.5
RATE = 2.0 / KERNEL_SCALE * float(np.log2(np.e))
F32 = jnp.float32
BF16 = jnp.bfloat16

ROW = ("y", "zh", "core")
COL = ("x", "zl")
CHIPS = ("y", "zh", "x", "zl")
SLAB_TILES = 8
BLOCK_TILES = 16
VMEM_LIMIT = 10 * 1024 * 1024
ROWS, SLABS, RANKS, GROUPS, STARTS = (8 + PAIRS * i for i in range(5))


def build_kernel(first, arrived, info, slab, half_rows, *refs):
    columns, refs = refs[:arrived], refs[arrived:]
    if first:
        _, old_degree, *refs = refs
    tiles, degree, made, sem_out = refs
    block_index = info[1]
    stores = made.shape[0]
    if first:
        degree[...] = old_degree[...]
    else:
        degree[...] = jnp.zeros_like(degree)

    begin, end = info[STARTS + first], info[STARTS + first + arrived]

    def store(entry):
        slot = lax.rem(entry, stores)
        return pltpu.make_async_copy(made.at[slot], tiles.at[entry], sem_out.at[slot])

    def step(column, own, entry, carry):
        @pl.when(entry - begin >= stores)
        def _():
            store(entry - stores).wait()

        slot = lax.rem(entry, stores)
        t = info[ROWS + entry]
        wide = column[...].astype(F32)
        half_column = 0.5 * jnp.sum(wide * wide, axis=1, keepdims=True)
        sums = []
        for n in range(2):
            lanes = pl.ds(n * 256, 256)
            inner = lax.dot_general(
                column[...], slab[t, lanes, :], (((1,), (1,)), ((), ())), preferred_element_type=F32
            )
            half_row = half_rows[pl.ds(t, 1), lanes]
            w = jnp.exp2(RATE * ((inner - half_row) - half_column)).astype(BF16)
            made[slot, :, lanes] = w
            sums.append(jnp.sum(w.astype(F32), axis=0, keepdims=True))
        old = degree[pl.ds(t, 1), :]
        degree[pl.ds(t, 1), :] = old + jnp.concatenate(sums, axis=1)
        if own:
            @pl.when(t == block_index)
            def _():
                w = made[slot]
                same = lax.broadcasted_iota(jnp.int32, (TILE, TILE), 0) == lax.broadcasted_iota(
                    jnp.int32, (TILE, TILE), 1
                )
                w = jnp.where(same, jnp.zeros_like(w), w)
                made[slot] = w
                degree[pl.ds(t, 1), :] = old + jnp.sum(w.astype(F32), axis=0, keepdims=True)

        store(entry).start()
        return carry

    for s, column in enumerate(columns):
        low, high = info[STARTS + first + s], info[STARTS + first + s + 1]
        lax.fori_loop(low, high, functools.partial(step, column, first + s == 0), 0)
    for back in range(stores):

        @pl.when(end - begin > back)
        def _():
            store(end - 1 - back).wait()


def in_hbm(value):
    return pltpu.with_memory_space_constraint(value, pltpu.HBM)


def in_vmem(value):
    return pltpu.with_memory_space_constraint(value, pltpu.VMEM)


def build(first, info, slab, half_rows, columns, made):
    hbm = pl.BlockSpec(memory_space=pltpu.HBM)
    vmem = pl.BlockSpec(memory_space=pltpu.VMEM)
    arrived = len(columns)
    pairs = max(1, PAIRS * arrived // BLOCK_TILES)
    return pl.pallas_call(
        functools.partial(build_kernel, first, arrived),
        out_shape=(
            pltpu.HBM((PAIRS, TILE, TILE), BF16),
            jax.ShapeDtypeStruct((SLAB_TILES, TILE), F32),
        ),
        in_specs=[pl.BlockSpec(memory_space=pltpu.SMEM), vmem, vmem]
        + [vmem] * arrived
        + ([hbm, vmem] if made else []),
        out_specs=(hbm, vmem),
        scratch_shapes=[
            pltpu.VMEM((4, TILE, TILE), BF16),
            pltpu.SemaphoreType.DMA((4,)),
        ],
        input_output_aliases={3 + arrived: 0} if made else {},
        compiler_params=pltpu.CompilerParams(vmem_limit_bytes=16 * 1024 * 1024),
        cost_estimate=pl.CostEstimate(
            flops=pairs * 2 * TILE * TILE * WIDTH,
            bytes_accessed=pairs * 5 * TILE * WIDTH,
            transcendentals=pairs * TILE * TILE,
        ),
        name="build_tiles",
    )(
        info,
        in_vmem(slab),
        half_rows,
        *(in_vmem(column) for column in columns),
        *([in_hbm(made[0]), made[1]] if made else []),
    )


def terms_of(value):
    high = value.astype(BF16).astype(F32)
    middle = (value - high).astype(BF16).astype(F32)
    low = (value - high) - middle
    wide = jnp.concatenate([high, middle, low, jnp.zeros((32, 16), F32)], axis=1)
    return jnp.concatenate([wide[:16], wide[16:]], axis=1).astype(BF16)


def value_of(terms):
    wide = jnp.concatenate([terms[:, :256], terms[:, 256:]], axis=0)
    return wide[:, :80] + (wide[:, 80:160] + wide[:, 160:240])


def lead_of(sums):
    total = sums[:1, 67:68]
    return jnp.concatenate([sums[:, 65:66], sums[:, 66:67]], axis=0) / total, total


def row_of(rows, start):
    return jnp.concatenate([rows[start + i : start + i + 1] for i in range(4)], axis=1)


def product_kernel(first, info, tiles, *refs):
    if first:
        mine, others, out, running, held, sem = refs
    else:
        mine, others, degree, out, running, held, sem = refs
    count = info[0]
    core = info[2]
    depth = held.shape[0]

    def fetch(entry):
        slot = lax.rem(entry, depth)
        return pltpu.make_async_copy(tiles.at[entry], held.at[slot], sem.at[slot])

    def piece(entry):
        q = info[SLABS + entry]
        own = q % 2 == core
        if first:
            known = jnp.where(own, mine[q // 2], others[q // 2])
            value, label = lax.rsqrt(row_of(known, 0)), row_of(known, 4)
            value = jnp.where(label < K, value, -value)
            label = jnp.where(label < K, label, label - K)
            same = label == lax.broadcasted_iota(jnp.int32, (K, TILE), 0).astype(F32)
            return jnp.where(same, jnp.broadcast_to(value, (K, TILE)), 0.0).astype(BF16)
        return jnp.where(own, mine[q // 2, :K, :], others[q // 2, :K, :])

    def term(entry):
        return jnp.dot(piece(entry), held[lax.rem(entry, depth)], preferred_element_type=F32)

    for entry in range(depth - 4):

        @pl.when(entry < count)
        def _():
            fetch(jnp.int32(entry)).start()

    running[...] = jnp.zeros_like(running)
    if not first:
        sums = jnp.sum(mine[:, K:, :].astype(F32), axis=0) + jnp.sum(others[:, K:, :].astype(F32), axis=0)
        sums = value_of(sums)
        terms = terms_of(sums)
        for t in range(SLAB_TILES):
            out[t, K:, :] = terms

    def step(turn, carry):
        entries = [4 * turn + i for i in range(4)]
        for entry in entries:

            @pl.when(entry + depth - 4 < count)
            def _(entry=entry):
                fetch(entry + depth - 4).start()

        for entry in entries:

            @pl.when(entry < count)
            def _(entry=entry):
                fetch(entry).wait()

        terms = [term(entry) for entry in entries]
        for entry, value in zip(entries, terms, strict=True):
            running[info[ROWS + entry]] += jnp.where(entry < count, value, 0.0)
        return carry

    lax.fori_loop(0, (count + 3) // 4, step, 0)
    if first:
        out[...] = running[...].astype(BF16)
    else:
        lead, _ = lead_of(sums)
        for t in range(SLAB_TILES):
            out[t, :K, :] = (running[t] - lead * degree[t : t + 1, :]).astype(BF16)


def product(info, tiles, *operands):
    vmem = pl.BlockSpec(memory_space=pltpu.VMEM)
    first = len(operands) == 2
    return pl.pallas_call(
        functools.partial(product_kernel, first),
        out_shape=jax.ShapeDtypeStruct(
            (SLAB_TILES, K if first else K + 16, TILE), BF16
        ),
        in_specs=[
            pl.BlockSpec(memory_space=pltpu.SMEM),
            pl.BlockSpec(memory_space=pltpu.HBM),
        ]
        + [vmem] * len(operands),
        out_specs=vmem,
        scratch_shapes=[
            pltpu.VMEM((SLAB_TILES, K, TILE), F32),
            pltpu.VMEM((PAIRS, TILE, TILE), BF16),
            pltpu.SemaphoreType.DMA((PAIRS,)),
        ],
        compiler_params=pltpu.CompilerParams(vmem_limit_bytes=20 * 1024 * 1024),
        name="product",
    )(info, in_hbm(tiles), *operands)


def weights_of(image, root):
    heavy = jnp.concatenate([image, jnp.broadcast_to(root, (8, TILE))], axis=0)
    weights = lax.dot_general(
        heavy,
        heavy,
        (((1,), (1,)), ((), ())),
        precision=lax.Precision.HIGHEST,
        preferred_element_type=F32,
    )
    half = K // 2
    rows = lax.broadcasted_iota(jnp.int32, (half, half), 0)
    columns = lax.broadcasted_iota(jnp.int32, (half, half), 1)
    corner = weights[half:K, half:K]
    return jnp.concatenate(
        [
            weights[half:K, :half],
            jnp.where(rows >= columns, weights[:half, :half], corner),
            jnp.sum(jnp.where(rows == columns, corner, 0.0), axis=1, keepdims=True),
            weights[:half, K : K + 1],
            weights[half:K, K : K + 1],
            jnp.broadcast_to(weights[K : K + 1, K : K + 1], (half, 1)),
            jnp.zeros((half, 12), F32),
        ],
        axis=1,
    )


def factor_of(sums, scale):
    half = K // 2
    rows = lax.broadcasted_iota(jnp.int32, (half, half), 0)
    columns = lax.broadcasted_iota(jnp.int32, (half, half), 1)
    lower, mixed = sums[:, :half], sums[:, half:K]
    strict = jnp.where(rows > columns, mixed, 0.0)
    upper = jnp.where(rows < columns, mixed, 0.0)
    diagonal = rows == columns
    left = strict + strict.T + jnp.where(diagonal, mixed, 0.0)
    right = upper + upper.T + jnp.where(diagonal, sums[:, K : K + 1], 0.0)
    gram = jnp.concatenate(
        [jnp.concatenate([left, lower.T], axis=1), jnp.concatenate([lower, right], axis=1)], axis=0
    )
    lead, total = lead_of(sums)
    rows = lax.broadcasted_iota(jnp.int32, (K, K), 0)
    columns = lax.broadcasted_iota(jnp.int32, (K, K), 1)
    across = jnp.sum(jnp.where(rows == columns, lead, 0.0), axis=0, keepdims=True)
    gram = (gram - lead * across * total) * scale
    work = jnp.concatenate([gram, (rows == columns).astype(F32)], axis=1)
    index = lax.broadcasted_iota(jnp.int32, (K, 2 * K), 0)
    pivots = jnp.ones((K, 2 * K), F32)
    for start in range(0, K, 16):
        index = index[-(K - start) :]
        spread = [
            jnp.broadcast_to(work[start:, j : j + 1], (K - start, 2 * K)) for j in range(start, start + 16)
        ]
        rest = work[start:]
        below = pivots[start:]
        for a in range(16):
            pivot = spread[a][a : a + 1, :]
            below = jnp.where(index == start + a, pivot, below)
            ratio = jnp.where(index > start + a, spread[a] * (1.0 / pivot), 0.0)
            rest = rest - ratio * rest[a : a + 1, :]
            for b in range(a + 1, 16):
                spread[b] = spread[b] - ratio * spread[b][a : a + 1, :]
        work = jnp.concatenate([work[:start], rest], axis=0) if start else rest
        pivots = jnp.concatenate([pivots[:start], below], axis=0) if start else below
    return work[:, K:] * lax.rsqrt(pivots[:, K:]), lead


def times(factor, block):
    return jnp.dot(factor, block, precision=lax.Precision.HIGHEST, preferred_element_type=F32)


def roots_of(info, known):
    degree = row_of(known[info[3]], 0)
    return lax.rsqrt(degree), jnp.sqrt(degree)


def weigh_kernel(info, parts, known, out):
    inv_root, root = roots_of(info, known)
    image = jnp.sum(parts[...].astype(F32), axis=0) * inv_root
    out[:K, :] = (image * inv_root).astype(BF16)
    out[K:, :] = terms_of(weights_of(image, root))


def middle_kernel(scale, info, parts, known, by_column, image, message):
    inv_root, root = roots_of(info, known)
    own = by_column[info[3]]
    columns = [value_of(parts[c, K:, :].astype(F32)) for c in range(SLAB_TILES)]
    factor, lead = factor_of(sum(columns), scale)
    whole = jnp.sum(parts[:, :K, :].astype(F32), axis=0)
    for c in range(SLAB_TILES):
        whole = whole + (lead_of(columns[c])[0] - lead) * row_of(own[c], 0)
    block = times(factor, whole * inv_root)
    image[...] = block
    message[:, :80] = weights_of(block, root)
    message[:, 80:] = jnp.zeros((K // 2, 48), F32)


def last_kernel(scale, info, message, image, known, out):
    _, root = roots_of(info, known)
    factor, lead = factor_of(message[:, :80], scale)
    out[...] = times(factor, image[...] - lead * root)


def local(kernel, name, out_shape, info, *operands):
    vmem = pl.BlockSpec(memory_space=pltpu.VMEM)
    return pl.pallas_call(
        kernel,
        out_shape=out_shape,
        in_specs=[pl.BlockSpec(memory_space=pltpu.SMEM)] + [vmem] * len(operands),
        out_specs=jax.tree.map(lambda _: vmem, out_shape),
        compiler_params=pltpu.CompilerParams(vmem_limit_bytes=VMEM_LIMIT),
        name=name,
    )(info, *operands)


def swap_cores(value):
    return lax.ppermute(value, "core", [(0, 1), (1, 0)])


def share(value, axes):
    size = lax.axis_size(axes)
    return lax.all_to_all(
        jnp.broadcast_to(value[None], (size,) + value.shape), axes, 0, 0, tiled=True
    )


def share_row(value):
    mine = share(value, ("y", "zh"))
    return mine, swap_cores(mine)


def sum_all(message):
    rows = message.shape[0] // 2
    core = lax.axis_index("core")
    keep = lax.dynamic_slice_in_dim(message, core * rows, rows, 0)
    give = lax.dynamic_slice_in_dim(message, (1 - core) * rows, rows, 0)
    summed = jnp.sum(share(keep + swap_cores(give), CHIPS), axis=0)
    other = swap_cores(summed)
    first = core == 0
    return jnp.concatenate([jnp.where(first, summed, other), jnp.where(first, other, summed)], 0)


def up(value):
    return lax.ppermute(value, "y", [(i, (i + 1) % 4) for i in range(4)])


def down(value):
    return lax.ppermute(value, "y", [(i, (i + 3) % 4) for i in range(4)])


def apart(value):
    return lax.ppermute(
        value,
        ("y", "core"),
        [(2 * i + k, 2 * ((i + 1 + 2 * k) % 4) + k) for i in range(4) for k in range(2)],
    )


def apart_z(value):
    moves = []
    for z in range(4):
        for k in range(2):
            to = (z + 1 + 2 * k) % 4
            moves.append((z // 2 * 4 + k * 2 + z % 2, to // 2 * 4 + k * 2 + to % 2))
    return lax.ppermute(value, ("zh", "core", "zl"), moves)


def cross(value):
    return lax.ppermute(value, ("zh", "zl"), [(0, 3), (3, 0), (1, 2), (2, 1)])


def pair_list(head, rows, slabs, arrivals):
    count = head[0]
    slot = jnp.arange(PAIRS, dtype=jnp.int32)
    rank = jnp.sum(
        jnp.where(slabs[:, None] == arrivals[None, :], jnp.arange(BLOCK_TILES, dtype=jnp.int32), 0), 1
    )
    key = jnp.where(slot < count, rank * PAIRS + slot, BLOCK_TILES * PAIRS + slot)
    place = jnp.sum((key[None, :] < key[:, None]).astype(jnp.int32), axis=1)
    at = place[None, :] == slot[:, None]

    def ordered(value):
        return jnp.sum(jnp.where(at, value[None, :], 0), axis=1)

    ranks = ordered(rank)
    fresh = jnp.concatenate([jnp.zeros(1, bool), ranks[1:] != ranks[:-1]])
    groups = jnp.sum(jnp.where(slot[None, :] <= slot[:, None], fresh[None, :], False).astype(jnp.int32), 1)
    limit = jnp.arange(BLOCK_TILES + 1, dtype=jnp.int32) * PAIRS
    starts = jnp.sum((key[None, :] < limit[:, None]).astype(jnp.int32), axis=1)
    head = jnp.stack(head + [jnp.int32(0)] * (8 - len(head)))
    return jnp.concatenate([head, ordered(rows), ordered(slabs), ranks, groups, starts]).astype(jnp.int32)


def shards(embeddings, labels, pair_rows, pair_cols, pair_count):
    y, zh, core = (lax.axis_index(a) for a in ROW)
    slab_index = lax.axis_index(ROW)
    block_index = lax.axis_index(COL)
    zero = core == 0
    slab = embeddings.reshape(SLAB_TILES, TILE, WIDTH)

    def of(dy, dz, k):
        return ((y + dy) % 4 * 2 + (zh + dz) % 2) * 2 + k

    def side(k):
        return jnp.where(k == 0, 3, 1)

    def both_of(dy, dz):
        return [of(dy, dz, core), of(dy, dz, 1 - core)]

    near_q, other_q = (
        [of(side(k ^ way), 1, k) for k in (core, 1 - core)] for way in (0, 1)
    )
    beyond_q, far_q = both_of(2, 0), both_of(2, 1)
    arrivals = both_of(0, 0)
    arrivals += [near_by[k] for k in (0, 1) for near_by in (both_of(0, 1), both_of(3, 0), both_of(1, 0))]
    arrivals += near_q
    arrivals += [beyond_q[0], other_q[0], beyond_q[1], other_q[1], far_q[0], far_q[1]]
    arrivals = jnp.stack(arrivals)
    head = [pair_count[0, 0], block_index, core, slab_index // 2]
    info = pair_list(head, pair_rows[0, 0], pair_cols[0, 0], arrivals)

    own = lax.dynamic_index_in_dim(slab, block_index, 0, keepdims=False)
    later, own = lax.optimization_barrier((slab, own))
    below = up(own)
    above = down(own)
    give = lax.dynamic_index_in_dim(later, block_index ^ 1, 0, keepdims=False)
    across = cross(give)
    half_rows = 0.5 * jnp.sum(jnp.square(slab.astype(F32)), axis=2)
    def both(*pieces):
        return [each for piece in pieces for each in (piece, swap_cores(piece))]

    def after(made, *pieces):
        tied = lax.optimization_barrier((made[1],) + pieces)
        return (made[0], tied[0]), tied[1:]

    made = build(0, info, slab, half_rows, both(own), ())
    made, (across, below, above) = after(made, across, below, above)
    near = apart(across)
    other = apart_z(jnp.where(zero, above, below))
    made = build(2, info, slab, half_rows, [across, below, above], made)
    made, (passed,) = after(made, jnp.where(zero, below, above))
    beyond = apart(passed)
    made = build(5, info, slab, half_rows, [swap_cores(piece) for piece in (across, below, above)], made)
    made, (near, other) = after(made, near, other)
    far = apart(near)
    other = apart_z(other)
    made = build(8, info, slab, half_rows, [near, swap_cores(near), beyond, other, swap_cores(beyond)], made)
    made, (far,) = after(made, far)
    made = build(13, info, slab, half_rows, [swap_cores(other), far], made)
    made = build(15, info, slab, half_rows, [swap_cores(far)], made)
    tiles, partial_degree = made

    in_block = (jnp.arange(SLAB_TILES) == block_index)[:, None, None]
    seeds = jnp.where(in_block, labels.astype(F32).reshape(1, 4, 128), 0.0)
    sent = jnp.concatenate([partial_degree.reshape(SLAB_TILES, 4, 128), seeds], axis=1)
    by_column = lax.all_to_all(
        jnp.broadcast_to(sent[None], (8,) + sent.shape).reshape(8 * SLAB_TILES, 8, 128), CHIPS, 0, 0, tiled=True
    ).reshape(8, SLAB_TILES, 8, 128)
    known = jnp.sum(by_column, axis=1)

    scale = 1.0 / (BLOCK_TILES * SLAB_TILES * TILE)
    block = jax.ShapeDtypeStruct((K, TILE), F32)
    running = product(info, tiles, known, swap_cores(known))
    parts = lax.all_to_all(running, COL, 0, 0, tiled=True)
    weighed = local(
        weigh_kernel, "weigh", jax.ShapeDtypeStruct((K + 16, TILE), BF16), info, parts, known
    )
    running = product(info, tiles, *share_row(weighed), partial_degree)
    parts = lax.all_to_all(running, COL, 0, 0, tiled=True)
    image, message = local(
        functools.partial(middle_kernel, scale),
        "middle",
        (block, jax.ShapeDtypeStruct((K // 2, 128), F32)),
        info,
        parts,
        known,
        by_column,
    )
    return local(
        functools.partial(last_kernel, scale), "last", block, info, sum_all(message), image, known
    )


def solution(mesh):
    fine = Mesh(np.asarray(mesh.devices).reshape(4, 2, 2, 4, 2), ROW + COL)
    in_specs = (
        P(ROW, None),
        P(ROW + COL),
        P(ROW, COL, None),
        P(ROW, COL, None),
        P(ROW, COL),
    )
    return jax.shard_map(
        shards, mesh=fine, in_specs=in_specs, out_specs=P(None, ROW + COL), check_vma=False
    )
```

```python
import functools

import jax
import jax.numpy as jnp
import numpy as np
from jax import lax
from jax.experimental import pallas as pl
from jax.experimental.pallas import tpu as pltpu
from jax.sharding import Mesh
from jax.sharding import PartitionSpec as P

TILE = 512
K = 64
PAIRS = 24
WIDTH = 1024
KERNEL_SCALE = 0.5
RATE = 2.0 / KERNEL_SCALE * float(np.log2(np.e))
F32 = jnp.float32
BF16 = jnp.bfloat16

ROW = ("y", "zh", "core")
COL = ("x", "zl")
CHIPS = ("y", "zh", "x", "zl")
SLAB_TILES = 8
BLOCK_TILES = 16
VMEM_LIMIT = 10 * 1024 * 1024
ROWS, SLABS, RANKS, GROUPS, STARTS = (8 + PAIRS * i for i in range(5))


def build_kernel(first, arrived, info, slab, half_rows, *refs):
    columns, refs = refs[:arrived], refs[arrived:]
    if first:
        _, old_degree, *refs = refs
    tiles, degree, made, sem_out = refs
    block_index = info[1]
    stores = made.shape[0]
    if first:
        degree[...] = old_degree[...]
    else:
        degree[...] = jnp.zeros_like(degree)

    begin, end = info[STARTS + first], info[STARTS + first + arrived]

    def store(entry):
        slot = lax.rem(entry, stores)
        return pltpu.make_async_copy(made.at[slot], tiles.at[entry], sem_out.at[slot])

    def step(column, own, entry, carry):
        @pl.when(entry - begin >= stores)
        def _():
            store(entry - stores).wait()

        slot = lax.rem(entry, stores)
        t = info[ROWS + entry]
        wide = column[...].astype(F32)
        half_column = 0.5 * jnp.sum(wide * wide, axis=1, keepdims=True)
        sums = []
        for n in range(2):
            lanes = pl.ds(n * 256, 256)
            inner = lax.dot_general(
                column[...], slab[t, lanes, :], (((1,), (1,)), ((), ())), preferred_element_type=F32
            )
            half_row = half_rows[pl.ds(t, 1), lanes]
            w = jnp.exp2(RATE * ((inner - half_row) - half_column)).astype(BF16)
            made[slot, :, lanes] = w
            sums.append(jnp.sum(w.astype(F32), axis=0, keepdims=True))
        old = degree[pl.ds(t, 1), :]
        degree[pl.ds(t, 1), :] = old + jnp.concatenate(sums, axis=1)
        if own:
            @pl.when(t == block_index)
            def _():
                w = made[slot]
                same = lax.broadcasted_iota(jnp.int32, (TILE, TILE), 0) == lax.broadcasted_iota(
                    jnp.int32, (TILE, TILE), 1
                )
                w = jnp.where(same, jnp.zeros_like(w), w)
                made[slot] = w
                degree[pl.ds(t, 1), :] = old + jnp.sum(w.astype(F32), axis=0, keepdims=True)

        store(entry).start()
        return carry

    for s, column in enumerate(columns):
        low, high = info[STARTS + first + s], info[STARTS + first + s + 1]
        lax.fori_loop(low, high, functools.partial(step, column, first + s == 0), 0)
    for back in range(stores):

        @pl.when(end - begin > back)
        def _():
            store(end - 1 - back).wait()


def in_hbm(value):
    return pltpu.with_memory_space_constraint(value, pltpu.HBM)


def in_vmem(value):
    return pltpu.with_memory_space_constraint(value, pltpu.VMEM)


def build(first, info, slab, half_rows, columns, made):
    hbm = pl.BlockSpec(memory_space=pltpu.HBM)
    vmem = pl.BlockSpec(memory_space=pltpu.VMEM)
    arrived = len(columns)
    pairs = max(1, PAIRS * arrived // BLOCK_TILES)
    return pl.pallas_call(
        functools.partial(build_kernel, first, arrived),
        out_shape=(
            pltpu.HBM((PAIRS, TILE, TILE), BF16),
            jax.ShapeDtypeStruct((SLAB_TILES, TILE), F32),
        ),
        in_specs=[pl.BlockSpec(memory_space=pltpu.SMEM), vmem, vmem]
        + [vmem] * arrived
        + ([hbm, vmem] if made else []),
        out_specs=(hbm, vmem),
        scratch_shapes=[
            pltpu.VMEM((4, TILE, TILE), BF16),
            pltpu.SemaphoreType.DMA((4,)),
        ],
        input_output_aliases={3 + arrived: 0} if made else {},
        compiler_params=pltpu.CompilerParams(vmem_limit_bytes=16 * 1024 * 1024),
        cost_estimate=pl.CostEstimate(
            flops=pairs * 2 * TILE * TILE * WIDTH,
            bytes_accessed=pairs * 5 * TILE * WIDTH,
            transcendentals=pairs * TILE * TILE,
        ),
        name="build_tiles",
    )(
        info,
        in_vmem(slab),
        half_rows,
        *(in_vmem(column) for column in columns),
        *([in_hbm(made[0]), made[1]] if made else []),
    )


def terms_of(value):
    high = value.astype(BF16).astype(F32)
    middle = (value - high).astype(BF16).astype(F32)
    low = (value - high) - middle
    wide = jnp.concatenate([high, middle, low, jnp.zeros((32, 16), F32)], axis=1)
    return jnp.concatenate([wide[:16], wide[16:]], axis=1).astype(BF16)


def value_of(terms):
    wide = jnp.concatenate([terms[:, :256], terms[:, 256:]], axis=0)
    return wide[:, :80] + (wide[:, 80:160] + wide[:, 160:240])


def lead_of(sums):
    total = sums[:1, 67:68]
    return jnp.concatenate([sums[:, 65:66], sums[:, 66:67]], axis=0) / total, total


def row_of(rows, start):
    return jnp.concatenate([rows[start + i : start + i + 1] for i in range(4)], axis=1)


def seeds_of(label, value):
    value = jnp.where(label < K, value, -value)
    label = jnp.where(label < K, label, label - K)
    same = label == lax.broadcasted_iota(jnp.int32, (K, TILE), 0).astype(F32)
    return jnp.where(same, jnp.broadcast_to(value, (K, TILE)), 0.0)


def product_kernel(first, info, tiles, *refs):
    mine, others, degree, out, running, held, sem = refs
    count = info[0]
    core = info[2]
    depth = held.shape[0]

    def fetch(entry):
        slot = lax.rem(entry, depth)
        return pltpu.make_async_copy(tiles.at[entry], held.at[slot], sem.at[slot])

    def piece(entry):
        q = info[SLABS + entry]
        own = q % 2 == core
        if first:
            known = jnp.where(own, mine[q // 2], others[q // 2])
            return seeds_of(row_of(known, 4), lax.rsqrt(row_of(known, 0))).astype(BF16)
        return jnp.where(own, mine[q // 2, :K, :], others[q // 2, :K, :])

    def term(entry):
        return jnp.dot(piece(entry), held[lax.rem(entry, depth)], preferred_element_type=F32)

    for entry in range(depth - 4):

        @pl.when(entry < count)
        def _():
            fetch(jnp.int32(entry)).start()

    running[...] = jnp.zeros_like(running)
    if first:
        weights = jnp.zeros((K, TILE), F32)
        degrees = jnp.zeros((1, TILE), F32)
        for known in (mine, others):
            for chip in range(8):
                value, label = row_of(known[chip], 0), row_of(known[chip], 4)
                degrees = degrees + value
                weights = weights + seeds_of(label, jnp.sqrt(value))
        weights = jnp.sum(weights, axis=1, keepdims=True)
        total = jnp.sum(degrees, axis=1, keepdims=True)
        half = K // 2
        sums = jnp.concatenate(
            [
                jnp.zeros((half, K + 1), F32),
                weights[:half],
                weights[half:],
                jnp.broadcast_to(total, (half, 1)),
                jnp.zeros((half, 12), F32),
            ],
            axis=1,
        )
    else:
        sums = jnp.sum(mine[:, K:, :].astype(F32), axis=0) + jnp.sum(others[:, K:, :].astype(F32), axis=0)
        sums = value_of(sums)
    terms = terms_of(sums)
    for t in range(SLAB_TILES):
        out[t, K:, :] = terms

    def step(turn, carry):
        entries = [4 * turn + i for i in range(4)]
        for entry in entries:

            @pl.when(entry + depth - 4 < count)
            def _(entry=entry):
                fetch(entry + depth - 4).start()

        for entry in entries:

            @pl.when(entry < count)
            def _(entry=entry):
                fetch(entry).wait()

        terms = [term(entry) for entry in entries]
        for entry, value in zip(entries, terms, strict=True):
            running[info[ROWS + entry]] += jnp.where(entry < count, value, 0.0)
        return carry

    lax.fori_loop(0, (count + 3) // 4, step, 0)
    lead, _ = lead_of(sums)
    for t in range(SLAB_TILES):
        out[t, :K, :] = (running[t] - lead * degree[t : t + 1, :]).astype(BF16)


def product(first, info, tiles, *operands):
    vmem = pl.BlockSpec(memory_space=pltpu.VMEM)
    return pl.pallas_call(
        functools.partial(product_kernel, first),
        out_shape=jax.ShapeDtypeStruct(
            (SLAB_TILES, K + 16, TILE), BF16
        ),
        in_specs=[
            pl.BlockSpec(memory_space=pltpu.SMEM),
            pl.BlockSpec(memory_space=pltpu.HBM),
        ]
        + [vmem] * len(operands),
        out_specs=vmem,
        scratch_shapes=[
            pltpu.VMEM((SLAB_TILES, K, TILE), F32),
            pltpu.VMEM((PAIRS, TILE, TILE), BF16),
            pltpu.SemaphoreType.DMA((PAIRS,)),
        ],
        compiler_params=pltpu.CompilerParams(vmem_limit_bytes=20 * 1024 * 1024),
        name="product",
    )(info, in_hbm(tiles), *operands)


def weights_of(image, root):
    heavy = jnp.concatenate([image, jnp.broadcast_to(root, (8, TILE))], axis=0)
    weights = lax.dot_general(
        heavy,
        heavy,
        (((1,), (1,)), ((), ())),
        precision=lax.Precision.HIGHEST,
        preferred_element_type=F32,
    )
    half = K // 2
    rows = lax.broadcasted_iota(jnp.int32, (half, half), 0)
    columns = lax.broadcasted_iota(jnp.int32, (half, half), 1)
    corner = weights[half:K, half:K]
    return jnp.concatenate(
        [
            weights[half:K, :half],
            jnp.where(rows >= columns, weights[:half, :half], corner),
            jnp.sum(jnp.where(rows == columns, corner, 0.0), axis=1, keepdims=True),
            weights[:half, K : K + 1],
            weights[half:K, K : K + 1],
            jnp.broadcast_to(weights[K : K + 1, K : K + 1], (half, 1)),
            jnp.zeros((half, 12), F32),
        ],
        axis=1,
    )


def factor_of(sums, scale):
    half = K // 2
    rows = lax.broadcasted_iota(jnp.int32, (half, half), 0)
    columns = lax.broadcasted_iota(jnp.int32, (half, half), 1)
    lower, mixed = sums[:, :half], sums[:, half:K]
    strict = jnp.where(rows > columns, mixed, 0.0)
    upper = jnp.where(rows < columns, mixed, 0.0)
    diagonal = rows == columns
    left = strict + strict.T + jnp.where(diagonal, mixed, 0.0)
    right = upper + upper.T + jnp.where(diagonal, sums[:, K : K + 1], 0.0)
    gram = jnp.concatenate(
        [jnp.concatenate([left, lower.T], axis=1), jnp.concatenate([lower, right], axis=1)], axis=0
    )
    lead, total = lead_of(sums)
    rows = lax.broadcasted_iota(jnp.int32, (K, K), 0)
    columns = lax.broadcasted_iota(jnp.int32, (K, K), 1)
    across = jnp.sum(jnp.where(rows == columns, lead, 0.0), axis=0, keepdims=True)
    gram = (gram - lead * across * total) * scale
    work = jnp.concatenate([gram, (rows == columns).astype(F32)], axis=1)
    index = lax.broadcasted_iota(jnp.int32, (K, 2 * K), 0)
    pivots = jnp.ones((K, 2 * K), F32)
    for start in range(0, K, 16):
        index = index[-(K - start) :]
        spread = [
            jnp.broadcast_to(work[start:, j : j + 1], (K - start, 2 * K)) for j in range(start, start + 16)
        ]
        rest = work[start:]
        below = pivots[start:]
        for a in range(16):
            pivot = spread[a][a : a + 1, :]
            below = jnp.where(index == start + a, pivot, below)
            ratio = jnp.where(index > start + a, spread[a] * (1.0 / pivot), 0.0)
            rest = rest - ratio * rest[a : a + 1, :]
            for b in range(a + 1, 16):
                spread[b] = spread[b] - ratio * spread[b][a : a + 1, :]
        work = jnp.concatenate([work[:start], rest], axis=0) if start else rest
        pivots = jnp.concatenate([pivots[:start], below], axis=0) if start else below
    return work[:, K:] * lax.rsqrt(pivots[:, K:]), lead


def times(factor, block):
    return jnp.dot(factor, block, precision=lax.Precision.HIGHEST, preferred_element_type=F32)


def roots_of(info, known):
    degree = row_of(known[info[3]], 0)
    return lax.rsqrt(degree), jnp.sqrt(degree)


def whole_of(parts, columns, lead, by_column):
    whole = jnp.sum(parts[:, :K, :].astype(F32), axis=0)
    for c in range(SLAB_TILES):
        whole = whole + (lead_of(columns[c])[0] - lead) * row_of(by_column[c], 0)
    return whole


def weigh_kernel(info, parts, known, by_column, out):
    inv_root, root = roots_of(info, known)
    columns = [value_of(parts[c, K:, :].astype(F32)) for c in range(SLAB_TILES)]
    shift, _ = lead_of(sum(columns))
    image = whole_of(parts, columns, shift, by_column[info[3]]) * inv_root
    out[:K, :] = (image * inv_root).astype(BF16)
    out[K:, :] = terms_of(weights_of(image, root))


def middle_kernel(scale, info, parts, known, by_column, image, message):
    inv_root, root = roots_of(info, known)
    columns = [value_of(parts[c, K:, :].astype(F32)) for c in range(SLAB_TILES)]
    factor, lead = factor_of(sum(columns), scale)
    block = times(factor, whole_of(parts, columns, lead, by_column[info[3]]) * inv_root)
    image[...] = block
    message[:, :80] = weights_of(block, root)
    message[:, 80:] = jnp.zeros((K // 2, 48), F32)


def last_kernel(scale, info, message, image, known, out):
    _, root = roots_of(info, known)
    factor, lead = factor_of(message[:, :80], scale)
    out[...] = times(factor, image[...] - lead * root)


def local(kernel, name, out_shape, info, *operands):
    vmem = pl.BlockSpec(memory_space=pltpu.VMEM)
    return pl.pallas_call(
        kernel,
        out_shape=out_shape,
        in_specs=[pl.BlockSpec(memory_space=pltpu.SMEM)] + [vmem] * len(operands),
        out_specs=jax.tree.map(lambda _: vmem, out_shape),
        compiler_params=pltpu.CompilerParams(vmem_limit_bytes=VMEM_LIMIT),
        name=name,
    )(info, *operands)


def swap_cores(value):
    return lax.ppermute(value, "core", [(0, 1), (1, 0)])


def share(value, axes):
    size = lax.axis_size(axes)
    return lax.all_to_all(
        jnp.broadcast_to(value[None], (size,) + value.shape), axes, 0, 0, tiled=True
    )


def share_row(value):
    mine = share(value, ("y", "zh"))
    return mine, swap_cores(mine)


def sum_all(message):
    rows = message.shape[0] // 2
    core = lax.axis_index("core")
    keep = lax.dynamic_slice_in_dim(message, core * rows, rows, 0)
    give = lax.dynamic_slice_in_dim(message, (1 - core) * rows, rows, 0)
    summed = jnp.sum(share(keep + swap_cores(give), CHIPS), axis=0)
    other = swap_cores(summed)
    first = core == 0
    return jnp.concatenate([jnp.where(first, summed, other), jnp.where(first, other, summed)], 0)


def up(value):
    return lax.ppermute(value, "y", [(i, (i + 1) % 4) for i in range(4)])


def down(value):
    return lax.ppermute(value, "y", [(i, (i + 3) % 4) for i in range(4)])


def apart(value):
    return lax.ppermute(
        value,
        ("y", "core"),
        [(2 * i + k, 2 * ((i + 1 + 2 * k) % 4) + k) for i in range(4) for k in range(2)],
    )


def apart_z(value):
    moves = []
    for z in range(4):
        for k in range(2):
            to = (z + 1 + 2 * k) % 4
            moves.append((z // 2 * 4 + k * 2 + z % 2, to // 2 * 4 + k * 2 + to % 2))
    return lax.ppermute(value, ("zh", "core", "zl"), moves)


def cross(value):
    return lax.ppermute(value, ("zh", "zl"), [(0, 3), (3, 0), (1, 2), (2, 1)])


def pair_list(head, rows, slabs, arrivals):
    count = head[0]
    slot = jnp.arange(PAIRS, dtype=jnp.int32)
    rank = jnp.sum(
        jnp.where(slabs[:, None] == arrivals[None, :], jnp.arange(BLOCK_TILES, dtype=jnp.int32), 0), 1
    )
    key = jnp.where(slot < count, rank * PAIRS + slot, BLOCK_TILES * PAIRS + slot)
    place = jnp.sum((key[None, :] < key[:, None]).astype(jnp.int32), axis=1)
    at = place[None, :] == slot[:, None]

    def ordered(value):
        return jnp.sum(jnp.where(at, value[None, :], 0), axis=1)

    ranks = ordered(rank)
    fresh = jnp.concatenate([jnp.zeros(1, bool), ranks[1:] != ranks[:-1]])
    groups = jnp.sum(jnp.where(slot[None, :] <= slot[:, None], fresh[None, :], False).astype(jnp.int32), 1)
    limit = jnp.arange(BLOCK_TILES + 1, dtype=jnp.int32) * PAIRS
    starts = jnp.sum((key[None, :] < limit[:, None]).astype(jnp.int32), axis=1)
    head = jnp.stack(head + [jnp.int32(0)] * (8 - len(head)))
    return jnp.concatenate([head, ordered(rows), ordered(slabs), ranks, groups, starts]).astype(jnp.int32)


def shards(embeddings, labels, pair_rows, pair_cols, pair_count):
    y, zh, core = (lax.axis_index(a) for a in ROW)
    slab_index = lax.axis_index(ROW)
    block_index = lax.axis_index(COL)
    zero = core == 0
    slab = embeddings.reshape(SLAB_TILES, TILE, WIDTH)

    def of(dy, dz, k):
        return ((y + dy) % 4 * 2 + (zh + dz) % 2) * 2 + k

    def side(k):
        return jnp.where(k == 0, 3, 1)

    def both_of(dy, dz):
        return [of(dy, dz, core), of(dy, dz, 1 - core)]

    near_q, other_q = (
        [of(side(k ^ way), 1, k) for k in (core, 1 - core)] for way in (0, 1)
    )
    beyond_q, far_q = both_of(2, 0), both_of(2, 1)
    arrivals = both_of(0, 0)
    arrivals += [near_by[k] for k in (0, 1) for near_by in (both_of(0, 1), both_of(3, 0), both_of(1, 0))]
    arrivals += near_q
    arrivals += [beyond_q[0], other_q[0], beyond_q[1], other_q[1], far_q[0], far_q[1]]
    arrivals = jnp.stack(arrivals)
    head = [pair_count[0, 0], block_index, core, slab_index // 2]
    info = pair_list(head, pair_rows[0, 0], pair_cols[0, 0], arrivals)

    own = lax.dynamic_index_in_dim(slab, block_index, 0, keepdims=False)
    later, own = lax.optimization_barrier((slab, own))
    below = up(own)
    above = down(own)
    give = lax.dynamic_index_in_dim(later, block_index ^ 1, 0, keepdims=False)
    across = cross(give)
    half_rows = 0.5 * jnp.sum(jnp.square(slab.astype(F32)), axis=2)
    def both(*pieces):
        return [each for piece in pieces for each in (piece, swap_cores(piece))]

    def after(made, *pieces):
        tied = lax.optimization_barrier((made[1],) + pieces)
        return (made[0], tied[0]), tied[1:]

    made = build(0, info, slab, half_rows, both(own), ())
    made, (across, below, above) = after(made, across, below, above)
    near = apart(across)
    other = apart_z(jnp.where(zero, above, below))
    made = build(2, info, slab, half_rows, [across, below, above], made)
    made, (passed,) = after(made, jnp.where(zero, below, above))
    beyond = apart(passed)
    made = build(5, info, slab, half_rows, [swap_cores(piece) for piece in (across, below, above)], made)
    made, (near, other) = after(made, near, other)
    far = apart(near)
    other = apart_z(other)
    made = build(8, info, slab, half_rows, [near, swap_cores(near), beyond, other, swap_cores(beyond)], made)
    made, (far,) = after(made, far)
    made = build(13, info, slab, half_rows, [swap_cores(other), far], made)
    made = build(15, info, slab, half_rows, [swap_cores(far)], made)
    tiles, partial_degree = made

    in_block = (jnp.arange(SLAB_TILES) == block_index)[:, None, None]
    seeds = jnp.where(in_block, labels.astype(F32).reshape(1, 4, 128), 0.0)
    sent = jnp.concatenate([partial_degree.reshape(SLAB_TILES, 4, 128), seeds], axis=1)
    by_column = lax.all_to_all(
        jnp.broadcast_to(sent[None], (8,) + sent.shape).reshape(8 * SLAB_TILES, 8, 128), CHIPS, 0, 0, tiled=True
    ).reshape(8, SLAB_TILES, 8, 128)
    known = jnp.sum(by_column, axis=1)

    scale = 1.0 / (BLOCK_TILES * SLAB_TILES * TILE)
    block = jax.ShapeDtypeStruct((K, TILE), F32)
    running = product(True, info, tiles, known, swap_cores(known), partial_degree)
    parts = lax.all_to_all(running, COL, 0, 0, tiled=True)
    weighed = local(
        weigh_kernel, "weigh", jax.ShapeDtypeStruct((K + 16, TILE), BF16), info, parts, known, by_column
    )
    running = product(False, info, tiles, *share_row(weighed), partial_degree)
    parts = lax.all_to_all(running, COL, 0, 0, tiled=True)
    image, message = local(
        functools.partial(middle_kernel, scale),
        "middle",
        (block, jax.ShapeDtypeStruct((K // 2, 128), F32)),
        info,
        parts,
        known,
        by_column,
    )
    return local(
        functools.partial(last_kernel, scale), "last", block, info, sum_all(message), image, known
    )


def solution(mesh):
    fine = Mesh(np.asarray(mesh.devices).reshape(4, 2, 2, 4, 2), ROW + COL)
    in_specs = (
        P(ROW, None),
        P(ROW + COL),
        P(ROW, COL, None),
        P(ROW, COL, None),
        P(ROW, COL),
    )
    return jax.shard_map(
        shards, mesh=fine, in_specs=in_specs, out_specs=P(None, ROW + COL), check_vma=False
    )
```

```python
import functools

import jax
import jax.numpy as jnp
import numpy as np
from jax import lax
from jax.experimental import pallas as pl
from jax.experimental.pallas import tpu as pltpu
from jax.sharding import Mesh
from jax.sharding import PartitionSpec as P

TILE = 512
K = 64
PAIRS = 24
WIDTH = 1024
KERNEL_SCALE = 0.5
RATE = 2.0 / KERNEL_SCALE * float(np.log2(np.e))
F32 = jnp.float32
BF16 = jnp.bfloat16

ROW = ("y", "zh", "core")
COL = ("x", "zl")
CHIPS = ("y", "zh", "x", "zl")
SLAB_TILES = 8
BLOCK_TILES = 16
VMEM_LIMIT = 10 * 1024 * 1024
ROWS, SLABS, RANKS, GROUPS, STARTS = (8 + PAIRS * i for i in range(5))


def build_kernel(first, arrived, info, slab, half_rows, *refs):
    columns, refs = refs[:arrived], refs[arrived:]
    if first:
        _, old_degree, *refs = refs
    tiles, degree, made, sem_out = refs
    block_index = info[1]
    stores = made.shape[0]
    if first:
        degree[...] = old_degree[...]
    else:
        degree[...] = jnp.zeros_like(degree)

    begin, end = info[STARTS + first], info[STARTS + first + arrived]

    def store(entry, n):
        slot = lax.rem(entry, stores)
        lanes = pl.ds(n * 256, 256)
        return pltpu.make_async_copy(
            made.at[slot, :, lanes], tiles.at[entry, :, lanes], sem_out.at[slot, n]
        )

    def step(column, own, entry, carry):
        @pl.when(entry - begin >= stores)
        def _():
            for n in range(2):
                store(entry - stores, n).wait()

        slot = lax.rem(entry, stores)
        t = info[ROWS + entry]
        wide = column[...].astype(F32)
        half_column = 0.5 * jnp.sum(wide * wide, axis=1, keepdims=True)
        sums = []
        for n in range(2):
            lanes = pl.ds(n * 256, 256)
            inner = lax.dot_general(
                column[...], slab[t, lanes, :], (((1,), (1,)), ((), ())), preferred_element_type=F32
            )
            half_row = half_rows[pl.ds(t, 1), lanes]
            w = jnp.exp2(RATE * ((inner - half_row) - half_column)).astype(BF16)
            made[slot, :, lanes] = w
            if not own:
                store(entry, n).start()
            sums.append(jnp.sum(w.astype(F32), axis=0, keepdims=True))
        old = degree[pl.ds(t, 1), :]
        degree[pl.ds(t, 1), :] = old + jnp.concatenate(sums, axis=1)
        if own:
            @pl.when(t == block_index)
            def _():
                w = made[slot]
                same = lax.broadcasted_iota(jnp.int32, (TILE, TILE), 0) == lax.broadcasted_iota(
                    jnp.int32, (TILE, TILE), 1
                )
                w = jnp.where(same, jnp.zeros_like(w), w)
                made[slot] = w
                degree[pl.ds(t, 1), :] = old + jnp.sum(w.astype(F32), axis=0, keepdims=True)

            for n in range(2):
                store(entry, n).start()
        return carry

    for s, column in enumerate(columns):
        low, high = info[STARTS + first + s], info[STARTS + first + s + 1]
        lax.fori_loop(low, high, functools.partial(step, column, first + s == 0), 0)
    for back in range(stores):

        @pl.when(end - begin > back)
        def _():
            for n in range(2):
                store(end - 1 - back, n).wait()


def in_hbm(value):
    return pltpu.with_memory_space_constraint(value, pltpu.HBM)


def in_vmem(value):
    return pltpu.with_memory_space_constraint(value, pltpu.VMEM)


def build(first, info, slab, half_rows, columns, made):
    hbm = pl.BlockSpec(memory_space=pltpu.HBM)
    vmem = pl.BlockSpec(memory_space=pltpu.VMEM)
    arrived = len(columns)
    pairs = max(1, PAIRS * arrived // BLOCK_TILES)
    return pl.pallas_call(
        functools.partial(build_kernel, first, arrived),
        out_shape=(
            pltpu.HBM((PAIRS, TILE, TILE), BF16),
            jax.ShapeDtypeStruct((SLAB_TILES, TILE), F32),
        ),
        in_specs=[pl.BlockSpec(memory_space=pltpu.SMEM), vmem, vmem]
        + [vmem] * arrived
        + ([hbm, vmem] if made else []),
        out_specs=(hbm, vmem),
        scratch_shapes=[
            pltpu.VMEM((4, TILE, TILE), BF16),
            pltpu.SemaphoreType.DMA((4, 2)),
        ],
        input_output_aliases={3 + arrived: 0} if made else {},
        compiler_params=pltpu.CompilerParams(vmem_limit_bytes=16 * 1024 * 1024),
        cost_estimate=pl.CostEstimate(
            flops=pairs * 2 * TILE * TILE * WIDTH,
            bytes_accessed=pairs * 5 * TILE * WIDTH,
            transcendentals=pairs * TILE * TILE,
        ),
        name="build_tiles",
    )(
        info,
        in_vmem(slab),
        half_rows,
        *(in_vmem(column) for column in columns),
        *([in_hbm(made[0]), made[1]] if made else []),
    )


def terms_of(value):
    high = value.astype(BF16).astype(F32)
    middle = (value - high).astype(BF16).astype(F32)
    low = (value - high) - middle
    wide = jnp.concatenate([high, middle, low, jnp.zeros((32, 16), F32)], axis=1)
    return jnp.concatenate([wide[:16], wide[16:]], axis=1).astype(BF16)


def value_of(terms):
    wide = jnp.concatenate([terms[:, :256], terms[:, 256:]], axis=0)
    return wide[:, :80] + (wide[:, 80:160] + wide[:, 160:240])


def lead_of(sums):
    total = sums[:1, 67:68]
    return jnp.concatenate([sums[:, 65:66], sums[:, 66:67]], axis=0) / total, total


def row_of(rows, start):
    return jnp.concatenate([rows[start + i : start + i + 1] for i in range(4)], axis=1)


def product_kernel(first, info, tiles, *refs):
    if first:
        mine, others, out, running, held, sem = refs
    else:
        mine, others, degree, out, running, held, sem = refs
    count = info[0]
    core = info[2]
    depth = held.shape[0]

    def fetch(entry):
        slot = lax.rem(entry, depth)
        return pltpu.make_async_copy(tiles.at[entry], held.at[slot], sem.at[slot])

    def piece(entry):
        q = info[SLABS + entry]
        own = q % 2 == core
        if first:
            known = jnp.where(own, mine[q // 2], others[q // 2])
            value, label = lax.rsqrt(row_of(known, 0)), row_of(known, 4)
            value = jnp.where(label < K, value, -value)
            label = jnp.where(label < K, label, label - K)
            same = label == lax.broadcasted_iota(jnp.int32, (K, TILE), 0).astype(F32)
            return jnp.where(same, jnp.broadcast_to(value, (K, TILE)), 0.0).astype(BF16)
        return jnp.where(own, mine[q // 2, :K, :], others[q // 2, :K, :])

    def term(entry):
        return jnp.dot(piece(entry), held[lax.rem(entry, depth)], preferred_element_type=F32)

    for entry in range(depth - 4):

        @pl.when(entry < count)
        def _():
            fetch(jnp.int32(entry)).start()

    running[...] = jnp.zeros_like(running)
    if not first:
        sums = jnp.sum(mine[:, K:, :].astype(F32), axis=0) + jnp.sum(others[:, K:, :].astype(F32), axis=0)
        sums = value_of(sums)
        terms = terms_of(sums)
        for t in range(SLAB_TILES):
            out[t, K:, :] = terms

    def step(turn, carry):
        entries = [4 * turn + i for i in range(4)]
        for entry in entries:

            @pl.when(entry + depth - 4 < count)
            def _(entry=entry):
                fetch(entry + depth - 4).start()

        for entry in entries:

            @pl.when(entry < count)
            def _(entry=entry):
                fetch(entry).wait()

        terms = [term(entry) for entry in entries]
        for entry, value in zip(entries, terms, strict=True):
            running[info[ROWS + entry]] += jnp.where(entry < count, value, 0.0)
        return carry

    lax.fori_loop(0, (count + 3) // 4, step, 0)
    if first:
        out[...] = running[...].astype(BF16)
    else:
        lead, _ = lead_of(sums)
        for t in range(SLAB_TILES):
            out[t, :K, :] = (running[t] - lead * degree[t : t + 1, :]).astype(BF16)


def product(info, tiles, *operands):
    vmem = pl.BlockSpec(memory_space=pltpu.VMEM)
    first = len(operands) == 2
    return pl.pallas_call(
        functools.partial(product_kernel, first),
        out_shape=jax.ShapeDtypeStruct(
            (SLAB_TILES, K if first else K + 16, TILE), BF16
        ),
        in_specs=[
            pl.BlockSpec(memory_space=pltpu.SMEM),
            pl.BlockSpec(memory_space=pltpu.HBM),
        ]
        + [vmem] * len(operands),
        out_specs=vmem,
        scratch_shapes=[
            pltpu.VMEM((SLAB_TILES, K, TILE), F32),
            pltpu.VMEM((PAIRS, TILE, TILE), BF16),
            pltpu.SemaphoreType.DMA((PAIRS,)),
        ],
        compiler_params=pltpu.CompilerParams(vmem_limit_bytes=20 * 1024 * 1024),
        name="product",
    )(info, in_hbm(tiles), *operands)


def weights_of(image, root):
    heavy = jnp.concatenate([image, jnp.broadcast_to(root, (8, TILE))], axis=0)
    weights = lax.dot_general(
        heavy,
        heavy,
        (((1,), (1,)), ((), ())),
        precision=lax.Precision.HIGHEST,
        preferred_element_type=F32,
    )
    half = K // 2
    rows = lax.broadcasted_iota(jnp.int32, (half, half), 0)
    columns = lax.broadcasted_iota(jnp.int32, (half, half), 1)
    corner = weights[half:K, half:K]
    return jnp.concatenate(
        [
            weights[half:K, :half],
            jnp.where(rows >= columns, weights[:half, :half], corner),
            jnp.sum(jnp.where(rows == columns, corner, 0.0), axis=1, keepdims=True),
            weights[:half, K : K + 1],
            weights[half:K, K : K + 1],
            jnp.broadcast_to(weights[K : K + 1, K : K + 1], (half, 1)),
            jnp.zeros((half, 12), F32),
        ],
        axis=1,
    )


def factor_of(sums, scale):
    half = K // 2
    rows = lax.broadcasted_iota(jnp.int32, (half, half), 0)
    columns = lax.broadcasted_iota(jnp.int32, (half, half), 1)
    lower, mixed = sums[:, :half], sums[:, half:K]
    strict = jnp.where(rows > columns, mixed, 0.0)
    upper = jnp.where(rows < columns, mixed, 0.0)
    diagonal = rows == columns
    left = strict + strict.T + jnp.where(diagonal, mixed, 0.0)
    right = upper + upper.T + jnp.where(diagonal, sums[:, K : K + 1], 0.0)
    gram = jnp.concatenate(
        [jnp.concatenate([left, lower.T], axis=1), jnp.concatenate([lower, right], axis=1)], axis=0
    )
    lead, total = lead_of(sums)
    rows = lax.broadcasted_iota(jnp.int32, (K, K), 0)
    columns = lax.broadcasted_iota(jnp.int32, (K, K), 1)
    across = jnp.sum(jnp.where(rows == columns, lead, 0.0), axis=0, keepdims=True)
    gram = (gram - lead * across * total) * scale
    work = jnp.concatenate([gram, (rows == columns).astype(F32)], axis=1)
    index = lax.broadcasted_iota(jnp.int32, (K, 2 * K), 0)
    pivots = jnp.ones((K, 2 * K), F32)
    for start in range(0, K, 16):
        index = index[-(K - start) :]
        spread = [
            jnp.broadcast_to(work[start:, j : j + 1], (K - start, 2 * K)) for j in range(start, start + 16)
        ]
        rest = work[start:]
        below = pivots[start:]
        for a in range(16):
            pivot = spread[a][a : a + 1, :]
            below = jnp.where(index == start + a, pivot, below)
            ratio = jnp.where(index > start + a, spread[a] * (1.0 / pivot), 0.0)
            rest = rest - ratio * rest[a : a + 1, :]
            for b in range(a + 1, 16):
                spread[b] = spread[b] - ratio * spread[b][a : a + 1, :]
        work = jnp.concatenate([work[:start], rest], axis=0) if start else rest
        pivots = jnp.concatenate([pivots[:start], below], axis=0) if start else below
    return work[:, K:] * lax.rsqrt(pivots[:, K:]), lead


def times(factor, block):
    return jnp.dot(factor, block, precision=lax.Precision.HIGHEST, preferred_element_type=F32)


def roots_of(info, known):
    degree = row_of(known[info[3]], 0)
    return lax.rsqrt(degree), jnp.sqrt(degree)


def weigh_kernel(info, parts, known, out):
    inv_root, root = roots_of(info, known)
    image = jnp.sum(parts[...].astype(F32), axis=0) * inv_root
    out[:K, :] = (image * inv_root).astype(BF16)
    out[K:, :] = terms_of(weights_of(image, root))


def middle_kernel(scale, info, parts, known, by_column, image, message):
    inv_root, root = roots_of(info, known)
    own = by_column[info[3]]
    columns = [value_of(parts[c, K:, :].astype(F32)) for c in range(SLAB_TILES)]
    factor, lead = factor_of(sum(columns), scale)
    whole = jnp.sum(parts[:, :K, :].astype(F32), axis=0)
    for c in range(SLAB_TILES):
        whole = whole + (lead_of(columns[c])[0] - lead) * row_of(own[c], 0)
    block = times(factor, whole * inv_root)
    image[...] = block
    message[:, :80] = weights_of(block, root)
    message[:, 80:] = jnp.zeros((K // 2, 48), F32)


def last_kernel(scale, info, message, image, known, out):
    _, root = roots_of(info, known)
    factor, lead = factor_of(message[:, :80], scale)
    out[...] = times(factor, image[...] - lead * root)


def local(kernel, name, out_shape, info, *operands):
    vmem = pl.BlockSpec(memory_space=pltpu.VMEM)
    return pl.pallas_call(
        kernel,
        out_shape=out_shape,
        in_specs=[pl.BlockSpec(memory_space=pltpu.SMEM)] + [vmem] * len(operands),
        out_specs=jax.tree.map(lambda _: vmem, out_shape),
        compiler_params=pltpu.CompilerParams(vmem_limit_bytes=VMEM_LIMIT),
        name=name,
    )(info, *operands)


def swap_cores(value):
    return lax.ppermute(value, "core", [(0, 1), (1, 0)])


def share(value, axes):
    size = lax.axis_size(axes)
    return lax.all_to_all(
        jnp.broadcast_to(value[None], (size,) + value.shape), axes, 0, 0, tiled=True
    )


def share_row(value):
    mine = share(value, ("y", "zh"))
    return mine, swap_cores(mine)


def sum_all(message):
    rows = message.shape[0] // 2
    core = lax.axis_index("core")
    keep = lax.dynamic_slice_in_dim(message, core * rows, rows, 0)
    give = lax.dynamic_slice_in_dim(message, (1 - core) * rows, rows, 0)
    summed = jnp.sum(share(keep + swap_cores(give), CHIPS), axis=0)
    other = swap_cores(summed)
    first = core == 0
    return jnp.concatenate([jnp.where(first, summed, other), jnp.where(first, other, summed)], 0)


def up(value):
    return lax.ppermute(value, "y", [(i, (i + 1) % 4) for i in range(4)])


def down(value):
    return lax.ppermute(value, "y", [(i, (i + 3) % 4) for i in range(4)])


def apart(value):
    return lax.ppermute(
        value,
        ("y", "core"),
        [(2 * i + k, 2 * ((i + 1 + 2 * k) % 4) + k) for i in range(4) for k in range(2)],
    )


def apart_z(value):
    moves = []
    for z in range(4):
        for k in range(2):
            to = (z + 1 + 2 * k) % 4
            moves.append((z // 2 * 4 + k * 2 + z % 2, to // 2 * 4 + k * 2 + to % 2))
    return lax.ppermute(value, ("zh", "core", "zl"), moves)


def cross(value):
    return lax.ppermute(value, ("zh", "zl"), [(0, 3), (3, 0), (1, 2), (2, 1)])


def pair_list(head, rows, slabs, arrivals):
    count = head[0]
    slot = jnp.arange(PAIRS, dtype=jnp.int32)
    rank = jnp.sum(
        jnp.where(slabs[:, None] == arrivals[None, :], jnp.arange(BLOCK_TILES, dtype=jnp.int32), 0), 1
    )
    key = jnp.where(slot < count, rank * PAIRS + slot, BLOCK_TILES * PAIRS + slot)
    place = jnp.sum((key[None, :] < key[:, None]).astype(jnp.int32), axis=1)
    at = place[None, :] == slot[:, None]

    def ordered(value):
        return jnp.sum(jnp.where(at, value[None, :], 0), axis=1)

    ranks = ordered(rank)
    fresh = jnp.concatenate([jnp.zeros(1, bool), ranks[1:] != ranks[:-1]])
    groups = jnp.sum(jnp.where(slot[None, :] <= slot[:, None], fresh[None, :], False).astype(jnp.int32), 1)
    limit = jnp.arange(BLOCK_TILES + 1, dtype=jnp.int32) * PAIRS
    starts = jnp.sum((key[None, :] < limit[:, None]).astype(jnp.int32), axis=1)
    head = jnp.stack(head + [jnp.int32(0)] * (8 - len(head)))
    return jnp.concatenate([head, ordered(rows), ordered(slabs), ranks, groups, starts]).astype(jnp.int32)


def shards(embeddings, labels, pair_rows, pair_cols, pair_count):
    y, zh, core = (lax.axis_index(a) for a in ROW)
    slab_index = lax.axis_index(ROW)
    block_index = lax.axis_index(COL)
    zero = core == 0
    slab = embeddings.reshape(SLAB_TILES, TILE, WIDTH)

    def of(dy, dz, k):
        return ((y + dy) % 4 * 2 + (zh + dz) % 2) * 2 + k

    def side(k):
        return jnp.where(k == 0, 3, 1)

    def both_of(dy, dz):
        return [of(dy, dz, core), of(dy, dz, 1 - core)]

    near_q, other_q = (
        [of(side(k ^ way), 1, k) for k in (core, 1 - core)] for way in (0, 1)
    )
    beyond_q, far_q = both_of(2, 0), both_of(2, 1)
    arrivals = both_of(0, 0)
    arrivals += [near_by[k] for k in (0, 1) for near_by in (both_of(0, 1), both_of(3, 0), both_of(1, 0))]
    arrivals += near_q
    arrivals += [beyond_q[0], other_q[0], beyond_q[1], other_q[1], far_q[0], far_q[1]]
    arrivals = jnp.stack(arrivals)
    head = [pair_count[0, 0], block_index, core, slab_index // 2]
    info = pair_list(head, pair_rows[0, 0], pair_cols[0, 0], arrivals)

    own = lax.dynamic_index_in_dim(slab, block_index, 0, keepdims=False)
    later, own = lax.optimization_barrier((slab, own))
    below = up(own)
    above = down(own)
    give = lax.dynamic_index_in_dim(later, block_index ^ 1, 0, keepdims=False)
    across = cross(give)
    half_rows = 0.5 * jnp.sum(jnp.square(slab.astype(F32)), axis=2)
    def both(*pieces):
        return [each for piece in pieces for each in (piece, swap_cores(piece))]

    def after(made, *pieces):
        tied = lax.optimization_barrier((made[1],) + pieces)
        return (made[0], tied[0]), tied[1:]

    made = build(0, info, slab, half_rows, both(own), ())
    made, (across, below, above) = after(made, across, below, above)
    near = apart(across)
    other = apart_z(jnp.where(zero, above, below))
    made = build(2, info, slab, half_rows, [across, below, above], made)
    made, (passed,) = after(made, jnp.where(zero, below, above))
    beyond = apart(passed)
    made = build(5, info, slab, half_rows, [swap_cores(piece) for piece in (across, below, above)], made)
    made, (near, other) = after(made, near, other)
    far = apart(near)
    other = apart_z(other)
    made = build(8, info, slab, half_rows, [near, swap_cores(near), beyond, other, swap_cores(beyond)], made)
    made, (far,) = after(made, far)
    made = build(13, info, slab, half_rows, [swap_cores(other), far], made)
    made = build(15, info, slab, half_rows, [swap_cores(far)], made)
    tiles, partial_degree = made

    in_block = (jnp.arange(SLAB_TILES) == block_index)[:, None, None]
    seeds = jnp.where(in_block, labels.astype(F32).reshape(1, 4, 128), 0.0)
    sent = jnp.concatenate([partial_degree.reshape(SLAB_TILES, 4, 128), seeds], axis=1)
    by_column = lax.all_to_all(
        jnp.broadcast_to(sent[None], (8,) + sent.shape).reshape(8 * SLAB_TILES, 8, 128), CHIPS, 0, 0, tiled=True
    ).reshape(8, SLAB_TILES, 8, 128)
    known = jnp.sum(by_column, axis=1)

    scale = 1.0 / (BLOCK_TILES * SLAB_TILES * TILE)
    block = jax.ShapeDtypeStruct((K, TILE), F32)
    running = product(info, tiles, known, swap_cores(known))
    parts = lax.all_to_all(running, COL, 0, 0, tiled=True)
    weighed = local(
        weigh_kernel, "weigh", jax.ShapeDtypeStruct((K + 16, TILE), BF16), info, parts, known
    )
    running = product(info, tiles, *share_row(weighed), partial_degree)
    parts = lax.all_to_all(running, COL, 0, 0, tiled=True)
    image, message = local(
        functools.partial(middle_kernel, scale),
        "middle",
        (block, jax.ShapeDtypeStruct((K // 2, 128), F32)),
        info,
        parts,
        known,
        by_column,
    )
    return local(
        functools.partial(last_kernel, scale), "last", block, info, sum_all(message), image, known
    )


def solution(mesh):
    fine = Mesh(np.asarray(mesh.devices).reshape(4, 2, 2, 4, 2), ROW + COL)
    in_specs = (
        P(ROW, None),
        P(ROW + COL),
        P(ROW, COL, None),
        P(ROW, COL, None),
        P(ROW, COL),
    )
    return jax.shard_map(
        shards, mesh=fine, in_specs=in_specs, out_specs=P(None, ROW + COL), check_vma=False
    )
```

```python
import functools

import jax
import jax.numpy as jnp
import numpy as np
from jax import lax
from jax.experimental import pallas as pl
from jax.experimental.pallas import tpu as pltpu
from jax.sharding import Mesh
from jax.sharding import PartitionSpec as P

TILE = 512
K = 64
PAIRS = 24
WIDTH = 1024
KERNEL_SCALE = 0.5
RATE = 2.0 / KERNEL_SCALE * float(np.log2(np.e))
F32 = jnp.float32
BF16 = jnp.bfloat16

ROW = ("y", "zh", "core")
COL = ("x", "zl")
CHIPS = ("y", "zh", "x", "zl")
SLAB_TILES = 8
BLOCK_TILES = 16
VMEM_LIMIT = 10 * 1024 * 1024
ROWS, SLABS, RANKS, GROUPS, STARTS = (8 + PAIRS * i for i in range(5))


def build_kernel(first, arrived, info, slab, half_rows, *refs):
    columns, refs = refs[:arrived], refs[arrived:]
    if first:
        _, old_degree, *refs = refs
    tiles, degree, made, sem_out = refs
    block_index = info[1]
    stores = made.shape[0]
    if first:
        degree[...] = old_degree[...]
    else:
        degree[...] = jnp.zeros_like(degree)

    begin, end = info[STARTS + first], info[STARTS + first + arrived]

    def store(entry, n):
        slot = lax.rem(entry, stores)
        lanes = pl.ds(n * 256, 256)
        return pltpu.make_async_copy(
            made.at[slot, :, lanes], tiles.at[entry, :, lanes], sem_out.at[slot, n]
        )

    def step(column, own, entry, carry):
        @pl.when(entry - begin >= stores)
        def _():
            for n in range(2):
                store(entry - stores, n).wait()

        slot = lax.rem(entry, stores)
        t = info[ROWS + entry]
        wide = column[...].astype(F32)
        half_column = 0.5 * jnp.sum(wide * wide, axis=1, keepdims=True)
        sums = []
        for n in range(2):
            lanes = pl.ds(n * 256, 256)
            inner = lax.dot_general(
                column[...], slab[t, lanes, :], (((1,), (1,)), ((), ())), preferred_element_type=F32
            )
            half_row = half_rows[pl.ds(t, 1), lanes]
            w = jnp.exp2(RATE * ((inner - half_row) - half_column)).astype(BF16)
            made[slot, :, lanes] = w
            if not own:
                store(entry, n).start()
            sums.append(jnp.sum(w.astype(F32), axis=0, keepdims=True))
        old = degree[pl.ds(t, 1), :]
        degree[pl.ds(t, 1), :] = old + jnp.concatenate(sums, axis=1)
        if own:
            @pl.when(t == block_index)
            def _():
                w = made[slot]
                same = lax.broadcasted_iota(jnp.int32, (TILE, TILE), 0) == lax.broadcasted_iota(
                    jnp.int32, (TILE, TILE), 1
                )
                w = jnp.where(same, jnp.zeros_like(w), w)
                made[slot] = w
                degree[pl.ds(t, 1), :] = old + jnp.sum(w.astype(F32), axis=0, keepdims=True)

            for n in range(2):
                store(entry, n).start()
        return carry

    for s, column in enumerate(columns):
        low, high = info[STARTS + first + s], info[STARTS + first + s + 1]
        lax.fori_loop(low, high, functools.partial(step, column, first + s == 0), 0)
    for back in range(stores):

        @pl.when(end - begin > back)
        def _():
            for n in range(2):
                store(end - 1 - back, n).wait()


def in_hbm(value):
    return pltpu.with_memory_space_constraint(value, pltpu.HBM)


def in_vmem(value):
    return pltpu.with_memory_space_constraint(value, pltpu.VMEM)


def build(first, info, slab, half_rows, columns, made):
    hbm = pl.BlockSpec(memory_space=pltpu.HBM)
    vmem = pl.BlockSpec(memory_space=pltpu.VMEM)
    arrived = len(columns)
    pairs = max(1, PAIRS * arrived // BLOCK_TILES)
    return pl.pallas_call(
        functools.partial(build_kernel, first, arrived),
        out_shape=(
            pltpu.HBM((PAIRS, TILE, TILE), BF16),
            jax.ShapeDtypeStruct((SLAB_TILES, TILE), F32),
        ),
        in_specs=[pl.BlockSpec(memory_space=pltpu.SMEM), vmem, vmem]
        + [vmem] * arrived
        + ([hbm, vmem] if made else []),
        out_specs=(hbm, vmem),
        scratch_shapes=[
            pltpu.VMEM((4, TILE, TILE), BF16),
            pltpu.SemaphoreType.DMA((4, 2)),
        ],
        input_output_aliases={3 + arrived: 0} if made else {},
        compiler_params=pltpu.CompilerParams(vmem_limit_bytes=16 * 1024 * 1024),
        cost_estimate=pl.CostEstimate(
            flops=pairs * 2 * TILE * TILE * WIDTH,
            bytes_accessed=pairs * 5 * TILE * WIDTH,
            transcendentals=pairs * TILE * TILE,
        ),
        name="build_tiles",
    )(
        info,
        in_vmem(slab),
        half_rows,
        *(in_vmem(column) for column in columns),
        *([in_hbm(made[0]), made[1]] if made else []),
    )


def terms_of(value):
    high = value.astype(BF16).astype(F32)
    middle = (value - high).astype(BF16).astype(F32)
    low = (value - high) - middle
    wide = jnp.concatenate([high, middle, low, jnp.zeros((32, 16), F32)], axis=1)
    return jnp.concatenate([wide[:16], wide[16:]], axis=1).astype(BF16)


def value_of(terms):
    wide = jnp.concatenate([terms[:, :256], terms[:, 256:]], axis=0)
    return wide[:, :80] + (wide[:, 80:160] + wide[:, 160:240])


def lead_of(sums):
    total = sums[:1, 67:68]
    return jnp.concatenate([sums[:, 65:66], sums[:, 66:67]], axis=0) / total, total


def row_of(rows, start):
    return jnp.concatenate([rows[start + i : start + i + 1] for i in range(4)], axis=1)


def product_kernel(first, info, tiles, *refs):
    if first:
        mine, others, out, running, held, sem = refs
    else:
        mine, others, degree, out, running, held, sem = refs
    count = info[0]
    core = info[2]
    depth = held.shape[0]

    def fetch(entry):
        slot = lax.rem(entry, depth)
        return pltpu.make_async_copy(tiles.at[entry], held.at[slot], sem.at[slot])

    def piece(entry):
        q = info[SLABS + entry]
        own = q % 2 == core
        if first:
            known = jnp.where(own, mine[q // 2], others[q // 2])
            value, label = lax.rsqrt(row_of(known, 0)), row_of(known, 4)
            value = jnp.where(label < K, value, -value)
            label = jnp.where(label < K, label, label - K)
            same = label == lax.broadcasted_iota(jnp.int32, (K, TILE), 0).astype(F32)
            return jnp.where(same, jnp.broadcast_to(value, (K, TILE)), 0.0).astype(BF16)
        return jnp.where(own, mine[q // 2, :K, :], others[q // 2, :K, :])

    def term(entry):
        return jnp.dot(piece(entry), held[lax.rem(entry, depth)], preferred_element_type=F32)

    for entry in range(depth - 4):

        @pl.when(entry < count)
        def _():
            fetch(jnp.int32(entry)).start()

    running[...] = jnp.zeros_like(running)
    if not first:
        sums = jnp.sum(mine[:, K:, :].astype(F32), axis=0) + jnp.sum(others[:, K:, :].astype(F32), axis=0)
        sums = value_of(sums)
        terms = terms_of(sums)
        for t in range(SLAB_TILES):
            out[t, K:, :] = terms

    def step(turn, carry):
        entries = [4 * turn + i for i in range(4)]
        for entry in entries:

            @pl.when(entry + depth - 4 < count)
            def _(entry=entry):
                fetch(entry + depth - 4).start()

        for entry in entries:

            @pl.when(entry < count)
            def _(entry=entry):
                fetch(entry).wait()

        terms = [term(entry) for entry in entries]
        for entry, value in zip(entries, terms, strict=True):
            running[info[ROWS + entry]] += jnp.where(entry < count, value, 0.0)
        return carry

    lax.fori_loop(0, (count + 3) // 4, step, 0)
    if first:
        out[...] = running[...].astype(BF16)
    else:
        lead, _ = lead_of(sums)
        for t in range(SLAB_TILES):
            out[t, :K, :] = (running[t] - lead * degree[t : t + 1, :]).astype(BF16)


def product(info, tiles, *operands):
    vmem = pl.BlockSpec(memory_space=pltpu.VMEM)
    first = len(operands) == 2
    return pl.pallas_call(
        functools.partial(product_kernel, first),
        out_shape=jax.ShapeDtypeStruct(
            (SLAB_TILES, K if first else K + 16, TILE), BF16
        ),
        in_specs=[
            pl.BlockSpec(memory_space=pltpu.SMEM),
            pl.BlockSpec(memory_space=pltpu.HBM),
        ]
        + [vmem] * len(operands),
        out_specs=vmem,
        scratch_shapes=[
            pltpu.VMEM((SLAB_TILES, K, TILE), F32),
            pltpu.VMEM((PAIRS, TILE, TILE), BF16),
            pltpu.SemaphoreType.DMA((PAIRS,)),
        ],
        compiler_params=pltpu.CompilerParams(vmem_limit_bytes=20 * 1024 * 1024),
        name="product",
    )(info, in_hbm(tiles), *operands)


def weights_of(image, root):
    heavy = jnp.concatenate([image, jnp.broadcast_to(root, (8, TILE))], axis=0)
    weights = lax.dot_general(
        heavy,
        heavy,
        (((1,), (1,)), ((), ())),
        precision=lax.Precision.HIGHEST,
        preferred_element_type=F32,
    )
    half = K // 2
    rows = lax.broadcasted_iota(jnp.int32, (half, half), 0)
    columns = lax.broadcasted_iota(jnp.int32, (half, half), 1)
    corner = weights[half:K, half:K]
    return jnp.concatenate(
        [
            weights[half:K, :half],
            jnp.where(rows >= columns, weights[:half, :half], corner),
            jnp.sum(jnp.where(rows == columns, corner, 0.0), axis=1, keepdims=True),
            weights[:half, K : K + 1],
            weights[half:K, K : K + 1],
            jnp.broadcast_to(weights[K : K + 1, K : K + 1], (half, 1)),
            jnp.zeros((half, 12), F32),
        ],
        axis=1,
    )


def factor_of(sums, scale):
    half = K // 2
    rows = lax.broadcasted_iota(jnp.int32, (half, half), 0)
    columns = lax.broadcasted_iota(jnp.int32, (half, half), 1)
    lower, mixed = sums[:, :half], sums[:, half:K]
    strict = jnp.where(rows > columns, mixed, 0.0)
    upper = jnp.where(rows < columns, mixed, 0.0)
    diagonal = rows == columns
    left = strict + strict.T + jnp.where(diagonal, mixed, 0.0)
    right = upper + upper.T + jnp.where(diagonal, sums[:, K : K + 1], 0.0)
    gram = jnp.concatenate(
        [jnp.concatenate([left, lower.T], axis=1), jnp.concatenate([lower, right], axis=1)], axis=0
    )
    lead, total = lead_of(sums)
    rows = lax.broadcasted_iota(jnp.int32, (K, K), 0)
    columns = lax.broadcasted_iota(jnp.int32, (K, K), 1)
    across = jnp.sum(jnp.where(rows == columns, lead, 0.0), axis=0, keepdims=True)
    gram = (gram - lead * across * total) * scale
    work = jnp.concatenate([gram, (rows == columns).astype(F32)], axis=1)
    index = lax.broadcasted_iota(jnp.int32, (K, 2 * K), 0)
    pivots = jnp.ones((K, 2 * K), F32)
    for start in range(0, K, 32):
        index = index[-(K - start) :]
        spread = [
            jnp.broadcast_to(work[start:, j : j + 1], (K - start, 2 * K)) for j in range(start, start + 32)
        ]
        rest = work[start:]
        below = pivots[start:]
        for a in range(32):
            pivot = spread[a][a : a + 1, :]
            below = jnp.where(index == start + a, pivot, below)
            ratio = jnp.where(index > start + a, spread[a] * (1.0 / pivot), 0.0)
            rest = rest - ratio * rest[a : a + 1, :]
            for b in range(a + 1, 32):
                spread[b] = spread[b] - ratio * spread[b][a : a + 1, :]
        work = jnp.concatenate([work[:start], rest], axis=0) if start else rest
        pivots = jnp.concatenate([pivots[:start], below], axis=0) if start else below
    return work[:, K:] * lax.rsqrt(pivots[:, K:]), lead


def times(factor, block):
    return jnp.dot(factor, block, precision=lax.Precision.HIGHEST, preferred_element_type=F32)


def roots_of(info, known):
    degree = row_of(known[info[3]], 0)
    return lax.rsqrt(degree), jnp.sqrt(degree)


def weigh_kernel(info, parts, known, out):
    inv_root, root = roots_of(info, known)
    image = jnp.sum(parts[...].astype(F32), axis=0) * inv_root
    out[:K, :] = (image * inv_root).astype(BF16)
    out[K:, :] = terms_of(weights_of(image, root))


def middle_kernel(scale, info, parts, known, by_column, image, message):
    inv_root, root = roots_of(info, known)
    own = by_column[info[3]]
    columns = [value_of(parts[c, K:, :].astype(F32)) for c in range(SLAB_TILES)]
    factor, lead = factor_of(sum(columns), scale)
    whole = jnp.sum(parts[:, :K, :].astype(F32), axis=0)
    for c in range(SLAB_TILES):
        whole = whole + (lead_of(columns[c])[0] - lead) * row_of(own[c], 0)
    block = times(factor, whole * inv_root)
    image[...] = block
    message[:, :80] = weights_of(block, root)
    message[:, 80:] = jnp.zeros((K // 2, 48), F32)


def last_kernel(scale, info, message, image, known, out):
    _, root = roots_of(info, known)
    factor, lead = factor_of(message[:, :80], scale)
    out[...] = times(factor, image[...] - lead * root)


def local(kernel, name, out_shape, info, *operands):
    vmem = pl.BlockSpec(memory_space=pltpu.VMEM)
    return pl.pallas_call(
        kernel,
        out_shape=out_shape,
        in_specs=[pl.BlockSpec(memory_space=pltpu.SMEM)] + [vmem] * len(operands),
        out_specs=jax.tree.map(lambda _: vmem, out_shape),
        compiler_params=pltpu.CompilerParams(vmem_limit_bytes=VMEM_LIMIT),
        name=name,
    )(info, *operands)


def swap_cores(value):
    return lax.ppermute(value, "core", [(0, 1), (1, 0)])


def share(value, axes):
    size = lax.axis_size(axes)
    return lax.all_to_all(
        jnp.broadcast_to(value[None], (size,) + value.shape), axes, 0, 0, tiled=True
    )


def share_row(value):
    mine = share(value, ("y", "zh"))
    return mine, swap_cores(mine)


def sum_all(message):
    rows = message.shape[0] // 2
    core = lax.axis_index("core")
    keep = lax.dynamic_slice_in_dim(message, core * rows, rows, 0)
    give = lax.dynamic_slice_in_dim(message, (1 - core) * rows, rows, 0)
    summed = jnp.sum(share(keep + swap_cores(give), CHIPS), axis=0)
    other = swap_cores(summed)
    first = core == 0
    return jnp.concatenate([jnp.where(first, summed, other), jnp.where(first, other, summed)], 0)


def up(value):
    return lax.ppermute(value, "y", [(i, (i + 1) % 4) for i in range(4)])


def down(value):
    return lax.ppermute(value, "y", [(i, (i + 3) % 4) for i in range(4)])


def apart(value):
    return lax.ppermute(
        value,
        ("y", "core"),
        [(2 * i + k, 2 * ((i + 1 + 2 * k) % 4) + k) for i in range(4) for k in range(2)],
    )


def apart_z(value):
    moves = []
    for z in range(4):
        for k in range(2):
            to = (z + 1 + 2 * k) % 4
            moves.append((z // 2 * 4 + k * 2 + z % 2, to // 2 * 4 + k * 2 + to % 2))
    return lax.ppermute(value, ("zh", "core", "zl"), moves)


def cross(value):
    return lax.ppermute(value, ("zh", "zl"), [(0, 3), (3, 0), (1, 2), (2, 1)])


def pair_list(head, rows, slabs, arrivals):
    count = head[0]
    slot = jnp.arange(PAIRS, dtype=jnp.int32)
    rank = jnp.sum(
        jnp.where(slabs[:, None] == arrivals[None, :], jnp.arange(BLOCK_TILES, dtype=jnp.int32), 0), 1
    )
    key = jnp.where(slot < count, rank * PAIRS + slot, BLOCK_TILES * PAIRS + slot)
    place = jnp.sum((key[None, :] < key[:, None]).astype(jnp.int32), axis=1)
    at = place[None, :] == slot[:, None]

    def ordered(value):
        return jnp.sum(jnp.where(at, value[None, :], 0), axis=1)

    ranks = ordered(rank)
    fresh = jnp.concatenate([jnp.zeros(1, bool), ranks[1:] != ranks[:-1]])
    groups = jnp.sum(jnp.where(slot[None, :] <= slot[:, None], fresh[None, :], False).astype(jnp.int32), 1)
    limit = jnp.arange(BLOCK_TILES + 1, dtype=jnp.int32) * PAIRS
    starts = jnp.sum((key[None, :] < limit[:, None]).astype(jnp.int32), axis=1)
    head = jnp.stack(head + [jnp.int32(0)] * (8 - len(head)))
    return jnp.concatenate([head, ordered(rows), ordered(slabs), ranks, groups, starts]).astype(jnp.int32)


def shards(embeddings, labels, pair_rows, pair_cols, pair_count):
    y, zh, core = (lax.axis_index(a) for a in ROW)
    slab_index = lax.axis_index(ROW)
    block_index = lax.axis_index(COL)
    zero = core == 0
    slab = embeddings.reshape(SLAB_TILES, TILE, WIDTH)

    def of(dy, dz, k):
        return ((y + dy) % 4 * 2 + (zh + dz) % 2) * 2 + k

    def side(k):
        return jnp.where(k == 0, 3, 1)

    def both_of(dy, dz):
        return [of(dy, dz, core), of(dy, dz, 1 - core)]

    near_q, other_q = (
        [of(side(k ^ way), 1, k) for k in (core, 1 - core)] for way in (0, 1)
    )
    beyond_q, far_q = both_of(2, 0), both_of(2, 1)
    arrivals = both_of(0, 0)
    arrivals += [near_by[k] for k in (0, 1) for near_by in (both_of(0, 1), both_of(3, 0), both_of(1, 0))]
    arrivals += near_q
    arrivals += [beyond_q[0], other_q[0], beyond_q[1], other_q[1], far_q[0], far_q[1]]
    arrivals = jnp.stack(arrivals)
    head = [pair_count[0, 0], block_index, core, slab_index // 2]
    info = pair_list(head, pair_rows[0, 0], pair_cols[0, 0], arrivals)

    own = lax.dynamic_index_in_dim(slab, block_index, 0, keepdims=False)
    later, own = lax.optimization_barrier((slab, own))
    below = up(own)
    above = down(own)
    give = lax.dynamic_index_in_dim(later, block_index ^ 1, 0, keepdims=False)
    across = cross(give)
    half_rows = 0.5 * jnp.sum(jnp.square(slab.astype(F32)), axis=2)
    def both(*pieces):
        return [each for piece in pieces for each in (piece, swap_cores(piece))]

    def after(made, *pieces):
        tied = lax.optimization_barrier((made[1],) + pieces)
        return (made[0], tied[0]), tied[1:]

    made = build(0, info, slab, half_rows, both(own), ())
    made, (across, below, above) = after(made, across, below, above)
    near = apart(across)
    other = apart_z(jnp.where(zero, above, below))
    made = build(2, info, slab, half_rows, [across, below, above], made)
    made, (passed,) = after(made, jnp.where(zero, below, above))
    beyond = apart(passed)
    made = build(5, info, slab, half_rows, [swap_cores(piece) for piece in (across, below, above)], made)
    made, (near, other) = after(made, near, other)
    far = apart(near)
    other = apart_z(other)
    made = build(8, info, slab, half_rows, [near, swap_cores(near), beyond, other, swap_cores(beyond)], made)
    made, (far,) = after(made, far)
    made = build(13, info, slab, half_rows, [swap_cores(other), far], made)
    made = build(15, info, slab, half_rows, [swap_cores(far)], made)
    tiles, partial_degree = made

    in_block = (jnp.arange(SLAB_TILES) == block_index)[:, None, None]
    seeds = jnp.where(in_block, labels.astype(F32).reshape(1, 4, 128), 0.0)
    sent = jnp.concatenate([partial_degree.reshape(SLAB_TILES, 4, 128), seeds], axis=1)
    by_column = lax.all_to_all(
        jnp.broadcast_to(sent[None], (8,) + sent.shape).reshape(8 * SLAB_TILES, 8, 128), CHIPS, 0, 0, tiled=True
    ).reshape(8, SLAB_TILES, 8, 128)
    known = jnp.sum(by_column, axis=1)

    scale = 1.0 / (BLOCK_TILES * SLAB_TILES * TILE)
    block = jax.ShapeDtypeStruct((K, TILE), F32)
    running = product(info, tiles, known, swap_cores(known))
    parts = lax.all_to_all(running, COL, 0, 0, tiled=True)
    weighed = local(
        weigh_kernel, "weigh", jax.ShapeDtypeStruct((K + 16, TILE), BF16), info, parts, known
    )
    running = product(info, tiles, *share_row(weighed), partial_degree)
    parts = lax.all_to_all(running, COL, 0, 0, tiled=True)
    image, message = local(
        functools.partial(middle_kernel, scale),
        "middle",
        (block, jax.ShapeDtypeStruct((K // 2, 128), F32)),
        info,
        parts,
        known,
        by_column,
    )
    return local(
        functools.partial(last_kernel, scale), "last", block, info, sum_all(message), image, known
    )


def solution(mesh):
    fine = Mesh(np.asarray(mesh.devices).reshape(4, 2, 2, 4, 2), ROW + COL)
    in_specs = (
        P(ROW, None),
        P(ROW + COL),
        P(ROW, COL, None),
        P(ROW, COL, None),
        P(ROW, COL),
    )
    return jax.shard_map(
        shards, mesh=fine, in_specs=in_specs, out_specs=P(None, ROW + COL), check_vma=False
    )
```
